32 devices in a mesh: batch: 8 (over z, y), slot: 4 (over x, core).
Axes of the slice: x: 2, y: 2, z: 4, core: 2. Of those that a mesh axis runs over, the one named last changes fastest.
Arguments:
- tokens: bfloat16 [2, 16384, 512], P(None, ('batch', 'slot')), may hold values from -6 to 6
- memory: bfloat16 [2, 8, 64, 512], P(None, 'batch', 'slot'), may hold values from -6 to 6
- doc_lengths: int32 [2, 16], replicated, may hold values from 1 to 4096, 16384 in all within a row
- key_mask: int32 [2, 16384], P(None, 'batch'), may hold values 0 or 1
- w_query: bfloat16 [512, 512], P(('batch', 'slot')), may hold values from -0.375 to 0.375
- w_key: bfloat16 [512, 512], P(('batch', 'slot')), may hold values from -0.25 to 0.25
- w_value: bfloat16 [512, 512], P(('batch', 'slot')), may hold values from -0.25 to 0.25
- w_out: bfloat16 [512, 512], P(('batch', 'slot')), may hold values from -2 to 2
- w_up: bfloat16 [512, 2048], P(('batch', 'slot')), may hold values from -0.25 to 0.25
- w_down: bfloat16 [2048, 512], P(('batch', 'slot')), may hold values from -0.125 to 0.125
- w_slot_query: bfloat16 [512, 512], P(('batch', 'slot')), may hold values from -0.375 to 0.375
- w_slot_out: bfloat16 [512, 512], P(('batch', 'slot')), may hold values from -4 to 4
- w_forget: bfloat16 [512, 512], P(('batch', 'slot')), may hold values from -0.25 to 0.25
- norm_gain: bfloat16 [512], P(('batch', 'slot')), may hold values from 0.5 to 1.5
- ffn_gain: bfloat16 [512], P(('batch', 'slot')), may hold values from 0.5 to 1.5
- memory_gain: bfloat16 [512], P(('batch', 'slot')), may hold values from 0.5 to 1.5
- out_grad: bfloat16 [2, 16384, 512], P(None, ('batch', 'slot')), may hold values from -6 to 6
- memory_grad: bfloat16 [2, 8, 64, 512], P(None, 'batch', 'slot'), may hold values from -6 to 6
Outputs:
- layer_out: bfloat16 [2, 16384, 512], P(None, ('batch', 'slot'))
- memory_out: bfloat16 [2, 8, 64, 512], P(None, 'batch', 'slot')
- tokens_grad: bfloat16 [2, 16384, 512], P(None, ('batch', 'slot'))
- memory_in_grad: bfloat16 [2, 8, 64, 512], P(None, 'batch', 'slot')
- grad_query: float32 [512, 512], P(('batch', 'slot'))
- grad_key: float32 [512, 512], P(('batch', 'slot'))
- grad_value: float32 [512, 512], P(('batch', 'slot'))
- grad_out: float32 [512, 512], P(('batch', 'slot'))
- grad_up: float32 [512, 2048], P(('batch', 'slot'))
- grad_down: float32 [2048, 512], P(('batch', 'slot'))
- grad_slot_query: float32 [512, 512], P(('batch', 'slot'))
- grad_slot_out: float32 [512, 512], P(('batch', 'slot'))
- grad_forget: float32 [512, 512], P(('batch', 'slot'))
- grad_norm_gain: float32 [512], P(('batch', 'slot'))
- grad_ffn_gain: float32 [512], P(('batch', 'slot'))
- grad_memory_gain: float32 [512], P(('batch', 'slot'))
The draws below stay inside these ranges and needn't reach their ends.
Inputs may be any that keep to these rules, and one draw needn't show every extreme that they name: `doc_lengths`: in each micro-batch the 16 lengths sum to 16384, and the longest is 4096.
All inputs are finite; a program needn't handle non-finite values. No bound on the sum of `key_mask` on one device may be relied on, other than what follows from the above.
Results may differ from the reference program's by a relative error of at most 0.015.
Values may be sent and summed in bfloat16 or wider, within the bound.
No kernel may reach another device: no remote copies, remote signals or barrier semaphores. Data moves between devices by JAX's collectives and lax.ppermute only.
A program may use at most 256 MiB of HBM per device.

```python
import math
import jax
import jax.numpy as jnp
import numpy as np
from jax import lax

D = 512
HEADS = 8
HEAD_DIM = 64
FF = 2048
SLOTS = 64
SEG = 512
MICRO = 2
DOC_MOST = 4096
GT = 2048
GROUPS = 8
TOKENS = 16384
NDOCS = 16


def with_ends(result, stream_key, least, high):
    longest = result.shape.index(max(result.shape))
    spots = []
    for shift in (0, 1):
        where = [jax.random.randint(jax.random.fold_in(stream_key, axis), (), 0, length) for axis, length in enumerate(result.shape)]
        where[longest] = (where[longest] + shift) % result.shape[longest]
        spots.append(tuple(where))
    return result.at[spots[0]].set(least).at[spots[1]].set(high)


def steps_of(rng, extent, split, smallest, largest):
    def one(dim, shards_of):
        steps = jax.random.uniform(jax.random.fold_in(jax.random.fold_in(rng, 6), dim), (shards_of,), jnp.float32, smallest / len(split), largest / len(split))
        return jnp.repeat(jnp.exp(steps), extent[dim] // shards_of).reshape((-1,) + (1,) * (len(extent) - dim - 1))

    factor_of = one(*split[0])
    for cut in split[1:]:
        factor_of = factor_of * one(*cut)
    return factor_of


def length_profile(number_of, total, most, slope):
    loads = [(1 << 20) // math.isqrt(rank ** slope) + 1 for rank in range(2, number_of + 1)]
    spare, given = total - most - (number_of - 1), [1] * (number_of - 1)
    while spare > 0:
        movable = [i for i in range(number_of - 1) if given[i] < most]
        whole, budget = sum([loads[i] for i in movable]), spare
        for i in movable:
            more = min(most - given[i], max(1, budget * loads[i] // whole), spare)
            given[i] = given[i] + more
            spare = spare - more
    return np.array([most] + given)


def ragged(key, count, total, bound, skew):
    if count == 2:
        one = jax.random.randint(key, (), max(1, total - bound), min(bound, total - 1) + 1)
        return jnp.stack([one, total - one])
    sizes = jnp.asarray(length_profile(count, total, bound, skew), jnp.int32)
    pairs = (count - 1) // 2
    giver, sink = sizes[1:1 + 2 * pairs:2], sizes[2:2 + 2 * pairs:2]
    margin = jnp.minimum(giver - 1, bound - sink)
    shifted = jax.random.randint(jax.random.fold_in(key, 1), (pairs,), 0, 1 << 20) % (margin + 1)
    sizes = sizes.at[1:1 + 2 * pairs:2].set(giver - shifted).at[2:2 + 2 * pairs:2].set(sink + shifted)
    return sizes[jax.random.permutation(jax.random.fold_in(key, 2), count)]


def bell_draw(rng, shape, width, most, pieces=(), kind=jnp.bfloat16):
    drawn = jax.random.normal(rng, shape, jnp.float32) * width
    if len(pieces) > 0:
        drawn = steps_of(rng, shape, pieces, -0.22, 0.18) * drawn
    return jnp.clip(drawn, min=-most, max=most).astype(kind)


def setup_inputs(seed: int = 0) -> dict:
    streams_of = jax.random.split(jax.random.key(seed), 19)
    tokens = bell_draw(streams_of[0], (MICRO, TOKENS, D), 1.0, 6.0, ((1, 32),))
    memory = bell_draw(streams_of[1], (MICRO, GROUPS, SLOTS, D), 1.0, 6.0, ((1, 8), (2, 4)))
    doc_lengths = jax.vmap(lambda own: ragged(own, NDOCS, TOKENS, DOC_MOST, 2))(jax.random.split(streams_of[2], MICRO)).reshape((MICRO, NDOCS)).astype(jnp.int32)
    key_mask = with_ends((jax.random.randint(streams_of[3], (MICRO, TOKENS), 0, 8) < 7).astype(jnp.int32), jax.random.fold_in(streams_of[3], 1), 0, 1)
    w_query = bell_draw(streams_of[4], (D, D), (D // 2) ** -0.5, 0.375, ((0, 32),))
    w_key = bell_draw(streams_of[5], (D, D), D ** -0.5, 0.25, ((0, 32),))
    w_value = bell_draw(streams_of[6], (D, D), D ** -0.5, 0.25, ((0, 32),))
    w_out = bell_draw(streams_of[7], (D, D), (D // 64) ** -0.5, 2.0, ((0, 32),))
    w_up = bell_draw(streams_of[8], (D, FF), D ** -0.5, 0.25, ((0, 32),))
    w_down = bell_draw(streams_of[9], (FF, D), FF ** -0.5, 0.125, ((0, 32),))
    w_slot_query = bell_draw(streams_of[10], (D, D), (D // 2) ** -0.5, 0.375, ((0, 32),))
    w_slot_out = bell_draw(streams_of[11], (D, D), (D // 256) ** -0.5, 4.0, ((0, 32),))
    w_forget = bell_draw(streams_of[12], (D, D), D ** -0.5, 0.25, ((0, 32),))
    norm_gain = jnp.clip(1.0 + 0.1 * jax.random.normal(streams_of[13], (D,), jnp.float32), 0.5, 1.5).astype(jnp.bfloat16)
    ffn_gain = jnp.clip(1.0 + 0.1 * jax.random.normal(streams_of[14], (D,), jnp.float32), 0.5, 1.5).astype(jnp.bfloat16)
    memory_gain = jnp.clip(1.0 + 0.1 * jax.random.normal(streams_of[15], (D,), jnp.float32), 0.5, 1.5).astype(jnp.bfloat16)
    out_grad = bell_draw(streams_of[16], (MICRO, TOKENS, D), 1.0, 6.0, ((1, 32),))
    memory_grad = bell_draw(streams_of[17], (MICRO, GROUPS, SLOTS, D), 1.0, 6.0, ((1, 8), (2, 4)))
    return dict(tokens=tokens, memory=memory, doc_lengths=doc_lengths, key_mask=key_mask, w_query=w_query, w_key=w_key, w_value=w_value, w_out=w_out, w_up=w_up, w_down=w_down, w_slot_query=w_slot_query, w_slot_out=w_slot_out, w_forget=w_forget, norm_gain=norm_gain, ffn_gain=ffn_gain, memory_gain=memory_gain, out_grad=out_grad, memory_grad=memory_grad)


EPSILON = 1e-05
MASKED = -1e+30
PRECISE = lax.Precision.HIGHEST

@jax.custom_vjp
def low(v):
    return lax.optimization_barrier(v.astype(jnp.bfloat16)).astype(jnp.float32)

@jax.custom_vjp
def low_back(v):
    return v

def low_keep(v):
    return (low(v), None)

def low_pass(kept, grad):
    return (grad,)

def back_keep(v):
    return (v, None)

def back_low(kept, grad):
    return (low(grad),)
low.defvjp(low_keep, low_pass)
low_back.defvjp(back_keep, back_low)

def mat_mul(first_op, second_op):
    return jnp.dot(first_op, second_op, precision=PRECISE, preferred_element_type=jnp.float32)

def layer_norm(operand, gain_row):
    centre = lax.optimization_barrier(jnp.mean(operand, axis=-1, keepdims=True))
    centred = operand - centre
    spread = lax.optimization_barrier(jnp.mean(centred * centred, axis=-1, keepdims=True))
    return centred * lax.rsqrt(spread + EPSILON) * gain_row

def group_forward(params, group_tokens, group_memory, group_docs, group_keep):
    w_query, w_key, w_value, w_out, w_up, w_down, w_slot_query, w_slot_out, w_forget, norm_gain, ffn_gain, memory_gain = params
    score_scale = HEAD_DIM ** (-0.5)
    blocks = GT // SEG
    normed = low(layer_norm(group_tokens, norm_gain))
    queries = low(low_back(mat_mul(normed, w_query)))
    tok_keys = low(low_back(mat_mul(normed, w_key)))
    tok_values = low(low_back(mat_mul(normed, w_value)))
    slot_keys = low(low_back(mat_mul(group_memory, w_key)))
    slot_values = low(low_back(mat_mul(group_memory, w_value)))
    query_heads = queries.reshape(blocks, SEG, HEADS, HEAD_DIM)
    key_heads = tok_keys.reshape(blocks, SEG, HEADS, HEAD_DIM)
    value_heads = tok_values.reshape(blocks, SEG, HEADS, HEAD_DIM)
    slot_key_heads = slot_keys.reshape(SLOTS, HEADS, HEAD_DIM)
    slot_value_heads = slot_values.reshape(SLOTS, HEADS, HEAD_DIM)
    positions = jnp.arange(SEG, dtype=jnp.int32)
    causal = positions[:, None] >= positions[None, :]
    doc_ids = group_docs.reshape(blocks, SEG)
    key_keep = group_keep.reshape(blocks, SEG)
    allowed = causal[None] & (doc_ids[:, :, None] == doc_ids[:, None, :]) & (key_keep[:, None, :] > 0)
    mem_scores = jnp.einsum('bqhd,khd->bhqk', query_heads, slot_key_heads, precision=PRECISE) * score_scale
    tok_scores = jnp.einsum('bqhd,bkhd->bhqk', query_heads, key_heads, precision=PRECISE) * score_scale
    tok_scores = jnp.where(allowed[:, None], tok_scores, MASKED)
    all_scores = low_back(jnp.concatenate([mem_scores, tok_scores], axis=-1))
    attn_prob = low(jax.nn.softmax(all_scores, axis=-1))
    attn_mix = jnp.einsum('bhqk,khd->bqhd', attn_prob[..., :SLOTS], slot_value_heads, precision=PRECISE)
    attn_mix = attn_mix + jnp.einsum('bhqk,bkhd->bqhd', attn_prob[..., SLOTS:], value_heads, precision=PRECISE)
    attended = low(low_back(attn_mix.reshape(GT, D)))
    resid = group_tokens + low_back(mat_mul(attended, w_out))
    ffn_normed = low(layer_norm(resid, ffn_gain))
    hidden = low_back(mat_mul(ffn_normed, w_up))
    activation = low(jax.nn.gelu(hidden))
    block_out = resid + low_back(mat_mul(activation, w_down))
    slot_queries = low(low_back(mat_mul(group_memory, w_slot_query))).reshape(SLOTS, HEADS, HEAD_DIM)
    all_keys = tok_keys.reshape(GT, HEADS, HEAD_DIM)
    all_values = tok_values.reshape(GT, HEADS, HEAD_DIM)
    self_scores = jnp.einsum('shd,shd->hs', slot_queries, slot_key_heads, precision=PRECISE) * score_scale
    read_scores = jnp.einsum('shd,thd->hst', slot_queries, all_keys, precision=PRECISE) * score_scale
    read_scores = jnp.where(group_keep[None, None, :] > 0, read_scores, MASKED)
    writer_scores = low_back(jnp.concatenate([self_scores[..., None], read_scores], axis=-1))
    writer_prob = low(jax.nn.softmax(writer_scores, axis=-1))
    written = jnp.einsum('hs,shd->shd', writer_prob[..., 0], slot_value_heads, precision=PRECISE)
    written = written + jnp.einsum('hst,thd->shd', writer_prob[..., 1:], all_values, precision=PRECISE)
    written = low(low_back(written.reshape(SLOTS, D)))
    update = low_back(mat_mul(written, w_slot_out))
    forget_gate = jax.nn.sigmoid(low_back(mat_mul(group_memory, w_forget)))
    blended = forget_gate * group_memory + (1.0 - forget_gate) * update
    return (block_out, layer_norm(blended, memory_gain))

def reference(tokens, memory, doc_lengths, key_mask, w_query, w_key, w_value, w_out, w_up, w_down, w_slot_query, w_slot_out, w_forget, norm_gain, ffn_gain, memory_gain, out_grad, memory_grad):
    params = tuple((weight.astype(jnp.float32) for weight in (w_query, w_key, w_value, w_out, w_up, w_down, w_slot_query, w_slot_out, w_forget, norm_gain, ffn_gain, memory_gain)))
    doc_ends = jnp.cumsum(doc_lengths, axis=1, dtype=jnp.int32)
    positions = jnp.arange(TOKENS, dtype=jnp.int32)

    def doc_of(ends_row):
        return lax.optimization_barrier(jnp.sum((positions[:, None] >= ends_row[None, :]).astype(jnp.int32), axis=1)).astype(jnp.int32)
    doc_ids = lax.map(doc_of, doc_ends)
    flat_docs = doc_ids.reshape(MICRO * GROUPS, GT)
    flat_keep = key_mask.reshape(MICRO * GROUPS, GT)

    def forward(weights, token_rows, memory_rows):
        flat_tokens = token_rows.reshape(MICRO * GROUPS, GT, D)
        flat_memory = memory_rows.reshape(MICRO * GROUPS, SLOTS, D)

        def one_group(item):
            return group_forward(weights, item[0], item[1], item[2], item[3])
        block_out, memory_new = lax.map(jax.checkpoint(one_group), (flat_tokens, flat_memory, flat_docs, flat_keep))
        return (block_out.reshape(MICRO, TOKENS, D), memory_new.reshape(MICRO, GROUPS, SLOTS, D))
    (layer_out, memory_out), pullback = jax.vjp(forward, params, tokens.astype(jnp.float32), memory.astype(jnp.float32))
    weight_grads, tokens_grad, memory_in_grad = pullback((out_grad.astype(jnp.float32), memory_grad.astype(jnp.float32)))
    return (layer_out.astype(jnp.bfloat16), memory_out.astype(jnp.bfloat16), tokens_grad.astype(jnp.bfloat16), memory_in_grad.astype(jnp.bfloat16), weight_grads[0], weight_grads[1], weight_grads[2], weight_grads[3], weight_grads[4], weight_grads[5], weight_grads[6], weight_grads[7], weight_grads[8], weight_grads[9], weight_grads[10], weight_grads[11])
```

```python
import functools

import jax
import jax.numpy as jnp
from jax import lax
from jax.sharding import PartitionSpec as P

HEADS = 8
HEAD_DIM = 64
SEG = 512
EPSILON = 1e-05
MASKED = -1e30
BF16 = jnp.bfloat16
F32 = jnp.float32
SCALE = HEAD_DIM ** (-0.5)


def stages():
    batch_bits = lax.axis_size("batch").bit_length() - 1
    slot_bits = lax.axis_size("slot").bit_length() - 1
    found = []
    for bit in range(slot_bits):
        found.append(("slot", 1 << bit, batch_bits + slot_bits - 1 - bit))
    for bit in range(batch_bits):
        found.append(("batch", 1 << bit, batch_bits - 1 - bit))
    return found


def rotated(turn):
    steps = stages()
    first, middle, last = steps[:1], steps[1:4], steps[4:]
    turn = turn % 3
    return first + middle[turn:] + middle[:turn] + last


def swap(value, axis, distance):
    pairs = [(i, i ^ distance) for i in range(lax.axis_size(axis))]
    return lax.ppermute(value, axis, pairs)


def own_bit(axis, distance):
    return (lax.axis_index(axis) // distance) % 2


def gather_rows(shard, turn):
    steps = rotated(turn)
    held = shard.reshape((1,) * len(steps) + shard.shape)
    for axis, distance, dim in reversed(steps):
        mine = own_bit(axis, distance)
        got = swap(held, axis, distance)
        low = jnp.where(mine == 0, held, got)
        high = jnp.where(mine == 0, got, held)
        held = jnp.concatenate([low, high], dim)
    return held.reshape((-1,) + shard.shape)


def scatter_sum(full, turn):
    steps = rotated(turn)
    held = full.reshape((2,) * len(steps) + full.shape[1:])
    for axis, distance, dim in steps:
        mine = own_bit(axis, distance)
        send = lax.dynamic_slice_in_dim(held, 1 - mine, 1, dim)
        keep = lax.dynamic_slice_in_dim(held, mine, 1, dim)
        held = keep + swap(send, axis, distance)
    return held.reshape(full.shape[1:])


def layer_norm(operand, gain_row):
    centre = jnp.mean(operand, axis=-1, keepdims=True)
    centred = operand - centre
    spread = jnp.mean(centred * centred, axis=-1, keepdims=True)
    return centred * lax.rsqrt(spread + EPSILON) * gain_row


def mat_mul(first_op, second_op):
    return jnp.dot(first_op, second_op, preferred_element_type=F32)


def lead_dot(first_op, second_op):
    return lax.dot_general(
        first_op, second_op, (((0,), (0,)), ((), ())), preferred_element_type=F32
    )


def tail_dot(first_op, second_op):
    return lax.dot_general(
        first_op, second_op, (((1,), (1,)), ((), ())), preferred_element_type=F32
    )


def ein(spec, a, b):
    return jnp.einsum(spec, a, b, preferred_element_type=F32)


def on_device(
    tokens,
    memory,
    doc_lengths,
    key_mask,
    w_query,
    w_key,
    w_value,
    w_out,
    w_up,
    w_down,
    w_slot_query,
    w_slot_out,
    w_forget,
    norm_gain,
    ffn_gain,
    memory_gain,
    out_grad,
    memory_grad,
):
    slot_count = lax.axis_size("slot")
    slot_index = lax.axis_index("slot")
    micro, tok_dev, width = tokens.shape
    slot_rows = memory.shape[2]
    slots = slot_rows * slot_count
    group_tok = tok_dev * slot_count
    dev_start = slot_index * tok_dev
    rows = w_query.shape[0]
    ff = w_up.shape[1]
    cuts = ff // width
    blocks = tok_dev // SEG

    gains = gather_rows(
        jnp.stack([norm_gain, ffn_gain, memory_gain]), 0
    )
    gains = gains.transpose(1, 0, 2).reshape(3, width).astype(F32)
    norm_gain, ffn_gain, memory_gain = gains[0], gains[1], gains[2]
    w_query = gather_rows(w_query, 0).reshape(width, width)
    w_key = gather_rows(w_key, 1).reshape(width, width)
    w_value = gather_rows(w_value, 2).reshape(width, width)
    pair = jnp.stack([memory[:, 0], memory_grad[:, 0]])
    pair = lax.all_gather(pair, "slot", axis=2, tiled=True)
    mem_low = pair[0]
    mem_cot = pair[1].reshape(micro * slots, width).astype(F32)
    mem_flat = mem_low.reshape(micro * slots, width)
    mem_f32 = mem_flat.astype(F32)
    mixed = gather_rows(jnp.concatenate([w_slot_query, w_out, w_slot_out, w_forget]), 0)
    mixed = mixed.reshape(-1, 4, rows, width).transpose(1, 0, 2, 3).reshape(4, width, width)
    w_slot_query, w_out, w_slot_out, w_forget = mixed[0], mixed[1], mixed[2], mixed[3]
    w_up = gather_rows(
        w_up.reshape(rows, cuts, width).transpose(1, 0, 2).reshape(cuts * rows, width), 1
    )
    w_up = w_up.reshape(-1, cuts, rows, width).transpose(0, 2, 1, 3).reshape(width, ff)
    w_down = gather_rows(w_down, 2).reshape(ff, width)

    token_f32 = tokens.reshape(micro * tok_dev, width).astype(F32)
    normed, norm_pull = jax.vjp(layer_norm, token_f32, norm_gain)
    normed_low = normed.astype(BF16)
    queries = mat_mul(normed_low, w_query).astype(BF16)
    tok_keys = mat_mul(normed_low, w_key).astype(BF16)
    tok_values = mat_mul(normed_low, w_value).astype(BF16)
    slot_keys = mat_mul(mem_flat, w_key).astype(BF16)
    slot_values = mat_mul(mem_flat, w_value).astype(BF16)
    slot_queries = mat_mul(mem_flat, w_slot_query).astype(BF16)

    heads = lambda m, n: m.reshape(micro, n, HEADS, HEAD_DIM)
    qh, kh, vh = (heads(m, tok_dev) for m in (queries, tok_keys, tok_values))
    skh, svh, sqh = (heads(m, slots) for m in (slot_keys, slot_values, slot_queries))

    keep = lax.dynamic_slice_in_dim(key_mask, dev_start, tok_dev, 1)
    group_start = lax.axis_index("batch") * group_tok
    positions = group_start + dev_start + jnp.arange(tok_dev, dtype=jnp.int32)
    doc_ends = jnp.cumsum(doc_lengths, axis=1, dtype=jnp.int32)
    docs = jnp.sum((positions[None, :, None] >= doc_ends[:, None, :]).astype(jnp.int32), axis=2)

    read_scores = ein("mshd,mthd->mhst", sqh, kh) * SCALE
    read_scores = jnp.where(keep[:, None, None, :] > 0, read_scores, MASKED)
    self_scores = ein("mshd,mshd->mhs", sqh, skh) * SCALE
    part_top = jnp.maximum(jnp.max(read_scores, axis=-1), self_scores)
    part_exp = jnp.exp(read_scores - part_top[..., None])
    part_total = jnp.sum(part_exp, axis=-1)
    part_mix = ein("mhst,mthd->mhsd", part_exp.astype(BF16), vh)

    top, total, mix = part_top, part_total, part_mix
    for axis, distance, _ in stages()[: slot_count.bit_length() - 1]:
        stats = jnp.stack([top, total])
        other = swap(stats, axis, distance)
        other_mix = swap(mix, axis, distance)
        new_top = jnp.maximum(top, other[0])
        a, b = jnp.exp(top - new_top), jnp.exp(other[0] - new_top)
        total = total * a + other[1] * b
        mix = mix * a[..., None] + other_mix * b[..., None]
        top = new_top
    self_exp = jnp.exp(self_scores - top)
    total = total + self_exp
    writer_log = top + jnp.log(total)
    self_prob = self_exp / total
    written = mix / total[..., None] + self_prob[..., None] * svh.transpose(0, 2, 1, 3).astype(F32)
    written = written.transpose(0, 2, 1, 3).reshape(micro * slots, width)
    written_low = written.astype(BF16)
    update = mat_mul(written_low, w_slot_out)
    forget_gate = jax.nn.sigmoid(mat_mul(mem_flat, w_forget))
    blended = forget_gate * mem_f32 + (1.0 - forget_gate) * update
    mine = (jnp.arange(slots) // slot_rows == slot_index).astype(F32)
    mine = jnp.tile(mine, micro)[:, None]
    memory_new, memory_pull = jax.vjp(layer_norm, blended, memory_gain)
    d_blend, _ = memory_pull(mem_cot)
    gain_pull = jax.vjp(lambda g: layer_norm(blended, g), memory_gain)[1]
    grad_memory_gain = gain_pull(mem_cot * mine)[0]
    d_forget_pre = (d_blend * (mem_f32 - update) * forget_gate * (1.0 - forget_gate)).astype(BF16)
    d_update = (d_blend * (1.0 - forget_gate)).astype(BF16)
    mine_low = mine.astype(BF16)
    d_forget_own = d_forget_pre * mine_low
    grad_forget = lead_dot(mem_flat, d_forget_own)
    grad_slot_out = lead_dot(written_low, d_update * mine_low)
    d_memory = d_blend * forget_gate * mine + tail_dot(d_forget_own, w_forget)
    d_written = tail_dot(d_update, w_slot_out).astype(BF16)
    dwh = heads(d_written, slots)
    delta = jnp.sum(heads(d_written.astype(F32) * written, slots), axis=-1).transpose(0, 2, 1)
    read_prob = jnp.exp(read_scores - writer_log[..., None])
    read_dprob = ein("mshd,mthd->mhst", dwh, vh)
    read_dscore = (read_prob * (read_dprob - delta[..., None])).astype(BF16)
    self_dprob = ein("mshd,mshd->mhs", dwh, svh)
    self_dscore = (self_prob * (self_dprob - delta)).astype(BF16)
    writer_dkeys = ein("mhst,mshd->mthd", read_dscore, sqh)
    writer_dvalues = ein("mhst,mshd->mthd", read_prob.astype(BF16), dwh)
    own_rows = mine.reshape(micro, 1, slots, 1)
    self_own = self_dscore.astype(F32)[..., None] * own_rows
    self_prob_own = self_prob.astype(BF16).astype(F32)[..., None] * own_rows
    by_head = lambda m: m.transpose(0, 2, 1, 3).astype(F32)
    d_slot_queries = ein("mhst,mthd->mhsd", read_dscore, kh) + self_own * by_head(skh)
    own_dkeys = self_own * by_head(sqh)
    own_dvalues = self_prob_own * by_head(dwh)

    at = jnp.arange(tok_dev, dtype=jnp.int32)
    allowed = (
        (at[:, None] >= at[None, :])[None]
        & (at[:, None] // SEG == at[None, :] // SEG)[None]
        & (docs[:, :, None] == docs[:, None, :])
        & (keep[:, None, :] > 0)
    )
    mem_scores = ein("mqhd,mkhd->mhqk", qh, skh) * SCALE
    tok_scores = ein("mqhd,mkhd->mhqk", qh, kh) * SCALE
    tok_scores = jnp.where(allowed[:, None], tok_scores, MASKED)
    row_top = jnp.maximum(jnp.max(mem_scores, axis=-1), jnp.max(tok_scores, axis=-1))
    mem_exp = jnp.exp(mem_scores - row_top[..., None])
    tok_exp = jnp.exp(tok_scores - row_top[..., None])
    row_total = 1.0 / (jnp.sum(mem_exp, axis=-1) + jnp.sum(tok_exp, axis=-1))
    mem_prob = (mem_exp * row_total[..., None]).astype(BF16)
    tok_prob = (tok_exp * row_total[..., None]).astype(BF16)
    attn_mix = ein("mhqk,mkhd->mqhd", mem_prob, svh) + ein("mhqk,mkhd->mqhd", tok_prob, vh)
    attn_mix = attn_mix.reshape(micro * tok_dev, width)
    attended = attn_mix.astype(BF16)
    resid = token_f32 + mat_mul(attended, w_out)
    ffn_normed, ffn_pull = jax.vjp(layer_norm, resid, ffn_gain)
    ffn_low_rows = ffn_normed.astype(BF16)
    hidden = mat_mul(ffn_low_rows, w_up)
    activation_f32, gelu_pull = jax.vjp(jax.nn.gelu, hidden)
    activation = activation_f32.astype(BF16)
    block_out = resid + mat_mul(activation, w_down)

    out_cot = out_grad.reshape(micro * tok_dev, width)
    grad_down = lead_dot(activation, out_cot)
    d_hidden = gelu_pull(tail_dot(out_cot, w_down))[0].astype(BF16)
    grad_up = lead_dot(ffn_low_rows, d_hidden)
    d_resid_norm, grad_ffn_gain = ffn_pull(tail_dot(d_hidden, w_up))
    d_resid = out_cot.astype(F32) + d_resid_norm
    d_attn = d_resid.astype(BF16)
    grad_out = lead_dot(attended, d_attn)
    d_attended = tail_dot(d_attn, w_out).astype(BF16)
    dah = heads(d_attended, tok_dev)
    mem_dprob = ein("mqhd,mkhd->mhqk", dah, svh)
    tok_dprob = ein("mqhd,mkhd->mhqk", dah, vh)
    row_delta = jnp.sum(heads(d_attended.astype(F32) * attn_mix, tok_dev), axis=-1)
    row_delta = row_delta.transpose(0, 2, 1)[..., None]
    mem_dscore = (mem_prob.astype(F32) * (mem_dprob - row_delta)).astype(BF16)
    tok_dscore = (tok_prob.astype(F32) * (tok_dprob - row_delta)).astype(BF16)
    d_queries = (ein("mhqk,mkhd->mqhd", mem_dscore, skh) + ein("mhqk,mkhd->mqhd", tok_dscore, kh)) * SCALE
    d_queries = d_queries.reshape(micro * tok_dev, width).astype(BF16)
    d_keys = (ein("mhqk,mqhd->mkhd", tok_dscore, qh) + writer_dkeys) * SCALE
    d_keys = d_keys.reshape(micro * tok_dev, width).astype(BF16)
    d_values = ein("mhqk,mqhd->mkhd", tok_prob, dah) + writer_dvalues
    d_values = d_values.reshape(micro * tok_dev, width).astype(BF16)
    flat_slots = lambda m: m.transpose(0, 2, 1, 3).reshape(micro * slots, width).astype(BF16)
    d_slot_keys = flat_slots((ein("mhqk,mqhd->mhkd", mem_dscore, qh) + own_dkeys) * SCALE)
    d_slot_values = flat_slots(ein("mhqk,mqhd->mhkd", mem_prob, dah) + own_dvalues)
    d_slot_queries = flat_slots(d_slot_queries * SCALE)

    grad_slot_query = lead_dot(mem_flat, d_slot_queries)
    grad_query = lead_dot(normed_low, d_queries)
    grad_key = lead_dot(normed_low, d_keys) + lead_dot(mem_flat, d_slot_keys)
    grad_value = lead_dot(normed_low, d_values) + lead_dot(mem_flat, d_slot_values)
    d_normed = tail_dot(d_queries, w_query) + tail_dot(d_keys, w_key) + tail_dot(d_values, w_value)
    d_token_norm, grad_norm_gain = norm_pull(d_normed)
    tokens_grad = d_resid + d_token_norm
    d_memory = (
        d_memory
        + tail_dot(d_slot_queries, w_slot_query)
        + tail_dot(d_slot_keys, w_key)
        + tail_dot(d_slot_values, w_value)
    )
    moved = d_memory.reshape(micro, slots, width)
    for axis, distance, _ in reversed(stages()[: slot_count.bit_length() - 1]):
        half = moved.shape[1] // 2
        bit = own_bit(axis, distance)
        send = lax.dynamic_slice_in_dim(moved, (1 - bit) * half, half, 1)
        held = lax.dynamic_slice_in_dim(moved, bit * half, half, 1)
        moved = held + swap(send, axis, distance)

    devices = lambda m: m.astype(BF16).reshape(-1, rows, m.shape[1])
    down_share = scatter_sum(grad_down.astype(BF16).reshape(-1, cuts * rows, width), 2)
    up_parts = [devices(grad_up[:, i * width : (i + 1) * width]) for i in range(cuts)]
    up_share = scatter_sum(jnp.concatenate(up_parts, 1), 1).reshape(cuts, rows, width)
    up_share = up_share.transpose(1, 0, 2).reshape(rows, ff)
    mixed = (grad_slot_query, grad_out, grad_slot_out, grad_forget)
    mixed_share = scatter_sum(jnp.concatenate([devices(m) for m in mixed], 1), 0)
    mixed_share = mixed_share.reshape(4, rows, width)
    query_share = scatter_sum(devices(grad_query), 0)
    key_share = scatter_sum(devices(grad_key), 1)
    value_share = scatter_sum(devices(grad_value), 2)
    gain_grads = jnp.stack([grad_norm_gain, grad_ffn_gain, grad_memory_gain])
    gain_share = scatter_sum(gain_grads.reshape(3, -1, rows).transpose(1, 0, 2), 0)

    own_memory = lax.dynamic_slice_in_dim(
        memory_new.reshape(micro, slots, width), slot_index * slot_rows, slot_rows, 1
    )
    out = lambda m: m.astype(F32)
    return (
        block_out.astype(BF16).reshape(micro, tok_dev, width),
        own_memory.astype(BF16)[:, None],
        tokens_grad.astype(BF16).reshape(micro, tok_dev, width),
        moved.astype(BF16)[:, None],
        out(query_share),
        out(key_share),
        out(value_share),
        out(mixed_share[1]),
        out(up_share),
        out(down_share),
        out(mixed_share[0]),
        out(mixed_share[2]),
        out(mixed_share[3]),
        gain_share[0],
        gain_share[1],
        gain_share[2],
    )


def solution(mesh):
    weight = P(("batch", "slot"), None)
    gain = P(("batch", "slot"))
    rows = P(None, ("batch", "slot"), None)
    slots = P(None, "batch", "slot", None)
    return jax.shard_map(
        on_device,
        mesh=mesh,
        in_specs=(rows, slots, P(), P(None, "batch")) + (weight,) * 9 + (gain,) * 3 + (rows, slots),
        out_specs=(rows, slots, rows, slots) + (weight,) * 9 + (gain,) * 3,
        check_vma=False,
    )
```

```python
import jax
import jax.numpy as jnp
from jax import lax
from jax.experimental import pallas as pl
from jax.experimental.pallas import tpu as pltpu
from jax.sharding import PartitionSpec as P

HEADS = 8
HEAD_DIM = 64
SEG = 512
EPSILON = 1e-05
MASKED = -1e30
BF16 = jnp.bfloat16
F32 = jnp.float32
SCALE = HEAD_DIM ** (-0.5)


def stages():
    batch_bits = lax.axis_size("batch").bit_length() - 1
    slot_bits = lax.axis_size("slot").bit_length() - 1
    found = []
    for bit in range(slot_bits):
        found.append(("slot", 1 << bit, batch_bits + slot_bits - 1 - bit))
    for bit in range(batch_bits):
        found.append(("batch", 1 << bit, batch_bits - 1 - bit))
    return found


def rotated(turn):
    steps = stages()
    first, middle, last = steps[:1], steps[1:4], steps[4:]
    turn = turn % 3
    return first + middle[turn:] + middle[:turn] + last


def swap(value, axis, distance):
    pairs = [(i, i ^ distance) for i in range(lax.axis_size(axis))]
    return lax.ppermute(value, axis, pairs)


def own_bit(axis, distance):
    return (lax.axis_index(axis) // distance) % 2


def gather_rows(shard, turn):
    steps = rotated(turn)
    lead, rows, width = shard.shape
    held = shard.reshape((lead,) + (1,) * len(steps) + (rows, width))
    for axis, distance, dim in reversed(steps):
        mine = own_bit(axis, distance)
        got = swap(held, axis, distance)
        low = jnp.where(mine == 0, held, got)
        high = jnp.where(mine == 0, got, held)
        held = jnp.concatenate([low, high], dim + 1)
    return held.reshape(lead, -1, width)


def scatter_sum(full, turn):
    steps = rotated(turn)
    lead, _, width = full.shape
    held = full.reshape((lead,) + (2,) * len(steps) + (-1, width))
    rows = held.shape[-2]
    for axis, distance, dim in steps:
        mine = own_bit(axis, distance)
        send = lax.dynamic_slice_in_dim(held, 1 - mine, 1, dim + 1)
        keep = lax.dynamic_slice_in_dim(held, mine, 1, dim + 1)
        held = keep + swap(send, axis, distance)
    return held.reshape(lead, rows, width)


def dot(a, b):
    return jnp.dot(a, b, preferred_element_type=F32)


def dot_nt(a, b):
    return lax.dot_general(a, b, (((1,), (1,)), ((), ())), preferred_element_type=F32)


def dot_tn(a, b):
    return lax.dot_general(a, b, (((0,), (0,)), ((), ())), preferred_element_type=F32)


def norm_parts(rows):
    centre = jnp.mean(rows, axis=-1, keepdims=True)
    centred = rows - centre
    spread = jnp.mean(centred * centred, axis=-1, keepdims=True)
    inverse = lax.rsqrt(spread + EPSILON)
    return centred * inverse, inverse


def norm_back(cot, hat, inverse, gain):
    d_hat = cot * gain
    first = jnp.mean(d_hat, axis=-1, keepdims=True)
    second = jnp.mean(d_hat * hat, axis=-1, keepdims=True)
    return inverse * (d_hat - first - hat * second)


def head_lanes(value, head):
    lane = lax.broadcasted_iota(jnp.int32, value.shape, 1)
    return jnp.where(lane // HEAD_DIM == head, value, jnp.zeros_like(value))


def head_rows(value, head):
    row = lax.broadcasted_iota(jnp.int32, value.shape, 0)
    return jnp.where(row // HEAD_DIM == head, value, jnp.zeros_like(value))


def both_heads(value):
    return jnp.concatenate([head_lanes(value, 0), head_lanes(value, 1)], 0)


def to_slot_lanes(value):
    turned = value.T
    return jnp.concatenate([turned[:HEAD_DIM], turned[HEAD_DIM:]], 1)


def to_slot_rows(value):
    turned = value.T
    half = turned.shape[0] // 2
    return jnp.concatenate([turned[:half], turned[half:]], 1)


def diagonal(value):
    lane = lax.broadcasted_iota(jnp.int32, (HEAD_DIM, value.shape[1]), 1)
    return jnp.where(lane < value.shape[1] // 2, value[:HEAD_DIM], value[HEAD_DIM:])


def project_kernel(tok, mem, gain, wq, wk, wv, normed, q, k, v, sk, sv):
    hat, _ = norm_parts(tok[...].astype(F32))
    low = (hat * gain[0:1, :]).astype(BF16)
    normed[...] = low
    q[...] = dot(low, wq[...]).astype(BF16)
    k[...] = dot(low, wk[...]).astype(BF16)
    v[...] = dot(low, wv[...]).astype(BF16)

    @pl.when(pl.program_id(0) == 0)
    def _():
        sk[...] = dot(mem[...], wk[...]).astype(BF16)
        sv[...] = dot(mem[...], wv[...]).astype(BF16)


def read_kernel(q, k, v, sk, sv, starts, keep, attended, out_t, inv, e_ref, bias):
    tok = q.shape[0]
    half = tok // 2
    slots = sk.shape[0]

    @pl.when(pl.program_id(1) == 0)
    def _():
        key_at = lax.broadcasted_iota(jnp.int32, (tok, tok), 0)
        query_at = lax.broadcasted_iota(jnp.int32, (tok, tok), 1)
        start = starts[0, 0:1, :]
        kept = jnp.broadcast_to(keep[0, 0:1, :], (128, tok)).T
        kept = jnp.concatenate([kept] * (tok // 128), 1)
        good = (key_at >= start) & (key_at <= query_at) & (kept > 0)
        bias[...] = jnp.where(good, 0.0, MASKED)

    scaled = q[...] * jnp.asarray(SCALE, BF16)
    keys, values = k[...], v[...]
    slot_keys = sk[...]
    values_t = values.T
    slot_values_t = sv[...].T
    outs, inverses = [], []
    for head in range(2):
        qm = head_lanes(scaled, head)
        rows = slice(head * HEAD_DIM, (head + 1) * HEAD_DIM)
        s_mem = dot_nt(slot_keys, qm)
        s_a = dot_nt(keys[:half], qm) + bias[:half, :]
        s_b = dot_nt(keys[half:], qm[half:]) + bias[half:, half:]
        top = jnp.maximum(jnp.max(s_mem, 0, keepdims=True), jnp.max(s_a, 0, keepdims=True))
        top_b = jnp.maximum(top[:, half:], jnp.max(s_b, 0, keepdims=True))
        top = jnp.concatenate([top[:, :half], top_b], 1)
        e_mem = jnp.exp(s_mem - top)
        e_a = jnp.exp(s_a - top)
        e_b = jnp.exp(s_b - top_b)
        total = jnp.sum(e_mem, 0, keepdims=True) + jnp.sum(e_a, 0, keepdims=True)
        total_b = total[:, half:] + jnp.sum(e_b, 0, keepdims=True)
        total = jnp.concatenate([total[:, :half], total_b], 1)
        e_mem, e_a, e_b = e_mem.astype(BF16), e_a.astype(BF16), e_b.astype(BF16)
        e_ref[0, head, :slots, :] = e_mem
        e_ref[0, head, slots : slots + half, :] = e_a
        e_ref[0, head, slots + half :, half:] = e_b
        e_ref[0, head, slots + half :, :half] = jnp.zeros((half, half), BF16)
        mix = dot(slot_values_t[rows], e_mem) + dot(values_t[rows, :half], e_a)
        mix_b = mix[:, half:] + dot(values_t[rows, half:], e_b)
        mix = jnp.concatenate([mix[:, :half], mix_b], 1)
        inverse = 1.0 / total
        outs.append(mix * inverse)
        inverses.append(inverse)
    out = jnp.concatenate(outs, 0)
    out_t[...] = out
    inv[0] = jnp.concatenate(inverses + [jnp.zeros((6, tok), F32)], 0)
    attended[...] = out.T.astype(BF16)


def write_kernel(mem, wsq, k, v, sk, keep, sq_ref, part):
    micro = keep.shape[0]
    tok = k.shape[0] // micro
    slots = mem.shape[0] // micro
    pairs = k.shape[1] // 128
    sq = dot(mem[...], wsq[...]).astype(BF16)
    sq_ref[...] = sq
    for m in range(micro):
        kept = jnp.broadcast_to(keep[m, 0:1, :], (128, tok)).T
        bias = jnp.where(kept > 0, 0.0, MASKED)
        for p in range(pairs):
            lanes = slice(p * 128, p * 128 + 128)
            mine = sq[m * slots : (m + 1) * slots, lanes]
            own = to_slot_lanes(
                mine.astype(F32) * sk[m * slots : (m + 1) * slots, lanes].astype(F32)
            )
            own = jnp.sum(own, 0, keepdims=True) * SCALE
            scores = dot_nt(k[m * tok : (m + 1) * tok, lanes], both_heads(mine)) * SCALE + bias
            top = jnp.maximum(jnp.max(scores, 0, keepdims=True), own)
            e = jnp.exp(scores - top)
            total = jnp.sum(e, 0, keepdims=True)
            mix = diagonal(dot_tn(v[m * tok : (m + 1) * tok, lanes], e.astype(BF16)))
            part[m, :HEAD_DIM, lanes] = mix
            part[m, HEAD_DIM:, lanes] = jnp.concatenate(
                [top, total, own, jnp.zeros((5, 128), F32)], 0
            )


def ffn_kernel(
    att, tok, cot, wout, wup, wdown, gain,
    layer_out, d_resid_ref, da_t, g_down, g_up, g_out, g_gain,
    act_all, dh_all, low_all, dattn_all, att_all, cot_all,
):
    step = pl.program_id(0)
    rows = att.shape[0]
    cuts = wup.shape[0]
    width = att.shape[1]
    here = pl.ds(pl.multiple_of(step * rows, rows), rows)
    gain_row = gain[1:2, :]
    resid = tok[...].astype(F32) + dot(att[...], wout[...])
    hat, inverse = norm_parts(resid)
    low = (hat * gain_row).astype(BF16)
    low_all[here, :] = low
    att_all[here, :] = att[...]
    cot_low = cot[...]
    cot_all[here, :] = cot_low
    out = resid
    d_low = jnp.zeros((rows, width), F32)
    root = 0.7978845608028654
    for cut in range(cuts):
        hidden = dot(low, wup[cut])
        square = hidden * hidden
        bent = jnp.tanh(hidden * (root + (root * 0.044715) * square))
        half = 0.5 + 0.5 * bent
        act = (hidden * half).astype(BF16)
        slope = half + (0.5 * hidden) * (1.0 - bent * bent) * (
            root + (3.0 * root * 0.044715) * square
        )
        down = wdown[cut * width : (cut + 1) * width, :]
        d_hidden = (dot_nt(cot_low, down) * slope).astype(BF16)
        act_all[here, cut * width : (cut + 1) * width] = act
        dh_all[here, cut * width : (cut + 1) * width] = d_hidden
        out = out + dot(act, down)
        d_low = d_low + dot_nt(d_hidden, wup[cut])
    layer_out[...] = out.astype(BF16)
    d_resid = cot_low.astype(F32) + norm_back(d_low, hat, inverse, gain_row)
    d_resid_ref[...] = d_resid
    d_attn = d_resid.astype(BF16)
    dattn_all[here, :] = d_attn
    da_t[...] = dot_nt(wout[...], d_attn)
    gain_part = jnp.sum(d_low * hat, 0, keepdims=True)

    @pl.when(step == 0)
    def _():
        g_gain[...] = jnp.zeros_like(g_gain)

    g_gain[0:1, :] += gain_part

    @pl.when(step == pl.num_programs(0) - 1)
    def _():
        for cut in range(cuts):
            cols = slice(cut * width, (cut + 1) * width)
            g_down[cols, :] = dot_tn(act_all[:, cols], cot_all[...]).astype(BF16)
            g_up[cut] = dot_tn(low_all[...], dh_all[:, cols]).astype(BF16)
        g_out[...] = dot_tn(att_all[...], dattn_all[...]).astype(BF16)


def memory_kernel(
    slot_ref, part, mem, cot, sk, sv, sq, wso, wfg, gain,
    new_ref, g_forget, g_slot_out, base, dw_ref, rows_ref, ds_x, p_x, g_gain,
    held,
):
    micro = part.shape[0]
    slots = mem.shape[0] // micro
    own_rows = new_ref.shape[1]
    pairs = mem.shape[1] // 128
    row_at = lax.broadcasted_iota(jnp.int32, (mem.shape[0], 1), 0)
    mine = ((row_at % slots) // own_rows == slot_ref[0]).astype(F32)
    probs, tots, lses = [], [], []
    lines = []
    for m in range(micro):
        here = slice(m * slots, (m + 1) * slots)
        line, prob_line = [], []
        for p in range(pairs):
            lanes = slice(p * 128, p * 128 + 128)
            top0 = part[m, HEAD_DIM : HEAD_DIM + 1, lanes]
            total0 = part[m, HEAD_DIM + 1 : HEAD_DIM + 2, lanes]
            own = part[m, HEAD_DIM + 2 : HEAD_DIM + 3, lanes]
            top = jnp.maximum(top0, own)
            own_e = jnp.exp(own - top)
            shift = jnp.exp(top0 - top)
            total = total0 * shift + own_e
            inverse = 1.0 / total
            prob = own_e * inverse
            values = to_slot_lanes(sv[here, lanes].astype(F32))
            mixed = part[m, :HEAD_DIM, lanes] * (shift * inverse) + prob * values
            line.append(to_slot_rows(mixed))
            prob_line.append((prob, top + jnp.log(total)))
        lines.append(jnp.concatenate(line, 1))
        probs.append(prob_line)
    written = jnp.concatenate(lines, 0)
    written_low = written.astype(BF16)
    mem_low = mem[...]
    mem_f32 = mem_low.astype(F32)
    update = dot(written_low, wso[...])
    gate = 1.0 / (1.0 + jnp.exp(-dot(mem_low, wfg[...])))
    gain_row = gain[2:3, :]
    hat, inverse = norm_parts(gate * mem_f32 + (1.0 - gate) * update)
    held[...] = hat * gain_row
    cot_f32 = cot[...].astype(F32)
    for m in range(micro):
        at = pl.multiple_of(m * slots + slot_ref[0] * own_rows, own_rows)
        new_ref[m] = held[pl.ds(at, own_rows), :].astype(BF16)
    g_gain[...] = jnp.broadcast_to(jnp.sum(cot_f32 * hat * mine, 0, keepdims=True), g_gain.shape)
    d_blend = norm_back(cot_f32, hat, inverse, gain_row)
    d_pre = (d_blend * (mem_f32 - update) * gate * (1.0 - gate) * mine).astype(BF16)
    d_update = (d_blend * (1.0 - gate)).astype(BF16)
    g_forget[...] = dot_tn(mem_low, d_pre).astype(BF16)
    g_slot_out[...] = dot_tn(written_low, (d_update.astype(F32) * mine).astype(BF16)).astype(BF16)
    base[...] = d_blend * gate * mine + dot_nt(d_pre, wfg[...])
    d_written = dot_nt(d_update, wso[...]).astype(BF16)
    dw_ref[...] = d_written
    dw_f32 = d_written.astype(F32)
    product = dw_f32 * written
    for m in range(micro):
        here = slice(m * slots, (m + 1) * slots)
        for p in range(pairs):
            lanes = slice(p * 128, p * 128 + 128)
            prob, lse = probs[m][p]
            delta = jnp.sum(to_slot_lanes(product[here, lanes]), 0, keepdims=True)
            own_dp = dw_f32[here, lanes] * sv[here, lanes].astype(F32)
            own_dp = jnp.sum(to_slot_lanes(own_dp), 0, keepdims=True)
            own_ds = prob * (own_dp - delta)
            wide = lambda r: to_slot_rows(jnp.broadcast_to(r, (HEAD_DIM, 128)))
            ds_x[here, lanes] = wide(own_ds) * mine[here]
            p_x[here, lanes] = wide(prob) * mine[here]
            rows_ref[m, :, lanes] = jnp.concatenate([lse, delta, jnp.zeros((6, 128), F32)], 0)


def back_kernel(
    q, k, v, sk, sv, sq, keep, da_t, out_t, inv, e_ref, dw, rows_ref, ds_x, p_x,
    dq, dk, dv, dsq, dsk, dsv,
):
    tok = q.shape[0]
    half = tok // 2
    slots = sk.shape[0]
    scaled = q[...] * jnp.asarray(SCALE, BF16)
    keys, values = k[...], v[...]
    slot_keys, slot_values = sk[...], sv[...]
    keys_t = keys.T
    slot_keys_t = slot_keys.T
    norm = jnp.concatenate(
        [jnp.broadcast_to(inv[0, i : i + 1, :], (HEAD_DIM, tok)) for i in range(2)], 0
    )
    da = (da_t[...] * norm).astype(BF16)
    product = da.astype(F32) * out_t[...]
    da_rows = da.T
    dq_parts = []
    dk_a = dk_b = dv_a = dv_b = dk_m = dv_m = 0.0
    for head in range(2):
        rows = slice(head * HEAD_DIM, (head + 1) * HEAD_DIM)
        qm = head_lanes(scaled, head)
        dam_t = head_rows(da, head)
        dam = head_lanes(da_rows, head)
        delta = jnp.sum(product[rows], 0, keepdims=True)
        e_mem = e_ref[0, head, :slots, :]
        e_a = e_ref[0, head, slots : slots + half, :]
        e_b = e_ref[0, head, slots + half :, half:]
        ds_mem = (e_mem.astype(F32) * (dot(slot_values, dam_t) - delta)).astype(BF16)
        ds_a = (e_a.astype(F32) * (dot(values[:half], dam_t) - delta)).astype(BF16)
        ds_b = (
            e_b.astype(F32) * (dot(values[half:], dam_t[:, half:]) - delta[:, half:])
        ).astype(BF16)
        part = dot(slot_keys_t[rows], ds_mem) + dot(keys_t[rows, :half], ds_a)
        part_b = part[:, half:] + dot(keys_t[rows, half:], ds_b)
        dq_parts.append(jnp.concatenate([part[:, :half], part_b], 1))
        dk_a = dk_a + dot(ds_a, qm)
        dk_b = dk_b + dot(ds_b, qm[half:])
        dk_m = dk_m + dot(ds_mem, qm)
        dv_a = dv_a + dot(e_a, dam)
        dv_b = dv_b + dot(e_b, dam[half:])
        dv_m = dv_m + dot(e_mem, dam)
    dq[...] = (jnp.concatenate(dq_parts, 0) * SCALE).T.astype(BF16)

    kept = jnp.broadcast_to(keep[0, 0:1, :], (128, tok)).T
    bias = jnp.where(kept > 0, 0.0, MASKED)
    sq_low = sq[...]
    sq_both = both_heads(sq_low * jnp.asarray(SCALE, BF16))
    dw_low = dw[...]
    dw_both = both_heads(dw_low)
    prob = jnp.exp(dot_nt(keys, sq_both) + bias - rows_ref[0, 0:1, :])
    d_score = (prob * (dot_nt(values, dw_both) - rows_ref[0, 1:2, :])).astype(BF16)
    wk = dot(d_score, sq_both)
    wv = dot(prob.astype(BF16), dw_both)
    dk[:half, :] = (dk_a + wk[:half]).astype(BF16)
    dk[half:, :] = (dk_b + wk[half:]).astype(BF16)
    dv[:half, :] = (dv_a + wv[:half]).astype(BF16)
    dv[half:, :] = (dv_b + wv[half:]).astype(BF16)
    d_read = to_slot_rows(diagonal(dot(keys_t, d_score)))
    own_ds = ds_x[...] * SCALE
    dsq[...] = (d_read * SCALE + own_ds * slot_keys.astype(F32)).astype(BF16)
    dsk[...] = (dk_m + own_ds * sq_low.astype(F32)).astype(BF16)
    dsv[...] = (dv_m + p_x[...] * dw_low.astype(F32)).astype(BF16)


def grads_kernel(normed, dq, dk, dv, mem, dsq, dsk, dsv, gq, gk, gv, gsq):
    rows = normed[...]
    mem_low = mem[...]
    gq[...] = dot_tn(rows, dq[...]).astype(BF16)
    gk[...] = (dot_tn(rows, dk[...]) + dot_tn(mem_low, dsk[...])).astype(BF16)
    gv[...] = (dot_tn(rows, dv[...]) + dot_tn(mem_low, dsv[...])).astype(BF16)
    gsq[...] = dot_tn(mem_low, dsq[...]).astype(BF16)


def input_kernel(
    tok, d_resid, dq, dk, dv, dsq, dsk, dsv, base, wq, wk, wv, wsq, gain,
    tok_grad, d_mem, g_gain,
):
    step = pl.program_id(0)
    hat, inverse = norm_parts(tok[...].astype(F32))
    d_normed = dot_nt(dq[...], wq[...]) + dot_nt(dk[...], wk[...]) + dot_nt(dv[...], wv[...])
    back = norm_back(d_normed, hat, inverse, gain[0:1, :])
    tok_grad[...] = (d_resid[...] + back).astype(BF16)

    @pl.when(step == 0)
    def _():
        g_gain[...] = jnp.zeros_like(g_gain)
        d_mem[...] = (
            base[...]
            + dot_nt(dsq[...], wsq[...])
            + dot_nt(dsk[...], wk[...])
            + dot_nt(dsv[...], wv[...])
        )

    g_gain[0:1, :] += jnp.sum(d_normed * hat, 0, keepdims=True)


def whole(shape):
    return pl.BlockSpec(shape, lambda *_: (0,) * len(shape))


def like(shape, dtype):
    return jax.ShapeDtypeStruct(shape, dtype)


def params(mib):
    return pltpu.CompilerParams(vmem_limit_bytes=mib << 20)


def cost(flops, nbytes, trans=0):
    return pl.CostEstimate(flops=flops, bytes_accessed=nbytes, transcendentals=trans)


def on_device(
    tokens,
    memory,
    doc_lengths,
    key_mask,
    w_query,
    w_key,
    w_value,
    w_out,
    w_up,
    w_down,
    w_slot_query,
    w_slot_out,
    w_forget,
    norm_gain,
    ffn_gain,
    memory_gain,
    out_grad,
    memory_grad,
):
    slot_count = lax.axis_size("slot")
    slot_index = lax.axis_index("slot")
    micro, tok_dev, width = tokens.shape
    slot_rows = memory.shape[2]
    slots = slot_rows * slot_count
    group_tok = tok_dev * slot_count
    dev_start = slot_index * tok_dev
    rows = w_query.shape[0]
    ff = w_up.shape[1]
    cuts = ff // width
    pairs = width // 128
    total = micro * tok_dev
    mem_rows = micro * slots
    keys = tok_dev + slots

    gains = gather_rows(jnp.stack([norm_gain, ffn_gain, memory_gain])[:, None], 0)
    gains = gains.reshape(3, width).astype(F32)
    w_query = gather_rows(w_query[None], 0)[0]
    w_key = gather_rows(w_key[None], 1)[0]
    w_value = gather_rows(w_value[None], 2)[0]
    pair = jnp.stack([memory[:, 0], memory_grad[:, 0]])
    pair = lax.all_gather(pair, "slot", axis=2, tiled=True)
    mem_low = pair[0].reshape(mem_rows, width)
    mem_cot = pair[1].reshape(mem_rows, width)
    mixed = gather_rows(jnp.stack([w_slot_query, w_out, w_slot_out, w_forget]), 0)
    w_slot_query, w_out, w_slot_out, w_forget = mixed[0], mixed[1], mixed[2], mixed[3]
    w_up = gather_rows(w_up.reshape(rows, cuts, width).transpose(1, 0, 2), 1)
    w_down = gather_rows(w_down[None], 2)[0]

    keep = lax.dynamic_slice_in_dim(key_mask, dev_start, tok_dev, 1).astype(F32)
    keep = jnp.broadcast_to(keep[:, None, :], (micro, 8, tok_dev))
    segment = lax.axis_index("batch") * group_tok + dev_start
    positions = segment + jnp.arange(tok_dev, dtype=jnp.int32)
    doc_ends = jnp.cumsum(doc_lengths, axis=1, dtype=jnp.int32)
    passed = positions[None, None, :] >= doc_ends[:, :, None]
    starts = jnp.max(jnp.where(passed, doc_ends[:, :, None] - segment, 0), axis=1)
    starts = jnp.broadcast_to(starts[:, None, :], (micro, 8, tok_dev))

    tok_flat = tokens.reshape(total, width)
    cot_flat = out_grad.reshape(total, width)
    low = lambda n, w: like((n, w), BF16)

    block = tok_dev // 2
    row_block = pl.BlockSpec((block, width), lambda i: (i, 0))
    square = whole((width, width))
    normed, queries, tok_keys, tok_values, slot_keys, slot_values = pl.pallas_call(
        project_kernel,
        grid=(total // block,),
        in_specs=[row_block, whole((mem_rows, width)), whole((3, width)), square, square, square],
        out_specs=[row_block] * 4 + [whole((mem_rows, width))] * 2,
        out_shape=[low(total, width)] * 4 + [low(mem_rows, width)] * 2,
        compiler_params=params(24),
        cost_estimate=cost(6 * total * width * width, 8 << 20),
    )(tok_flat, mem_low, gains, w_query, w_key, w_value)

    def pair_specs(base):
        tok_block = pl.BlockSpec((tok_dev, 128), lambda m, p: (m + base, p))
        slot_block = pl.BlockSpec((slots, 128), lambda m, p: (m + base, p))
        line = pl.BlockSpec((1, 8, tok_dev), lambda m, p: (m + base, 0, 0))
        return tok_block, slot_block, line

    turned = pl.BlockSpec((128, tok_dev), lambda m, p: (m * pairs + p, 0))
    inv_spec = pl.BlockSpec((1, 8, tok_dev), lambda m, p: (m * pairs + p, 0, 0))
    e_spec = pl.BlockSpec((1, 2, keys, tok_dev), lambda m, p: (m * pairs + p, 0, 0, 0))
    tok_block, slot_block, line = pair_specs(0)
    attended, out_t, inv, e_all = pl.pallas_call(
        read_kernel,
        grid=(micro, pairs),
        in_specs=[tok_block] * 3 + [slot_block] * 2 + [line] * 2,
        out_specs=[tok_block, turned, inv_spec, e_spec],
        out_shape=[
            low(total, width),
            like((micro * width, tok_dev), F32),
            like((micro * pairs, 8, tok_dev), F32),
            like((micro * pairs, 2, keys, tok_dev), BF16),
        ],
        scratch_shapes=[pltpu.VMEM((tok_dev, tok_dev), F32)],
        compiler_params=params(24),
        cost_estimate=cost(16 * total * width * keys, 16 << 20, total * keys * HEADS),
    )(queries, tok_keys, tok_values, slot_keys, slot_values, starts, keep)

    slot_queries, part = pl.pallas_call(
        write_kernel,
        out_shape=[low(mem_rows, width), like((micro, 72, slots * HEADS), F32)],
        compiler_params=params(24),
        cost_estimate=cost(8 * total * width * slots, 5 << 20, total * slots * HEADS),
    )(mem_low, w_slot_query, tok_keys, tok_values, slot_keys, keep)

    for axis, distance, _ in stages()[: slot_count.bit_length() - 1]:
        other = swap(part, axis, distance)
        top_a, top_b = part[:, 64:65], other[:, 64:65]
        top = jnp.maximum(top_a, top_b)
        scale_a, scale_b = jnp.exp(top_a - top), jnp.exp(top_b - top)
        mix = part[:, :64] * scale_a + other[:, :64] * scale_b
        tot = part[:, 65:66] * scale_a + other[:, 65:66] * scale_b
        part = jnp.concatenate([mix, top, tot, part[:, 66:]], 1)

    col_block = pl.BlockSpec((width, block), lambda i: (i // 2, i % 2))
    layer_out, d_resid, da_t, g_down, g_up, g_out, g_ffn = pl.pallas_call(
        ffn_kernel,
        grid=(total // block,),
        in_specs=[row_block] * 3
        + [square, whole((cuts, width, width)), whole((ff, width)), whole((3, width))],
        out_specs=[
            row_block,
            row_block,
            col_block,
            whole((ff, width)),
            whole((cuts, width, width)),
            square,
            whole((8, width)),
        ],
        out_shape=[
            low(total, width),
            like((total, width), F32),
            like((micro * width, tok_dev), F32),
            low(ff, width),
            like((cuts, width, width), BF16),
            low(width, width),
            like((8, width), F32),
        ],
        scratch_shapes=[
            pltpu.VMEM((total, ff), BF16),
            pltpu.VMEM((total, ff), BF16),
            pltpu.VMEM((total, width), BF16),
            pltpu.VMEM((total, width), BF16),
            pltpu.VMEM((total, width), BF16),
            pltpu.VMEM((total, width), BF16),
        ],
        compiler_params=params(56),
        cost_estimate=cost(14 * total * width * ff, 20 << 20, total * ff),
    )(attended, tok_flat, cot_flat, w_out, w_up, w_down, gains)

    slot_scalar = jnp.stack([slot_index, slot_index]).astype(jnp.int32)
    slot_like = low(mem_rows, width)
    new_memory, g_forget, g_slot_out, base, d_written, lines, ds_x, p_x, g_mem = pl.pallas_call(
        memory_kernel,
        in_specs=[pl.BlockSpec(memory_space=pltpu.SMEM)]
        + [pl.BlockSpec(memory_space=pltpu.VMEM)] * 9,
        out_shape=[
            like((micro, slot_rows, width), BF16),
            low(width, width),
            low(width, width),
            like((mem_rows, width), F32),
            slot_like,
            like((micro, 8, width), F32),
            like((mem_rows, width), F32),
            like((mem_rows, width), F32),
            like((8, width), F32),
        ],
        scratch_shapes=[pltpu.VMEM((mem_rows, width), F32)],
        compiler_params=params(24),
        cost_estimate=cost(12 * mem_rows * width * width, 6 << 20),
    )(slot_scalar, part, mem_low, mem_cot, slot_keys, slot_values, slot_queries, w_slot_out, w_forget, gains)

    row_line = pl.BlockSpec((1, 8, 128), lambda m, p: (m, 0, p))
    d_queries, d_keys, d_values, d_sq, d_sk, d_sv = pl.pallas_call(
        back_kernel,
        grid=(micro, pairs),
        in_specs=[tok_block] * 3
        + [slot_block] * 3
        + [line, turned, turned, inv_spec, e_spec, slot_block, row_line, slot_block, slot_block],
        out_specs=[tok_block] * 3 + [slot_block] * 3,
        out_shape=[low(total, width)] * 3 + [slot_like] * 3,
        compiler_params=params(24),
        cost_estimate=cost(24 * total * width * keys, 20 << 20, total * slots * HEADS),
    )(
        queries, tok_keys, tok_values, slot_keys, slot_values, slot_queries, keep,
        da_t, out_t, inv, e_all, d_written, lines, ds_x, p_x,
    )

    g_query, g_key, g_value, g_slot_query = pl.pallas_call(
        grads_kernel,
        out_shape=[low(width, width)] * 4,
        compiler_params=params(24),
        cost_estimate=cost(6 * total * width * width, 8 << 20),
    )(normed, d_queries, d_keys, d_values, mem_low, d_sq, d_sk, d_sv)

    mem_whole = whole((mem_rows, width))
    tokens_grad, d_memory, g_norm = pl.pallas_call(
        input_kernel,
        grid=(total // block,),
        in_specs=[row_block] * 5 + [mem_whole] * 4 + [square] * 4 + [whole((3, width))],
        out_specs=[row_block, mem_whole, whole((8, width))],
        out_shape=[low(total, width), like((mem_rows, width), F32), like((8, width), F32)],
        compiler_params=params(24),
        cost_estimate=cost(6 * total * width * width, 12 << 20),
    )(
        tok_flat, d_resid, d_queries, d_keys, d_values, d_sq, d_sk, d_sv, base,
        w_query, w_key, w_value, w_slot_query, gains,
    )

    moved = d_memory.reshape(micro, slots, width)
    for axis, distance, _ in reversed(stages()[: slot_count.bit_length() - 1]):
        half = moved.shape[1] // 2
        bit = own_bit(axis, distance)
        send = lax.dynamic_slice_in_dim(moved, (1 - bit) * half, half, 1)
        held = lax.dynamic_slice_in_dim(moved, bit * half, half, 1)
        moved = held + swap(send, axis, distance)

    down_share = scatter_sum(g_down[None], 2)[0]
    up_share = scatter_sum(g_up, 1).transpose(1, 0, 2).reshape(rows, ff)
    mixed = jnp.stack([g_slot_query, g_out, g_slot_out, g_forget])
    mixed_share = scatter_sum(mixed, 0)
    query_share = scatter_sum(g_query[None], 0)[0]
    key_share = scatter_sum(g_key[None], 1)[0]
    value_share = scatter_sum(g_value[None], 2)[0]
    gain_grads = jnp.stack([g_norm[0], g_ffn[0], g_mem[0]])
    gain_share = scatter_sum(gain_grads.reshape(3, -1, 1, rows).reshape(3, -1, rows), 0)[:, 0]
    out = lambda m: m.astype(F32)
    return (
        layer_out.reshape(micro, tok_dev, width),
        new_memory[:, None],
        tokens_grad.reshape(micro, tok_dev, width),
        moved.astype(BF16)[:, None],
        out(query_share),
        out(key_share),
        out(value_share),
        out(mixed_share[1]),
        out(up_share),
        out(down_share),
        out(mixed_share[0]),
        out(mixed_share[2]),
        out(mixed_share[3]),
        gain_share[0],
        gain_share[1],
        gain_share[2],
    )


def solution(mesh):
    weight = P(("batch", "slot"), None)
    gain = P(("batch", "slot"))
    rows = P(None, ("batch", "slot"), None)
    slots = P(None, "batch", "slot", None)
    return jax.shard_map(
        on_device,
        mesh=mesh,
        in_specs=(rows, slots, P(), P(None, "batch")) + (weight,) * 9 + (gain,) * 3 + (rows, slots),
        out_specs=(rows, slots, rows, slots) + (weight,) * 9 + (gain,) * 3,
        check_vma=False,
    )
```

```python
import functools

import jax
import jax.numpy as jnp
from jax import lax
from jax.experimental import pallas as pl
from jax.experimental.pallas import tpu as pltpu
from jax.sharding import PartitionSpec as P

HEADS = 8
HEAD_DIM = 64
SEG = 512
EPSILON = 1e-05
MASKED = -1e30
BF16 = jnp.bfloat16
F32 = jnp.float32
SCALE = HEAD_DIM ** (-0.5)
SMEM = pl.BlockSpec(memory_space=pltpu.SMEM)
VMEM = pl.BlockSpec(memory_space=pltpu.VMEM)
ANY = pl.BlockSpec(memory_space=pl.ANY)


def swap(value, axis, distance):
    pairs = [(i, i ^ distance) for i in range(lax.axis_size(axis))]
    return lax.ppermute(value, axis, pairs)


def own_bit(axis, distance):
    return (lax.axis_index(axis) // distance) % 2


def axis_bits(axis):
    return [(axis, 1 << i) for i in range(lax.axis_size(axis).bit_length() - 1)]


def exchange_orders(turn):
    rest = axis_bits("slot")[1:] + axis_bits("batch")
    if turn:
        rest = rest[2:3] + rest[:2] + rest[3:]
    other = list(rest)
    for i in range(0, len(rest) - 1, 2):
        other[i], other[i + 1] = rest[i + 1], rest[i]
    return rest, other


def lane_swap(value, orders, step):
    slots = lax.axis_size("slot")
    pairs = []
    for batch in range(lax.axis_size("batch")):
        for slot in range(slots):
            axis, distance = orders[slot % 2][step]
            to_batch, to_slot = batch, slot
            if axis == "batch":
                to_batch = batch ^ distance
            else:
                to_slot = slot ^ distance
            pairs.append((batch * slots + slot, to_batch * slots + to_slot))
    return lax.ppermute(value, ("batch", "slot"), pairs)


def lane_bit(orders, step):
    lane = own_bit("slot", 1)
    return jnp.where(lane == 0, own_bit(*orders[0][step]), own_bit(*orders[1][step]))


def own_info():
    slot = lax.axis_index("slot")
    info = [own_bit("slot", 1), slot, lax.axis_index("batch") * lax.axis_size("slot") + slot]
    for turn in range(2):
        orders = exchange_orders(turn)
        info += [lane_bit(orders, step) for step in range(len(orders[0]))]
    return jnp.stack([jnp.asarray(entry, jnp.int32) for entry in info])


def info_at(turn, step):
    return 3 + turn * len(exchange_orders(0)[0]) + step


def chunk_places(order):
    natural = (axis_bits("slot")[1:] + axis_bits("batch"))
    count = len(order)
    places = []
    for pair in range(1 << count):
        place = 0
        for step, bit in enumerate(order):
            place |= ((pair >> natural.index(bit)) & 1) << (count - 1 - step)
        places.append(place)
    return places


def tie(value, after):
    return lax.optimization_barrier((value,) + tuple(after))[0] if after else value


class Gather:
    def __init__(self, held, turn, left=None):
        self.turn, self.orders = turn, exchange_orders(turn)
        self.left = len(self.orders[0]) if left is None else left
        self.held, self.got = held, None

    def launch(self, after=()):
        held = tie(self.held, after)
        if self.left == 0:
            self.got = swap(held, "slot", 1)
            return
        self.left -= 1
        self.got = lane_swap(held, self.orders, self.left)

    def finish(self, after=()):
        mine = lane_bit(self.orders, self.left)
        got = tie(self.got, after)
        low = jnp.where(mine == 0, self.held, got)
        high = jnp.where(mine == 0, got, self.held)
        self.held = jnp.concatenate([low, high], 0)
        return self.held

    def until(self, left, after=()):
        while self.left > left:
            self.launch(after)
            self.finish()
        return self.held

    def unpack(self, sections, me, after=()):
        return unpack(self.held, self.got, self.turn, sections, me, after)


def place_kernel(places, sections, me_ref, held, got, *outs):
    for lane in range(2):

        @pl.when(me_ref[0] == lane)
        def _():
            for kind in range(2):
                source = held if kind == lane else got
                for pair, place in enumerate(places[kind]):
                    device = 2 * pair + kind
                    for (at, rows, lead), out in zip(sections, outs):
                        for i in range(lead):
                            here = slice(device * rows, (device + 1) * rows)
                            out[i, here, :] = source[place, at + i * rows : at + (i + 1) * rows, :]


def unpack(held, got, turn, sections, me, after):
    orders = exchange_orders(turn)
    places = [chunk_places(order) for order in orders]
    count, _, width = held.shape
    if all(rows % 16 == 0 for _, rows, _ in sections):
        body = functools.partial(place_kernel, places, sections)
        outs = [like((lead, 2 * count * rows, width), BF16) for _, rows, lead in sections]
        return kernel_call(
            body, [me, held, got], outs, 4, cost(0, 4 * held.size), "place", after
        )
    low = jnp.where(me[0] == 0, held, got)[jnp.array(places[0])]
    high = jnp.where(me[0] == 0, got, held)[jnp.array(places[1])]
    full = jnp.stack([low, high], 1).reshape(2 * count, -1, width)
    outs = []
    for at, rows, lead in sections:
        part = full[:, at : at + rows * lead].reshape(2 * count, lead, rows, width)
        outs.append(part.transpose(1, 0, 2, 3).reshape(lead, -1, width))
    return outs


class Shares:
    def __init__(self, turn, sections, me, width):
        self.turn, self.sections, self.me, self.width = turn, sections, me, width
        self.rows = sum(rows * lead for _, rows, lead in sections)
        self.places = [chunk_places(order) for order in exchange_orders(turn)]
        self.count = len(self.places[0])
        self.direct = all(rows % 16 == 0 for _, rows, _ in sections)

    def shapes(self):
        if self.direct:
            return [like((self.count, self.rows, self.width), BF16)] * 2
        return [
            like((lead, 2 * self.count * rows, self.width), BF16)
            for _, rows, lead in self.sections
        ]

    def put(self, refs, me_ref, section, lead, first_row, value):
        at, rows, _ = self.sections[section]
        if not self.direct:
            refs[section][lead, first_row : first_row + value.shape[0], :] = value
            return
        keep, send = refs
        at = at + lead * rows
        for lane in range(2):

            @pl.when(me_ref[0] == lane)
            def _():
                for i in range(value.shape[0] // rows):
                    device = first_row // rows + i
                    target = keep if device % 2 == lane else send
                    place = self.places[device % 2][device // 2]
                    target[place, at : at + rows, :] = value[i * rows : (i + 1) * rows]

    def split(self, outs):
        if self.direct:
            return outs
        parts = []
        for (_, rows, lead), out in zip(self.sections, outs):
            part = out.reshape(lead, 2 * self.count, rows, self.width).transpose(1, 0, 2, 3)
            parts.append(part.reshape(2 * self.count, lead * rows, self.width))
        full = jnp.concatenate(parts, 1).reshape(self.count, 2, -1, self.width)
        back = []
        for kind in range(2):
            order = [0] * self.count
            for pair, place in enumerate(self.places[kind]):
                order[place] = pair
            back.append(full[:, kind][jnp.array(order)])
        lane = self.me[0]
        return [jnp.where(lane == 0, back[0], back[1]), jnp.where(lane == 0, back[1], back[0])]

    def begin(self, outs, after=()):
        self.orders = exchange_orders(self.turn)
        self.steps = len(self.orders[0])
        self.done = 0
        self.keep, self.send = self.split(outs)
        self.got = swap(tie(self.send, after), "slot", 1)

    def finish(self, after=()):
        at = info_at(self.turn, self.done)
        self.keep, self.send = halve(self.keep, self.got, self.me, at, self.direct, after)
        return self.send

    def launch(self, after=()):
        self.got = lane_swap(tie(self.send, after), self.orders, self.done)
        self.done += 1

    def end(self):
        return self.keep[0].astype(F32) + self.got[0].astype(F32)


def halve_kernel(at, info, keep, got, keep_out, send_out):
    half = keep_out.shape[0]
    mine = pl.ds(info[at] * half, half)
    other = pl.ds((1 - info[at]) * half, half)
    send_out[...] = keep[other] + got[other]
    keep_out[...] = keep[mine] + got[mine]


def halve(keep, got, info, at, direct, after):
    count, rows, width = keep.shape
    half = count // 2
    if direct:
        return kernel_call(
            functools.partial(halve_kernel, at),
            [info, keep, got],
            [like((half, rows, width), BF16)] * 2,
            4,
            cost(keep.size, 6 * keep.size),
            "halve",
            after,
        )
    bit = info[at]
    total = tie(keep, after) + got
    take = lambda b: lax.dynamic_slice_in_dim(total, b * half, half, 0)
    return take(bit), take(1 - bit)


def dot(a, b):
    return jnp.dot(a, b, preferred_element_type=F32)


def dot_nt(a, b):
    return lax.dot_general(a, b, (((1,), (1,)), ((), ())), preferred_element_type=F32)


def dot_tn(a, b):
    return lax.dot_general(a, b, (((0,), (0,)), ((), ())), preferred_element_type=F32)


def norm_parts(rows):
    centre = jnp.mean(rows, axis=-1, keepdims=True)
    centred = rows - centre
    spread = jnp.mean(centred * centred, axis=-1, keepdims=True)
    inverse = lax.rsqrt(spread + EPSILON)
    return centred * inverse, inverse


def norm_back(cot, hat, inverse, gain):
    d_hat = cot * gain
    first = jnp.mean(d_hat, axis=-1, keepdims=True)
    second = jnp.mean(d_hat * hat, axis=-1, keepdims=True)
    return inverse * (d_hat - first - hat * second)


def head_lanes(value, head):
    lane = lax.broadcasted_iota(jnp.int32, value.shape, 1)
    return jnp.where(lane // HEAD_DIM == head, value, jnp.zeros_like(value))


def head_rows(value, head):
    row = lax.broadcasted_iota(jnp.int32, value.shape, 0)
    return jnp.where(row // HEAD_DIM == head, value, jnp.zeros_like(value))


def both_heads(value):
    return jnp.concatenate([head_lanes(value, 0), head_lanes(value, 1)], 0)


def to_slot_lanes(value):
    turned = value.T
    return jnp.concatenate([turned[:HEAD_DIM], turned[HEAD_DIM:]], 1)


def to_slot_rows(value):
    turned = value.T
    half = turned.shape[0] // 2
    return jnp.concatenate([turned[:half], turned[half:]], 1)


def diagonal(value):
    lane = lax.broadcasted_iota(jnp.int32, (HEAD_DIM, value.shape[1]), 1)
    return jnp.where(lane < value.shape[1] // 2, value[:HEAD_DIM], value[HEAD_DIM:])


ROWS = 256


def row_loop(total):
    return lambda body: pl.loop(0, total // ROWS)(
        lambda i: body(pl.ds(pl.multiple_of(i * ROWS, ROWS), ROWS))
    )


def pair_loop(width):
    return lambda body: pl.loop(0, width // 128)(
        lambda p: body(p, pl.ds(pl.multiple_of(p * 128, 128), 128))
    )


def project_kernel(tok, mem, gain, wq, wk, wv, normed, q, k, v, sk, sv):
    @row_loop(tok.shape[0])
    def _(here):
        hat, _ = norm_parts(tok[here, :].astype(F32))
        low = (hat * gain[0:1, :]).astype(BF16)
        normed[here, :] = low
        q[here, :] = dot(low, wq[...]).astype(BF16)
        k[here, :] = dot(low, wk[...]).astype(BF16)
        v[here, :] = dot(low, wv[...]).astype(BF16)

    sk[...] = dot(mem[...], wk[...]).astype(BF16)
    sv[...] = dot(mem[...], wv[...]).astype(BF16)


def read_kernel(m, q, k, v, sk, sv, starts, keep, attended, out_t, inv, e_far, bias, e_buf, sems):
    tok = attended.shape[0]
    slots = sk.shape[0] // keep.shape[0]
    key_at = lax.broadcasted_iota(jnp.int32, (tok, tok), 0)
    query_at = lax.broadcasted_iota(jnp.int32, (tok, tok), 1)
    start = starts[m, 0:1, :]
    kept = jnp.broadcast_to(keep[m, 0:1, :], (128, tok)).T
    kept = jnp.concatenate([kept] * (tok // 128), 1)
    good = (key_at >= start) & (key_at <= query_at) & (kept > 0)
    bias[...] = jnp.where(good, 0.0, MASKED)
    here, slot_here = pl.ds(m * tok, tok), pl.ds(m * slots, slots)

    pairs = q.shape[1] // 128
    copy = lambda p: pltpu.make_async_copy(e_buf.at[p % 2], e_far.at[p], sems.at[p % 2])

    @pair_loop(q.shape[1])
    def _(p, lanes):
        @pl.when(p >= 2)
        def _():
            copy(p - 2).wait()

        read_pair(
            q[here, lanes], k[here, lanes], v[here, lanes], sk[slot_here, lanes],
            sv[slot_here, lanes], bias, attended.at[:, lanes],
            out_t.at[pl.ds(pl.multiple_of(p * 128, 128), 128), :], inv.at[p], e_buf.at[p % 2],
        )
        copy(p).start()

    for p in range(pairs - 2, pairs):
        copy(p).wait()


def read_pair(q, keys, values, slot_keys, slot_values, bias, attended, out_t, inv, e_ref):
    tok = q.shape[0]
    half = tok // 2
    slots = slot_keys.shape[0]
    scaled = q * jnp.asarray(SCALE, BF16)
    values_t = values.T
    slot_values_t = slot_values.T
    outs, inverses = [], []
    for head in range(2):
        qm = head_lanes(scaled, head)
        rows = slice(head * HEAD_DIM, (head + 1) * HEAD_DIM)
        s_mem = dot_nt(slot_keys, qm)
        s_a = dot_nt(keys[:half], qm) + bias[:half, :]
        s_b = dot_nt(keys[half:], qm[half:]) + bias[half:, half:]
        top = jnp.maximum(jnp.max(s_mem, 0, keepdims=True), jnp.max(s_a, 0, keepdims=True))
        top_b = jnp.maximum(top[:, half:], jnp.max(s_b, 0, keepdims=True))
        top = jnp.concatenate([top[:, :half], top_b], 1)
        e_mem = jnp.exp(s_mem - top)
        e_a = jnp.exp(s_a - top)
        e_b = jnp.exp(s_b - top_b)
        total = jnp.sum(e_mem, 0, keepdims=True) + jnp.sum(e_a, 0, keepdims=True)
        total_b = total[:, half:] + jnp.sum(e_b, 0, keepdims=True)
        total = jnp.concatenate([total[:, :half], total_b], 1)
        e_mem, e_a, e_b = e_mem.astype(BF16), e_a.astype(BF16), e_b.astype(BF16)
        e_ref[head, :slots, :] = e_mem
        e_ref[head, slots : slots + half, :] = e_a
        e_ref[head, slots + half :, half:] = e_b
        e_ref[head, slots + half :, :half] = jnp.zeros((half, half), BF16)
        mix = dot(slot_values_t[rows], e_mem) + dot(values_t[rows, :half], e_a)
        mix_b = mix[:, half:] + dot(values_t[rows, half:], e_b)
        mix = jnp.concatenate([mix[:, :half], mix_b], 1)
        inverse = 1.0 / total
        outs.append(mix * inverse)
        inverses.append(inverse)
    out = jnp.concatenate(outs, 0)
    out_t[...] = out
    inv[...] = jnp.concatenate(inverses + [jnp.zeros((6, tok), F32)], 0)
    attended[...] = out.T.astype(BF16)


def write_kernel(mem, wsq, k, v, sk, keep, sq_ref, part):
    micro = keep.shape[0]
    tok = k.shape[0] // micro
    slots = mem.shape[0] // micro
    pairs = k.shape[1] // 128
    sq = dot(mem[...], wsq[...]).astype(BF16)
    sq_ref[...] = sq
    for m in range(micro):
        kept = jnp.broadcast_to(keep[m, 0:1, :], (128, tok)).T
        bias = jnp.where(kept > 0, 0.0, MASKED)
        for p in range(pairs):
            lanes = slice(p * 128, p * 128 + 128)
            mine = sq[m * slots : (m + 1) * slots, lanes]
            own = to_slot_lanes(
                mine.astype(F32) * sk[m * slots : (m + 1) * slots, lanes].astype(F32)
            )
            own = jnp.sum(own, 0, keepdims=True) * SCALE
            scores = dot_nt(k[m * tok : (m + 1) * tok, lanes], both_heads(mine)) * SCALE + bias
            top = jnp.maximum(jnp.max(scores, 0, keepdims=True), own)
            e = jnp.exp(scores - top)
            total = jnp.sum(e, 0, keepdims=True)
            mix = diagonal(dot_tn(v[m * tok : (m + 1) * tok, lanes], e.astype(BF16)))
            part[m, :HEAD_DIM, lanes] = mix
            part[m, HEAD_DIM:, lanes] = jnp.concatenate(
                [top, total, own, jnp.zeros((5, 128), F32)], 0
            )


def gelu_pair(hidden):
    root = 0.7978845608028654
    square = hidden * hidden
    bent = jnp.tanh(hidden * (root + (root * 0.044715) * square))
    half = 0.5 + 0.5 * bent
    slope = half + (0.5 * hidden) * (1.0 - bent * bent) * (root + (3.0 * root * 0.044715) * square)
    return (hidden * half).astype(BF16), slope


def ffn_cuts(low, cot_low, up, down, here, act_all, dh_all):
    width = low.shape[1]
    out = d_low = 0.0
    for cut in range(up.shape[0]):
        cols = slice(cut * width, (cut + 1) * width)
        act, slope = gelu_pair(dot(low, up[cut]))
        d_hidden = (dot_nt(cot_low, down[cols, :]) * slope).astype(BF16)
        act_all[here, cols] = act
        dh_all[here, cols] = d_hidden
        out = out + dot(act, down[cols, :])
        d_low = d_low + dot_nt(d_hidden, up[cut])
    return out, d_low


def ffn_grads(shares, refs, me_ref, base, low_all, cot_all, act_all, dh_all, cuts):
    width = low_all.shape[1]
    low_t = low_all[...].T
    for cut in range(cuts):
        cols = slice(cut * width, (cut + 1) * width)
        shares.put(refs, me_ref, base, cut, 0, dot(low_t, dh_all[:, cols]).astype(BF16))
        grad = dot_tn(act_all[:, cols], cot_all[...]).astype(BF16)
        shares.put(refs, me_ref, base + 1, 0, cut * width, grad)


def ffn_first_kernel(
    shares, me_ref, att_a, att_b, tok, cot, wout, up, down, gain,
    resid_ref, out_ref, d_low_ref, *rest
):
    refs, (act_all, dh_all, low_all) = rest[:-3], rest[-3:]
    count = att_a.shape[0]
    for m, att in enumerate((att_a, att_b)):

        @row_loop(count)
        def _(there):
            here = pl.ds(there.start + m * count, ROWS)
            resid = tok[here, :].astype(F32) + dot(att[there, :], wout[...])
            hat, _ = norm_parts(resid)
            low = (hat * gain[1:2, :]).astype(BF16)
            low_all[here, :] = low
            out, d_low = ffn_cuts(low, cot[here, :], up, down, here, act_all, dh_all)
            resid_ref[here, :] = resid
            out_ref[here, :] = resid + out
            d_low_ref[here, :] = d_low

    ffn_grads(shares, refs, me_ref, 0, low_all, cot, act_all, dh_all, up.shape[0])


def ffn_second_kernel(
    shares, me_ref, att_a, att_b, resid, part, d_part, cot, wout, up, down, gain,
    mem, d_pre, written, d_upd, dsq,
    layer_out, d_resid_ref, da_a, da_b, g_gain, *rest
):
    refs, (act_all, dh_all, low_all, dattn_all) = rest[:-4], rest[-4:]
    count = att_a.shape[0]
    gain_row = gain[1:2, :]
    g_gain[...] = jnp.zeros_like(g_gain)
    for m, da_t in enumerate((da_a, da_b)):

        @row_loop(count)
        def _(there):
            here = pl.ds(there.start + m * count, ROWS)
            hat, inverse = norm_parts(resid[here, :])
            low = (hat * gain_row).astype(BF16)
            low_all[here, :] = low
            cot_low = cot[here, :]
            out, d_low = ffn_cuts(low, cot_low, up, down, here, act_all, dh_all)
            layer_out[here, :] = (part[here, :] + out).astype(BF16)
            d_low = d_part[here, :] + d_low
            d_resid = cot_low.astype(F32) + norm_back(d_low, hat, inverse, gain_row)
            d_resid_ref[here, :] = d_resid
            d_attn = d_resid.astype(BF16)
            dattn_all[here, :] = d_attn
            da_t[:, there] = dot_nt(wout[...], d_attn)
            g_gain[0:1, :] += jnp.sum(d_low * hat, 0, keepdims=True)

    ffn_grads(shares, refs, me_ref, 0, low_all, cot, act_all, dh_all, up.shape[0])
    mem_t = mem[...].T
    grad = dot_tn(att_a[...], dattn_all[:count, :]) + dot_tn(att_b[...], dattn_all[count:, :])
    shares.put(refs, me_ref, 2, 0, 0, grad.astype(BF16))
    shares.put(refs, me_ref, 3, 0, 0, dot(mem_t, dsq[...]).astype(BF16))
    shares.put(refs, me_ref, 4, 0, 0, dot_tn(written[...], d_upd[...]).astype(BF16))
    shares.put(refs, me_ref, 5, 0, 0, dot(mem_t, d_pre[...]).astype(BF16))


def memory_kernel(
    slot_ref, part, mem, cot, sk, sv, sq, k, v, keep, wso, wfg, gain,
    new_ref, base, d_pre_ref, written_ref, d_upd_ref, dsq_ref, osk, osv, wdk, wdv, g_gain,
    held,
):
    micro = part.shape[0]
    slots = mem.shape[0] // micro
    own_rows = new_ref.shape[1]
    pairs = mem.shape[1] // 128
    row_at = lax.broadcasted_iota(jnp.int32, (mem.shape[0], 1), 0)
    mine = ((row_at % slots) // own_rows == slot_ref[1]).astype(F32)
    probs, tots, lses = [], [], []
    lines = []
    for m in range(micro):
        here = slice(m * slots, (m + 1) * slots)
        line, prob_line = [], []
        for p in range(pairs):
            lanes = slice(p * 128, p * 128 + 128)
            top0 = part[m, HEAD_DIM : HEAD_DIM + 1, lanes]
            total0 = part[m, HEAD_DIM + 1 : HEAD_DIM + 2, lanes]
            own = part[m, HEAD_DIM + 2 : HEAD_DIM + 3, lanes]
            top = jnp.maximum(top0, own)
            own_e = jnp.exp(own - top)
            shift = jnp.exp(top0 - top)
            total = total0 * shift + own_e
            inverse = 1.0 / total
            prob = own_e * inverse
            values = to_slot_lanes(sv[here, lanes].astype(F32))
            mixed = part[m, :HEAD_DIM, lanes] * (shift * inverse) + prob * values
            line.append(to_slot_rows(mixed))
            prob_line.append((prob, top + jnp.log(total)))
        lines.append(jnp.concatenate(line, 1))
        probs.append(prob_line)
    written = jnp.concatenate(lines, 0)
    written_low = written.astype(BF16)
    mem_low = mem[...]
    mem_f32 = mem_low.astype(F32)
    update = dot(written_low, wso[...])
    gate = 1.0 / (1.0 + jnp.exp(-dot(mem_low, wfg[...])))
    gain_row = gain[2:3, :]
    hat, inverse = norm_parts(gate * mem_f32 + (1.0 - gate) * update)
    held[...] = hat * gain_row
    cot_f32 = cot[...].astype(F32)
    for m in range(micro):
        at = pl.multiple_of(m * slots + slot_ref[1] * own_rows, own_rows)
        new_ref[m] = held[pl.ds(at, own_rows), :].astype(BF16)
    g_gain[...] = jnp.broadcast_to(jnp.sum(cot_f32 * hat * mine, 0, keepdims=True), g_gain.shape)
    d_blend = norm_back(cot_f32, hat, inverse, gain_row)
    d_pre = (d_blend * (mem_f32 - update) * gate * (1.0 - gate) * mine).astype(BF16)
    d_update = (d_blend * (1.0 - gate)).astype(BF16)
    d_pre_ref[...] = d_pre
    written_ref[...] = written_low
    d_upd_ref[...] = (d_update.astype(F32) * mine).astype(BF16)
    base[...] = d_blend * gate * mine + dot_nt(d_pre, wfg[...])
    d_written = dot_nt(d_update, wso[...]).astype(BF16)
    dw_f32 = d_written.astype(F32)
    product = dw_f32 * written
    tok = k.shape[0] // micro
    for m in range(micro):
        here = slice(m * slots, (m + 1) * slots)
        there = slice(m * tok, (m + 1) * tok)
        kept = jnp.broadcast_to(keep[m, 0:1, :], (128, tok)).T
        bias = jnp.where(kept > 0, 0.0, MASKED)
        for p in range(pairs):
            lanes = slice(p * 128, p * 128 + 128)
            prob, lse = probs[m][p]
            values_f32 = sv[here, lanes].astype(F32)
            delta = jnp.sum(to_slot_lanes(product[here, lanes]), 0, keepdims=True)
            own_dp = jnp.sum(to_slot_lanes(dw_f32[here, lanes] * values_f32), 0, keepdims=True)
            own_ds = prob * (own_dp - delta)
            wide = lambda r: to_slot_rows(jnp.broadcast_to(r, (HEAD_DIM, 2 * slots)))
            own_ds = wide(own_ds) * mine[here] * SCALE
            own_p = wide(prob) * mine[here]
            sq_low = sq[here, lanes]
            sq_both = both_heads(sq_low * jnp.asarray(SCALE, BF16))
            dw_low = d_written[here, lanes]
            dw_both = both_heads(dw_low)
            keys, values = k[there, lanes], v[there, lanes]
            prob = jnp.exp(dot_nt(keys, sq_both) + bias - lse)
            d_score = (prob * (dot_nt(values, dw_both) - delta)).astype(BF16)
            wdk[there, lanes] = dot(d_score, sq_both).astype(BF16)
            wdv[there, lanes] = dot(prob.astype(BF16), dw_both).astype(BF16)
            d_read = to_slot_rows(diagonal(dot_tn(keys, d_score)))
            slot_keys = sk[here, lanes].astype(F32)
            dsq_ref[here, lanes] = (d_read * SCALE + own_ds * slot_keys).astype(BF16)
            osk[here, lanes] = own_ds * sq_low.astype(F32)
            osv[here, lanes] = own_p * dw_low.astype(F32)


def back_kernel(
    m, q, k, v, sk, sv, da_t, out_t, inv, e_far, wdk, wdv, osk, osv, dq, dk, dv, dsk, dsv,
    e_buf, sems,
):
    tok, slots = dq.shape[0], dsk.shape[0]
    here, slot_here = pl.ds(m * tok, tok), pl.ds(m * slots, slots)

    pairs = q.shape[1] // 128
    copy = lambda p: pltpu.make_async_copy(e_far.at[p], e_buf.at[p % 2], sems.at[p % 2])
    copy(0).start()

    @pair_loop(q.shape[1])
    def _(p, lanes):
        @pl.when(p + 1 < pairs)
        def _():
            copy(p + 1).start()

        copy(p).wait()
        turned = pl.ds(pl.multiple_of(p * 128, 128), 128)
        back_pair(
            q[here, lanes], k[here, lanes], v[here, lanes], sk[slot_here, lanes],
            sv[slot_here, lanes], da_t.at[turned, :], out_t.at[turned, :], inv.at[p],
            e_buf.at[p % 2], wdk.at[here, lanes], wdv.at[here, lanes], osk.at[slot_here, lanes],
            osv.at[slot_here, lanes], dq.at[:, lanes], dk.at[:, lanes], dv.at[:, lanes],
            dsk.at[:, lanes], dsv.at[:, lanes],
        )


def back_pair(
    q, keys, values, slot_keys, slot_values, da_t, out_t, inv, e_ref, wdk, wdv, osk, osv,
    dq, dk, dv, dsk, dsv,
):
    tok = q.shape[0]
    half = tok // 2
    slots = slot_keys.shape[0]
    scaled = q * jnp.asarray(SCALE, BF16)
    keys_t = keys.T
    slot_keys_t = slot_keys.T
    norm = jnp.concatenate(
        [jnp.broadcast_to(inv[i : i + 1, :], (HEAD_DIM, tok)) for i in range(2)], 0
    )
    da = (da_t[...] * norm).astype(BF16)
    product = da.astype(F32) * out_t[...]
    da_rows = da.T
    dq_parts = []
    dk_a = dk_b = dv_a = dv_b = dk_m = dv_m = 0.0
    for head in range(2):
        rows = slice(head * HEAD_DIM, (head + 1) * HEAD_DIM)
        qm = head_lanes(scaled, head)
        dam_t = head_rows(da, head)
        dam = head_lanes(da_rows, head)
        delta = jnp.sum(product[rows], 0, keepdims=True)
        e_mem = e_ref[head, :slots, :]
        e_a = e_ref[head, slots : slots + half, :]
        e_b = e_ref[head, slots + half :, half:]
        ds_mem = (e_mem.astype(F32) * (dot(slot_values, dam_t) - delta)).astype(BF16)
        ds_a = (e_a.astype(F32) * (dot(values[:half], dam_t) - delta)).astype(BF16)
        ds_b = (
            e_b.astype(F32) * (dot(values[half:], dam_t[:, half:]) - delta[:, half:])
        ).astype(BF16)
        part = dot(slot_keys_t[rows], ds_mem) + dot(keys_t[rows, :half], ds_a)
        part_b = part[:, half:] + dot(keys_t[rows, half:], ds_b)
        dq_parts.append(jnp.concatenate([part[:, :half], part_b], 1))
        dk_a = dk_a + dot(ds_a, qm)
        dk_b = dk_b + dot(ds_b, qm[half:])
        dk_m = dk_m + dot(ds_mem, qm)
        dv_a = dv_a + dot(e_a, dam)
        dv_b = dv_b + dot(e_b, dam[half:])
        dv_m = dv_m + dot(e_mem, dam)
    dq[...] = (jnp.concatenate(dq_parts, 0) * SCALE).T.astype(BF16)

    dk[:half, :] = (dk_a + wdk[:half, :].astype(F32)).astype(BF16)
    dk[half:, :] = (dk_b + wdk[half:, :].astype(F32)).astype(BF16)
    dv[:half, :] = (dv_a + wdv[:half, :].astype(F32)).astype(BF16)
    dv[half:, :] = (dv_b + wdv[half:, :].astype(F32)).astype(BF16)
    dsk[...] = (dk_m + osk[...]).astype(BF16)
    dsv[...] = (dv_m + osv[...]).astype(BF16)


def grads_kernel(
    shares, me_ref, normed, dq_a, dk_a, dv_a, dsk_a, dsv_a, dq_b, dk_b, dv_b, dsk_b, dsv_b,
    mem, wq, wk, wv, gain, g_ffn, g_mem, *refs
):
    count = dq_a.shape[0]
    slots = dsk_a.shape[0]
    rows_t = normed[...].T
    mem_t = mem[...].T
    weighted = 0.0
    sets = (
        (dq_a, dq_b, wq, None, None),
        (dk_a, dk_b, wk, dsk_a, dsk_b),
        (dv_a, dv_b, wv, dsv_a, dsv_b),
    )
    for i, (cot_a, cot_b, weight, slot_a, slot_b) in enumerate(sets):
        grad = dot(rows_t[:, :count], cot_a[...]) + dot(rows_t[:, count:], cot_b[...])
        weighted = weighted + grad * weight[...].astype(F32)
        if slot_a is not None:
            slot_cot = jnp.concatenate([slot_a[...], slot_b[...]], 0)
            grad = grad + dot(mem_t, slot_cot)
        shares.put(refs, me_ref, i, 0, 0, grad.astype(BF16))
    folded = weighted[:, :128]
    for i in range(1, weighted.shape[1] // 128):
        folded = folded + weighted[:, i * 128 : (i + 1) * 128]
    line = jnp.sum(folded.T, 0, keepdims=True) / gain[0:1, :]
    lines = [line, g_ffn[0:1, :], g_mem[0:1, :]]
    extra = shares.sections[3][1]
    lines = jnp.concatenate(lines + [jnp.zeros((extra - 3, line.shape[1]), F32)], 0).astype(BF16)
    for device in range(2 * shares.count):
        shares.put(refs, me_ref, 3, 0, device * extra, lines)


def last_kernel(
    shares, me_ref, normed, tok, d_resid,
    dq_a, dk_a, dv_a, dsk_a, dsv_a, dq_b, dk_b, dv_b, dsk_b, dsv_b, dsq, base, mem,
    wq, wk, wv, wsq, gain, g_ffn, g_mem, tok_grad, mem_keep, mem_send, *rest
):
    grads_kernel(
        shares, me_ref, normed, dq_a, dk_a, dv_a, dsk_a, dsv_a, dq_b, dk_b, dv_b, dsk_b, dsv_b,
        mem, wq, wk, wv, gain, g_ffn, g_mem, *rest[:-1]
    )
    d_mem = rest[-1]
    count = dq_a.shape[0]
    for m, (dq, dk, dv) in enumerate(((dq_a, dk_a, dv_a), (dq_b, dk_b, dv_b))):

        @row_loop(count)
        def _(there):
            here = pl.ds(there.start + m * count, ROWS)
            hat, inverse = norm_parts(tok[here, :].astype(F32))
            d_normed = dot_nt(dq[there, :], wq[...]) + dot_nt(dk[there, :], wk[...])
            d_normed = d_normed + dot_nt(dv[there, :], wv[...])
            back = norm_back(d_normed, hat, inverse, gain[0:1, :])
            tok_grad[here, :] = (d_resid[here, :] + back).astype(BF16)

    d_mem[...] = (
        base[...]
        + dot_nt(dsq[...], wsq[...])
        + dot_nt(jnp.concatenate([dsk_a[...], dsk_b[...]], 0), wk[...])
        + dot_nt(jnp.concatenate([dsv_a[...], dsv_b[...]], 0), wv[...])
    )
    micro, half, _ = mem_keep.shape
    slots = 2 * half
    rows = slots // 4
    for m in range(micro):
        for i in range(2):
            at = m * slots + 2 * i * rows
            mine = pl.ds(pl.multiple_of(at + me_ref[0] * rows, rows), rows)
            other = pl.ds(pl.multiple_of(at + (1 - me_ref[0]) * rows, rows), rows)
            mem_keep[m, i * rows : (i + 1) * rows, :] = d_mem[mine, :]
            mem_send[m, i * rows : (i + 1) * rows, :] = d_mem[other, :]


def split_kernel(bit, info, held, got, keep_out, send_out):
    half = keep_out.shape[1]
    mine = lax.rem(info[1] >> bit, 2)
    for m in range(held.shape[0]):
        own = pl.ds(pl.multiple_of(mine * half, half), half)
        other = pl.ds(pl.multiple_of((1 - mine) * half, half), half)
        keep_out[m] = held[m, own, :] + got[m, own, :]
        send_out[m] = held[m, other, :] + got[m, other, :]


def kernel_call(
    body, args, out_shape, mib, price, name, after=(), scalars=1, scratch_shapes=(), far=None
):
    count = len(args)

    def run(*refs):
        body(*refs[:count], *refs[count + len(after) :])

    in_specs = [SMEM] * scalars + [VMEM] * (count - scalars) + [ANY] * len(after)
    out_specs = [VMEM] * len(out_shape)
    args, out_shape = list(args), list(out_shape)
    if far is not None and far < count:
        in_specs[far] = ANY
        args[far] = pltpu.with_memory_space_constraint(args[far], pltpu.HBM)
    elif far is not None:
        out_specs[far - count] = ANY
        out_shape[far - count] = pltpu.HBM(
            out_shape[far - count].shape, out_shape[far - count].dtype
        )
    return pl.pallas_call(
        run,
        in_specs=in_specs,
        out_specs=out_specs,
        out_shape=out_shape,
        scratch_shapes=scratch_shapes,
        compiler_params=pltpu.CompilerParams(vmem_limit_bytes=int(mib * (1 << 20))),
        cost_estimate=price,
        name=name,
    )(*args, *after)


def like(shape, dtype):
    return jax.ShapeDtypeStruct(shape, dtype)


def cost(flops, nbytes, trans=0):
    return pl.CostEstimate(flops=flops, bytes_accessed=nbytes, transcendentals=trans)


def on_device(
    tokens,
    memory,
    doc_lengths,
    key_mask,
    w_query,
    w_key,
    w_value,
    w_out,
    w_up,
    w_down,
    w_slot_query,
    w_slot_out,
    w_forget,
    norm_gain,
    ffn_gain,
    memory_gain,
    out_grad,
    memory_grad,
):
    slot_count = lax.axis_size("slot")
    slot_index = lax.axis_index("slot")
    device_count = lax.axis_size("batch") * slot_count
    device = lax.axis_index("batch") * slot_count + slot_index
    micro, tok_dev, width = tokens.shape
    slot_rows = memory.shape[2]
    slots = slot_rows * slot_count
    group_tok = tok_dev * slot_count
    dev_start = slot_index * tok_dev
    rows = w_query.shape[0]
    ff = w_up.shape[1]
    pairs = width // 128
    total = micro * tok_dev
    mem_rows = micro * slots
    keys = tok_dev + slots
    down_rows = w_down.shape[0]
    part_rows = down_rows // 2
    cuts = ff // 2 // width
    extra = 16
    me = own_info()

    lane_at = jnp.arange(width, dtype=jnp.int32) // rows
    gain_rows = jnp.stack([norm_gain, ffn_gain, memory_gain])
    gain_rows = jnp.where(lane_at == device, jnp.tile(gain_rows, (1, device_count)), 0)
    gain_rows = jnp.pad(gain_rows.astype(BF16), ((0, extra - 3), (0, 0)))
    first = Gather(jnp.concatenate([w_query, w_key, w_value, gain_rows])[None], 0)
    up_parts = w_up.reshape(rows, device_count, 2, part_rows).transpose(2, 0, 1, 3)
    up_parts = up_parts.reshape(2, rows, cuts, width).transpose(0, 2, 1, 3)
    up_parts = up_parts.reshape(2, cuts * rows, width)
    rest = [w_slot_query, w_slot_out, w_forget, w_out]
    rest += [up_parts[0], w_down[:part_rows], up_parts[1], w_down[part_rows:]]
    rest = Gather(jnp.concatenate(rest)[None], 0)
    marks = [first.until(3)]
    rest.until(3)
    marks.append(first.until(2))
    first.launch()
    marks.append(first.finish())
    rest.launch(marks[1:2])
    first.launch()
    pair = tie(jnp.stack([memory[:, 0], memory_grad[:, 0]]), marks[:1])
    for axis, distance in axis_bits("slot")[::-1]:
        got = swap(pair, axis, distance)
        mine = own_bit(axis, distance)
        low, high = jnp.where(mine == 0, pair, got), jnp.where(mine == 0, got, pair)
        shape = pair.shape
        if distance == 1:
            cut = lambda m: m.reshape(shape[:2] + (-1, 1, slot_rows, width))
            pair = jnp.concatenate([cut(low), cut(high)], 3)
            pair = pair.reshape(shape[:2] + (-1, width))
        else:
            pair = jnp.concatenate([low, high], 2)
    mem_low = pair[0].reshape(mem_rows, width)
    mem_cot = pair[1].reshape(mem_rows, width)
    first.finish()
    first.launch()
    rest.finish([first.held])
    ends = [0, 4 * rows, 4 * rows + cuts * rows + part_rows, rest.held.shape[1]]
    second, third, fourth = [
        Gather(rest.held[:, a:b], 0, rest.left) for a, b in zip(ends, ends[1:])
    ]
    second.launch()

    one = [(i * rows, rows, 1) for i in range(4)]
    w_query, w_key, w_value, gain_sets = first.unpack(
        one[:3] + [(3 * rows, extra, 1)], me
    )
    gains = jnp.sum(gain_sets.reshape(device_count, extra, width).astype(F32), 0)
    w_query, w_key, w_value = w_query[0], w_key[0], w_value[0]

    keep = lax.dynamic_slice_in_dim(key_mask, dev_start, tok_dev, 1).astype(F32)
    keep = jnp.broadcast_to(keep[:, None, :], (micro, 8, tok_dev))
    segment = lax.axis_index("batch") * group_tok + dev_start
    positions = segment + jnp.arange(tok_dev, dtype=jnp.int32)
    doc_ends = jnp.cumsum(doc_lengths, axis=1, dtype=jnp.int32)
    passed = positions[None, None, :] >= doc_ends[:, :, None]
    starts = jnp.max(jnp.where(passed, doc_ends[:, :, None] - segment, 0), axis=1)
    starts = jnp.broadcast_to(starts[:, None, :], (micro, 8, tok_dev))

    tok_flat = tokens.reshape(total, width)
    cot_flat = out_grad.reshape(total, width)
    low = lambda n, w: like((n, w), BF16)

    wide = like((total, width), F32)
    slot_like = low(mem_rows, width)
    slot_wide = like((mem_rows, width), F32)
    normed, queries, tok_keys, tok_values, slot_keys, slot_values = kernel_call(
        project_kernel,
        [tok_flat, mem_low, gains, w_query, w_key, w_value],
        [low(total, width)] * 4 + [slot_like] * 2,
        3,
        cost(6 * total * width * width, 8 << 20),
        "project",
        scalars=0,
    )
    second.finish([normed])
    third.launch([second.held])
    second.launch([second.held])

    square = low(tok_dev, width)
    e_scratch = [pltpu.VMEM((2, 2, keys, tok_dev), BF16), pltpu.SemaphoreType.DMA((2,))]
    reads = []
    for m in range(micro):
        reads.append(
            kernel_call(
                functools.partial(read_kernel, m),
                [queries, tok_keys, tok_values, slot_keys, slot_values, starts, keep],
                [
                    square,
                    like((width, tok_dev), F32),
                    like((pairs, 8, tok_dev), F32),
                    like((pairs, 2, keys, tok_dev), BF16),
                ],
                6,
                cost(16 * total * width * keys // micro, 8 << 20, total * keys * HEADS // micro),
                "read",
                scalars=0,
                after=(second.held,) if m == 0 else (third.held,),
                scratch_shapes=[pltpu.VMEM((tok_dev, tok_dev), F32)] + e_scratch,
                far=10,
            )
        )
        if m == 0:
            third.finish([reads[0][0]])
            second.finish([reads[0][0]])
            third.launch([second.held, third.held])
            fourth.launch([second.held, third.held])
            second.launch([second.held, third.held])
    attended = [kept[0] for kept in reads]

    second_mats = second.unpack(one, me, [attended[1]])
    w_slot_query, w_slot_out, w_forget, w_out = (m[0] for m in second_mats)
    third.finish([attended[1]])
    fourth.finish([attended[1]])
    third.launch([w_slot_query, third.held, fourth.held])
    fourth.launch([w_slot_query, third.held, fourth.held])
    ffn_sections = [(0, rows, cuts), (cuts * rows, part_rows, 1)]
    up_first, down_first = third.unpack(ffn_sections, me)
    slot_queries, part = kernel_call(
        write_kernel,
        [mem_low, w_slot_query, tok_keys, tok_values, slot_keys, keep],
        [slot_like, like((micro, 72, slots * HEADS), F32)],
        3,
        cost(8 * total * width * slots, 5 << 20, total * slots * HEADS),
        "write",
        scalars=0,
        after=[third.held, fourth.held],
    )
    parts = [part]
    for axis, distance in axis_bits("slot"):
        other = swap(part, axis, distance)
        top_a, top_b = part[:, 64:65], other[:, 64:65]
        top = jnp.maximum(top_a, top_b)
        scale_a, scale_b = jnp.exp(top_a - top), jnp.exp(top_b - top)
        mix = part[:, :64] * scale_a + other[:, :64] * scale_b
        tot = part[:, 65:66] * scale_a + other[:, 65:66] * scale_b
        part = jnp.concatenate([mix, top, tot, part[:, 66:]], 1)
        parts.append(part)

    half_cost = cost(7 * total * width * ff, 14 << 20, total * ff // 2)
    tall = [pltpu.VMEM((total, ff // 2), BF16)] * 2 + [pltpu.VMEM((total, width), BF16)]
    sums_first = Shares(0, ffn_sections, me, width)
    resid, out_part, d_low, *outs = kernel_call(
        functools.partial(ffn_first_kernel, sums_first),
        [me, *attended, tok_flat, cot_flat, w_out, up_first, down_first[0], gains],
        [wide] * 3 + sums_first.shapes(),
        12,
        half_cost,
        "ffn_first",
        scratch_shapes=tall,
        after=parts[-2:-1],
    )
    part = tie(part, [resid])
    fourth.finish([resid])
    sums_first.begin(outs, [part, fourth.held])
    fourth.launch([part])

    new_memory, base, d_pre, written, d_upd, d_sq, own_sk, own_sv, w_dk, w_dv, g_mem = kernel_call(
        memory_kernel,
        [me, part, mem_low, mem_cot, slot_keys, slot_values, slot_queries]
        + [tok_keys, tok_values, keep, w_slot_out, w_forget, gains],
        [like((micro, slot_rows, width), BF16), slot_wide]
        + [slot_like] * 4
        + [slot_wide] * 2
        + [low(total, width)] * 2
        + [like((8, width), F32)],
        4,
        cost(12 * mem_rows * width * width + 12 * total * width * slots, 8 << 20),
        "memory",
        scratch_shapes=[pltpu.VMEM((mem_rows, width), F32)],
        after=[resid, fourth.held],
    )
    up_second, down_second = fourth.unpack(ffn_sections, me, [base])
    sums_first.finish([base])
    sums_first.launch([up_second])

    sections = [(0, rows, cuts), (cuts * rows, part_rows, 1)]
    sections += [(cuts * rows + part_rows + i * rows, rows, 1) for i in range(4)]
    sums_second = Shares(1, sections, me, width)
    turned = like((width, tok_dev), F32)
    layer_out, d_resid, da_a, da_b, g_ffn, *outs = kernel_call(
        functools.partial(ffn_second_kernel, sums_second),
        [me, *attended, resid, out_part, d_low, cot_flat, w_out, up_second, down_second[0], gains]
        + [mem_low, d_pre, written, d_upd, d_sq],
        [low(total, width), wide, turned, turned, like((8, width), F32)] + sums_second.shapes(),
        16,
        half_cost,
        "ffn_second",
        scratch_shapes=tall + [pltpu.VMEM((total, width), BF16)],
        after=[sums_first.send],
    )
    sums_first.finish([d_resid])
    sums_second.begin(outs, [sums_first.send])
    sums_first.launch()
    back = []
    for m, da_t in enumerate((da_a, da_b)):
        found = kernel_call(
            functools.partial(back_kernel, m),
            [queries, tok_keys, tok_values, slot_keys, slot_values]
            + [da_t, *reads[m][1:], w_dk, w_dv, own_sk, own_sv],
            [square] * 3 + [low(slots, width)] * 2,
            6,
            cost(24 * total * width * keys // micro, 10 << 20),
            "back",
            scalars=0,
            after=[sums_first.send] + ([sums_second.send] if m else []),
            scratch_shapes=e_scratch,
            far=8,
        )
        back += found
        sums_first.finish([found[0]])
        if m == 0:
            sums_second.finish([found[0]])
        sums_first.launch([sums_second.send])
        if m == 0:
            sums_second.launch([sums_first.send])

    sums_third = Shares(0, one[:3] + [(3 * rows, extra, 1)], me, width)
    tokens_grad, mem_keep, mem_send, *outs = kernel_call(
        functools.partial(last_kernel, sums_third),
        [me, normed, tok_flat, d_resid, *back, d_sq, base, mem_low]
        + [w_query, w_key, w_value, w_slot_query, gains, g_ffn, g_mem],
        [low(total, width)]
        + [like((micro, slots // 2, width), F32)] * 2
        + sums_third.shapes(),
        8,
        cost(12 * total * width * width, 16 << 20),
        "last",
        after=[sums_first.send],
        scratch_shapes=[pltpu.VMEM((mem_rows, width), F32)],
    )
    sums_second.finish([tokens_grad])
    sums_third.begin(outs, [sums_second.send])
    sums_second.launch()
    held, sent = mem_keep, mem_send
    bits = axis_bits("slot")
    for i, (axis, distance) in enumerate(bits):
        got = swap(sent, axis, distance)
        if i + 1 < len(bits):
            held, sent = kernel_call(
                functools.partial(split_kernel, i + 1),
                [me, held, got],
                [like((micro, held.shape[1] // 2, width), F32)] * 2,
                2,
                cost(held.size, 8 * held.size),
                "split",
            )
    moved = held + got
    sums_third.finish([sums_second.send])
    sums_third.launch()
    order = [sums_second, sums_third] * (sums_third.steps + 1)
    for sums in order:
        if sums.done < sums.steps:
            sums.finish()
            sums.launch()
    while sums_first.done < sums_first.steps:
        sums_first.finish()
        sums_first.launch()
    sums_first, sums_second, sums_third = sums_first.end(), sums_second.end(), sums_third.end()

    piece = lambda m, i: m[i * rows : (i + 1) * rows]

    def up_piece(m, at):
        return m[at : at + cuts * rows].reshape(cuts, rows, width).transpose(1, 0, 2).reshape(
            rows, device_count, 1, part_rows
        )

    up_share = jnp.concatenate([up_piece(sums_first, 0), up_piece(sums_second, 0)], 2)
    down_at = cuts * rows
    down_share = jnp.concatenate(
        [sums_first[down_at:], sums_second[down_at : down_at + part_rows]]
    )
    mixed = sums_second[down_at + part_rows :]
    gain_share = lax.dynamic_slice(sums_third, (3 * rows, device * rows), (3, rows))
    return (
        layer_out.reshape(micro, tok_dev, width),
        new_memory[:, None],
        tokens_grad.reshape(micro, tok_dev, width),
        moved.astype(BF16)[:, None],
        piece(sums_third, 0),
        piece(sums_third, 1),
        piece(sums_third, 2),
        piece(mixed, 0),
        up_share.reshape(rows, ff),
        down_share,
        piece(mixed, 1),
        piece(mixed, 2),
        piece(mixed, 3),
        gain_share[0],
        gain_share[1],
        gain_share[2],
    )


def solution(mesh):
    weight = P(("batch", "slot"), None)
    gain = P(("batch", "slot"))
    rows = P(None, ("batch", "slot"), None)
    slots = P(None, "batch", "slot", None)
    return jax.shard_map(
        on_device,
        mesh=mesh,
        in_specs=(rows, slots, P(), P(None, "batch")) + (weight,) * 9 + (gain,) * 3 + (rows, slots),
        out_specs=(rows, slots, rows, slots) + (weight,) * 9 + (gain,) * 3,
        check_vma=False,
    )
```

```python
import functools

import jax
import jax.numpy as jnp
from jax import lax
from jax.experimental import pallas as pl
from jax.experimental.pallas import tpu as pltpu
from jax.sharding import PartitionSpec as P

HEADS = 8
HEAD_DIM = 64
SEG = 512
EPSILON = 1e-05
MASKED = -1e30
BF16 = jnp.bfloat16
F32 = jnp.float32
SCALE = HEAD_DIM ** (-0.5)
SMEM = pl.BlockSpec(memory_space=pltpu.SMEM)
VMEM = pl.BlockSpec(memory_space=pltpu.VMEM)
ANY = pl.BlockSpec(memory_space=pl.ANY)


def swap(value, axis, distance):
    pairs = [(i, i ^ distance) for i in range(lax.axis_size(axis))]
    return lax.ppermute(value, axis, pairs)


def own_bit(axis, distance):
    return (lax.axis_index(axis) // distance) % 2


def axis_bits(axis):
    return [(axis, 1 << i) for i in range(lax.axis_size(axis).bit_length() - 1)]


def exchange_orders(turn):
    rest = axis_bits("slot")[1:] + axis_bits("batch")
    if turn:
        rest = rest[2:3] + rest[:2] + rest[3:]
    other = list(rest)
    for i in range(0, len(rest) - 1, 2):
        other[i], other[i + 1] = rest[i + 1], rest[i]
    return rest, other


def lane_swap(value, orders, step):
    slots = lax.axis_size("slot")
    pairs = []
    for batch in range(lax.axis_size("batch")):
        for slot in range(slots):
            axis, distance = orders[slot % 2][step]
            to_batch, to_slot = batch, slot
            if axis == "batch":
                to_batch = batch ^ distance
            else:
                to_slot = slot ^ distance
            pairs.append((batch * slots + slot, to_batch * slots + to_slot))
    return lax.ppermute(value, ("batch", "slot"), pairs)


def lane_bit(orders, step):
    lane = own_bit("slot", 1)
    return jnp.where(lane == 0, own_bit(*orders[0][step]), own_bit(*orders[1][step]))


def own_info():
    slot = lax.axis_index("slot")
    info = [own_bit("slot", 1), slot, lax.axis_index("batch") * lax.axis_size("slot") + slot]
    for turn in range(2):
        orders = exchange_orders(turn)
        info += [lane_bit(orders, step) for step in range(len(orders[0]))]
    return jnp.stack([jnp.asarray(entry, jnp.int32) for entry in info])


def info_at(turn, step):
    return 3 + turn * len(exchange_orders(0)[0]) + step


def chunk_places(order):
    natural = (axis_bits("slot")[1:] + axis_bits("batch"))
    count = len(order)
    places = []
    for pair in range(1 << count):
        place = 0
        for step, bit in enumerate(order):
            place |= ((pair >> natural.index(bit)) & 1) << (count - 1 - step)
        places.append(place)
    return places


def tie(value, after):
    return lax.optimization_barrier((value,) + tuple(after))[0] if after else value


class Gather:
    def __init__(self, held, turn, lows, left=None):
        self.turn, self.orders, self.lows = turn, exchange_orders(turn), lows
        self.left = len(self.orders[0]) if left is None else left
        self.held, self.got = held, None

    def launch(self, after=()):
        held = tie(self.held, after)
        if self.left == 0:
            self.got = swap(held, "slot", 1)
            return
        self.left -= 1
        self.got = lane_swap(held, self.orders, self.left)

    def finish(self, after=()):
        mine = self.lows[self.turn][self.left]
        got = tie(self.got, after)
        low = jnp.where(mine, self.held, got)
        high = jnp.where(mine, got, self.held)
        self.held = jnp.concatenate([low, high], 0)
        return self.held

    def until(self, left, after=()):
        while self.left > left:
            self.launch(after)
            self.finish()
        return self.held

    def unpack(self, sections, me, after=()):
        return unpack(self.held, self.got, self.turn, sections, me, after)


def place_kernel(places, sections, me_ref, held, got, *outs):
    for lane in range(2):

        @pl.when(me_ref[0] == lane)
        def _():
            sums = []
            for kind in range(2):
                source = held if kind == lane else got
                for pair, place in enumerate(places[kind]):
                    device = 2 * pair + kind
                    for (at, rows, lead), out in zip(sections, outs):
                        if lead == 0:
                            sums.append(source[place, at : at + rows, :].astype(F32))
                        for i in range(lead):
                            here = slice(device * rows, (device + 1) * rows)
                            out[i, here, :] = source[place, at + i * rows : at + (i + 1) * rows, :]
            if sums:
                outs[-1][...] = sum(sums[1:], sums[0])


def unpack(held, got, turn, sections, me, after):
    orders = exchange_orders(turn)
    places = [chunk_places(order) for order in orders]
    count, _, width = held.shape
    if all(rows % 16 == 0 for _, rows, lead in sections if lead):
        body = functools.partial(place_kernel, places, sections)
        outs = [
            like((lead, 2 * count * rows, width), BF16) if lead else like((rows, width), F32)
            for _, rows, lead in sections
        ]
        return kernel_call(
            body, [me, held, got], outs, 4, cost(0, 4 * held.size), "place", after
        )
    low = jnp.where(me[0] == 0, held, got)[jnp.array(places[0])]
    high = jnp.where(me[0] == 0, got, held)[jnp.array(places[1])]
    full = jnp.stack([low, high], 1).reshape(2 * count, -1, width)
    outs = []
    for at, rows, lead in sections:
        if lead == 0:
            outs.append(jnp.sum(full[:, at : at + rows].astype(F32), 0))
            continue
        part = full[:, at : at + rows * lead].reshape(2 * count, lead, rows, width)
        outs.append(part.transpose(1, 0, 2, 3).reshape(lead, -1, width))
    return outs


class Shares:
    def __init__(self, turn, sections, me, width):
        self.turn, self.sections, self.me, self.width = turn, sections, me, width
        self.rows = sum(rows * lead for _, rows, lead in sections)
        self.places = [chunk_places(order) for order in exchange_orders(turn)]
        self.count = len(self.places[0])
        self.direct = all(rows % 8 == 0 for _, rows, _ in sections)

    def shapes(self):
        if self.direct:
            return [like((self.count, self.rows, self.width), BF16)] * 2
        return [
            like((lead, 2 * self.count * rows, self.width), BF16)
            for _, rows, lead in self.sections
        ]

    def put(self, refs, me_ref, section, lead, first_row, value):
        at, rows, _ = self.sections[section]
        if not self.direct:
            refs[section][lead, first_row : first_row + value.shape[0], :] = value
            return
        keep, send = refs
        at = at + lead * rows
        for lane in range(2):

            @pl.when(me_ref[0] == lane)
            def _():
                for i in range(value.shape[0] // rows):
                    device = first_row // rows + i
                    target = keep if device % 2 == lane else send
                    place = self.places[device % 2][device // 2]
                    target[place, at : at + rows, :] = value[i * rows : (i + 1) * rows]

    def split(self, outs):
        if self.direct:
            return outs
        parts = []
        for (_, rows, lead), out in zip(self.sections, outs):
            part = out.reshape(lead, 2 * self.count, rows, self.width).transpose(1, 0, 2, 3)
            parts.append(part.reshape(2 * self.count, lead * rows, self.width))
        full = jnp.concatenate(parts, 1).reshape(self.count, 2, -1, self.width)
        back = []
        for kind in range(2):
            order = [0] * self.count
            for pair, place in enumerate(self.places[kind]):
                order[place] = pair
            back.append(full[:, kind][jnp.array(order)])
        lane = self.me[0]
        return [jnp.where(lane == 0, back[0], back[1]), jnp.where(lane == 0, back[1], back[0])]

    def begin(self, outs, after=()):
        self.orders = exchange_orders(self.turn)
        self.steps = len(self.orders[0])
        self.done, self.extra = 0, []
        self.keep, self.send = self.split(outs)
        self.got = swap(tie(self.send, after), "slot", 1)

    def join(self, outs, after=()):
        keep, send = outs
        got = swap(tie(send, after), "slot", 1)
        self.extra.append((keep, got))

    def finish(self, after=()):
        at = info_at(self.turn, self.done)
        if self.extra:
            keep, got = self.extra.pop()
            self.keep, self.send = halve_two(
                self.keep, self.got, keep, got, self.me, at, self.direct, after
            )
            return self.send
        self.keep, self.send = halve(self.keep, self.got, self.me, at, self.direct, after)
        return self.send

    def launch(self, after=()):
        self.got = lane_swap(tie(self.send, after), self.orders, self.done)
        self.done += 1

    def end(self, after=()):
        return self.keep[0].astype(F32) + tie(self.got, after)[0].astype(F32)


def halve_two_kernel(at, info, keep_a, got_a, keep_b, got_b, keep_out, send_out):
    rows = keep_a.shape[1]
    halve_kernel(at, info, keep_a, got_a, keep_out.at[:, :rows], send_out.at[:, :rows])
    halve_kernel(at, info, keep_b, got_b, keep_out.at[:, rows:], send_out.at[:, rows:])


def halve_two(keep_a, got_a, keep_b, got_b, info, at, direct, after):
    if not direct:
        keep = jnp.concatenate([keep_a, keep_b], 1)
        return halve(keep, jnp.concatenate([got_a, got_b], 1), info, at, direct, after)
    count, rows, width = keep_a.shape
    shape = (count // 2, rows + keep_b.shape[1], width)
    return kernel_call(
        functools.partial(halve_two_kernel, at),
        [info, keep_a, got_a, keep_b, got_b],
        [like(shape, BF16)] * 2,
        4,
        cost(2 * keep_a.size, 12 * keep_a.size),
        "halve",
        after,
    )


def halve_kernel(at, info, keep, got, keep_out, send_out):
    half = keep_out.shape[0]
    mine = pl.ds(info[at] * half, half)
    other = pl.ds((1 - info[at]) * half, half)
    send_out[...] = keep[other] + got[other]
    keep_out[...] = keep[mine] + got[mine]


def halve(keep, got, info, at, direct, after):
    count, rows, width = keep.shape
    half = count // 2
    if direct:
        return kernel_call(
            functools.partial(halve_kernel, at),
            [info, keep, got],
            [like((half, rows, width), BF16)] * 2,
            4,
            cost(keep.size, 6 * keep.size),
            "halve",
            after,
        )
    bit = info[at]
    total = tie(keep, after) + got
    take = lambda b: lax.dynamic_slice_in_dim(total, b * half, half, 0)
    return take(bit), take(1 - bit)


def dot(a, b):
    return jnp.dot(a, b, preferred_element_type=F32)


def dot_nt(a, b):
    return lax.dot_general(a, b, (((1,), (1,)), ((), ())), preferred_element_type=F32)


def dot_tn(a, b):
    return lax.dot_general(a, b, (((0,), (0,)), ((), ())), preferred_element_type=F32)


def norm_parts(rows):
    centre = jnp.mean(rows, axis=-1, keepdims=True)
    centred = rows - centre
    spread = jnp.mean(centred * centred, axis=-1, keepdims=True)
    inverse = lax.rsqrt(spread + EPSILON)
    return centred * inverse, inverse


def norm_back(cot, hat, inverse, gain):
    d_hat = cot * gain
    first = jnp.mean(d_hat, axis=-1, keepdims=True)
    second = jnp.mean(d_hat * hat, axis=-1, keepdims=True)
    return inverse * (d_hat - first - hat * second)


def head_lanes(value, head):
    lane = lax.broadcasted_iota(jnp.int32, value.shape, 1)
    return jnp.where(lane // HEAD_DIM == head, value, jnp.zeros_like(value))


def head_rows(value, head):
    row = lax.broadcasted_iota(jnp.int32, value.shape, 0)
    return jnp.where(row // HEAD_DIM == head, value, jnp.zeros_like(value))


def both_heads(value):
    return jnp.concatenate([head_lanes(value, 0), head_lanes(value, 1)], 0)


def to_slot_lanes(value):
    turned = value.T
    return jnp.concatenate([turned[:HEAD_DIM], turned[HEAD_DIM:]], 1)


def to_slot_rows(value):
    turned = value.T
    half = turned.shape[0] // 2
    return jnp.concatenate([turned[:half], turned[half:]], 1)


def diagonal(value):
    lane = lax.broadcasted_iota(jnp.int32, (HEAD_DIM, value.shape[1]), 1)
    return jnp.where(lane < value.shape[1] // 2, value[:HEAD_DIM], value[HEAD_DIM:])


ROWS = 512


def row_loop(total):
    return lambda body: pl.loop(0, total // ROWS)(
        lambda i: body(pl.ds(pl.multiple_of(i * ROWS, ROWS), ROWS))
    )


def pair_loop(width):
    return lambda body: pl.loop(0, width // 128, unroll=2)(
        lambda p: body(p, pl.ds(pl.multiple_of(p * 128, 128), 128))
    )


def project_kernel(
    me_ref, tok, pair, other, gain, wq, wk, wv, normed, q, k, v, sk, sv, mem, mem_cot
):
    half = pair.shape[2]
    rows = half // 2
    for lane in range(2):

        @pl.when(me_ref[0] == lane)
        def _():
            for kind, out in enumerate((mem, mem_cot)):
                for m in range(pair.shape[1]):
                    for i in range(2):
                        for core in range(2):
                            source = pair if core == lane else other
                            at = 2 * (m * half + i * rows) + core * rows
                            block = source[kind, m, i * rows : (i + 1) * rows, :]
                            out[at : at + rows, :] = block

    @row_loop(tok.shape[0])
    def _(here):
        hat, _ = norm_parts(tok[here, :].astype(F32))
        low = (hat * gain[0:1, :]).astype(BF16)
        normed[here, :] = low
        q[here, :] = dot(low, wq[...]).astype(BF16)
        k[here, :] = dot(low, wk[...]).astype(BF16)
        v[here, :] = dot(low, wv[...]).astype(BF16)

    sk[...] = dot(mem[...], wk[...]).astype(BF16)
    sv[...] = dot(mem[...], wv[...]).astype(BF16)


def read_kernel(m, q, k, v, sk, sv, starts, keep, attended, out_t, inv, e_ref, bias):
    tok = attended.shape[0]
    slots = sk.shape[0] // keep.shape[0]
    key_at = lax.broadcasted_iota(jnp.int32, (tok, tok), 0)
    query_at = lax.broadcasted_iota(jnp.int32, (tok, tok), 1)
    start = starts[m, 0:1, :]
    kept = jnp.broadcast_to(keep[m, 0:1, :], (128, tok)).T
    kept = jnp.concatenate([kept] * (tok // 128), 1)
    good = (key_at >= start) & (key_at <= query_at) & (kept > 0)
    bias[...] = jnp.where(good, 0.0, MASKED)
    here, slot_here = pl.ds(m * tok, tok), pl.ds(m * slots, slots)

    @pair_loop(q.shape[1])
    def _(p, lanes):
        read_pair(
            q[here, lanes], k[here, lanes], v[here, lanes], sk[slot_here, lanes],
            sv[slot_here, lanes], bias, attended.at[:, lanes],
            out_t.at[pl.ds(pl.multiple_of(p * 128, 128), 128), :], inv.at[p], e_ref.at[p],
        )


def read_pair(q, keys, values, slot_keys, slot_values, bias, attended, out_t, inv, e_ref):
    tok = q.shape[0]
    half = tok // 2
    slots = slot_keys.shape[0]
    scaled = q * jnp.asarray(SCALE, BF16)
    values_t = values.T
    slot_values_t = slot_values.T
    outs, inverses = [], []
    for head in range(2):
        qm = head_lanes(scaled, head)
        rows = slice(head * HEAD_DIM, (head + 1) * HEAD_DIM)
        s_mem = dot_nt(slot_keys, qm)
        s_a = dot_nt(keys[:half], qm) + bias[:half, :]
        s_b = dot_nt(keys[half:], qm[half:]) + bias[half:, half:]
        top = jnp.maximum(jnp.max(s_mem, 0, keepdims=True), jnp.max(s_a, 0, keepdims=True))
        top_b = jnp.maximum(top[:, half:], jnp.max(s_b, 0, keepdims=True))
        top = jnp.concatenate([top[:, :half], top_b], 1)
        e_mem = jnp.exp(s_mem - top)
        e_a = jnp.exp(s_a - top)
        e_b = jnp.exp(s_b - top_b)
        total = jnp.sum(e_mem, 0, keepdims=True) + jnp.sum(e_a, 0, keepdims=True)
        total_b = total[:, half:] + jnp.sum(e_b, 0, keepdims=True)
        total = jnp.concatenate([total[:, :half], total_b], 1)
        e_mem, e_a, e_b = e_mem.astype(BF16), e_a.astype(BF16), e_b.astype(BF16)
        e_ref[head, :slots, :] = e_mem
        e_ref[head, slots : slots + half, :] = e_a
        e_ref[head, slots + half :, half:] = e_b
        e_ref[head, slots + half :, :half] = jnp.zeros((half, half), BF16)
        mix = dot(slot_values_t[rows], e_mem) + dot(values_t[rows, :half], e_a)
        mix_b = mix[:, half:] + dot(values_t[rows, half:], e_b)
        mix = jnp.concatenate([mix[:, :half], mix_b], 1)
        inverse = 1.0 / total
        outs.append(mix * inverse)
        inverses.append(inverse)
    out = jnp.concatenate(outs, 0)
    out_t[...] = out
    inv[...] = jnp.concatenate(inverses + [jnp.zeros((6, tok), F32)], 0)
    attended[...] = out.T.astype(BF16)


def write_kernel(mem, wsq, k, v, sk, keep, sq_ref, part):
    micro = keep.shape[0]
    tok = k.shape[0] // micro
    slots = mem.shape[0] // micro
    pairs = k.shape[1] // 128
    sq = dot(mem[...], wsq[...]).astype(BF16)
    sq_ref[...] = sq
    for m in range(micro):
        kept = jnp.broadcast_to(keep[m, 0:1, :], (128, tok)).T
        bias = jnp.where(kept > 0, 0.0, MASKED)
        for p in range(pairs):
            lanes = slice(p * 128, p * 128 + 128)
            mine = sq[m * slots : (m + 1) * slots, lanes]
            own = to_slot_lanes(
                mine.astype(F32) * sk[m * slots : (m + 1) * slots, lanes].astype(F32)
            )
            own = jnp.sum(own, 0, keepdims=True) * SCALE
            scores = dot_nt(k[m * tok : (m + 1) * tok, lanes], both_heads(mine)) * SCALE + bias
            top = jnp.maximum(jnp.max(scores, 0, keepdims=True), own)
            e = jnp.exp(scores - top)
            total = jnp.sum(e, 0, keepdims=True)
            mix = diagonal(dot_tn(v[m * tok : (m + 1) * tok, lanes], e.astype(BF16)))
            part[m, :HEAD_DIM, lanes] = mix
            part[m, HEAD_DIM:, lanes] = jnp.concatenate(
                [top, total, own, jnp.zeros((5, 128), F32)], 0
            )


def gelu_pair(hidden):
    root = 0.7978845608028654
    square = hidden * hidden
    bent = jnp.tanh(hidden * (root + (root * 0.044715) * square))
    half = 0.5 + 0.5 * bent
    slope = half + (0.5 * hidden) * (1.0 - bent * bent) * (root + (3.0 * root * 0.044715) * square)
    return (hidden * half).astype(BF16), slope


def ffn_cuts(low, cot_low, up, down, here, act_all, dh_all):
    width = low.shape[1]
    out = d_low = 0.0
    for cut in range(up.shape[0]):
        cols = slice(cut * width, (cut + 1) * width)
        act, slope = gelu_pair(dot(low, up[cut]))
        d_hidden = (dot_nt(cot_low, down[cols, :]) * slope).astype(BF16)
        act_all[here, cols] = act
        dh_all[here, cols] = d_hidden
        out = out + dot(act, down[cols, :])
        d_low = d_low + dot_nt(d_hidden, up[cut])
    return out, d_low


def ffn_grads(shares, refs, me_ref, base, low_all, cot_all, act_all, dh_all, cuts):
    width = low_all.shape[1]
    low_t = low_all[...].T
    for cut in range(cuts):
        cols = slice(cut * width, (cut + 1) * width)
        shares.put(refs, me_ref, base, cut, 0, dot(low_t, dh_all[:, cols]).astype(BF16))
        grad = dot_tn(act_all[:, cols], cot_all[...]).astype(BF16)
        shares.put(refs, me_ref, base + 1, 0, cut * width, grad)


def ffn_first_kernel(
    shares, me_ref, att_a, att_b, tok, cot, wout, up, down, gain,
    resid_ref, out_ref, d_low_ref, *rest
):
    refs, (act_all, dh_all, low_all) = rest[:-3], rest[-3:]
    count = att_a.shape[0]
    for m, att in enumerate((att_a, att_b)):

        @row_loop(count)
        def _(there):
            here = pl.ds(there.start + m * count, ROWS)
            resid = tok[here, :].astype(F32) + dot(att[there, :], wout[...])
            hat, _ = norm_parts(resid)
            low = (hat * gain[1:2, :]).astype(BF16)
            low_all[here, :] = low
            out, d_low = ffn_cuts(low, cot[here, :], up, down, here, act_all, dh_all)
            resid_ref[here, :] = resid
            out_ref[here, :] = resid + out
            d_low_ref[here, :] = d_low

    ffn_grads(shares, refs, me_ref, 0, low_all, cot, act_all, dh_all, up.shape[0])


def ffn_second_kernel(
    shares, me_ref, att_a, att_b, resid, part, d_part, cot, wout, up, down, gain,
    layer_out, d_resid_ref, da_a, da_b, g_gain, *rest
):
    refs, (act_all, dh_all, low_all, dattn_all) = rest[:-4], rest[-4:]
    count = att_a.shape[0]
    gain_row = gain[1:2, :]
    g_gain[...] = jnp.zeros_like(g_gain)
    for m, da_t in enumerate((da_a, da_b)):

        @row_loop(count)
        def _(there):
            here = pl.ds(there.start + m * count, ROWS)
            hat, inverse = norm_parts(resid[here, :])
            low = (hat * gain_row).astype(BF16)
            low_all[here, :] = low
            cot_low = cot[here, :]
            out, d_low = ffn_cuts(low, cot_low, up, down, here, act_all, dh_all)
            layer_out[here, :] = (part[here, :] + out).astype(BF16)
            d_low = d_part[here, :] + d_low
            d_resid = cot_low.astype(F32) + norm_back(d_low, hat, inverse, gain_row)
            d_resid_ref[here, :] = d_resid
            d_attn = d_resid.astype(BF16)
            dattn_all[here, :] = d_attn
            da_t[:, there] = dot_nt(wout[...], d_attn)
            g_gain[0:1, :] += jnp.sum(d_low * hat, 0, keepdims=True)

    ffn_grads(shares, refs, me_ref, 0, low_all, cot, act_all, dh_all, up.shape[0])
    grad = dot_tn(att_a[...], dattn_all[:count, :]) + dot_tn(att_b[...], dattn_all[count:, :])
    shares.put(refs, me_ref, 2, 0, 0, grad.astype(BF16))


def memory_kernel(
    shares, slot_ref, part, mem, cot, sk, sv, sq, k, v, keep, wso, wfg, gain,
    new_ref, base, dsq_ref, osk, osv, wdk, wdv, g_gain, *rest
):
    refs, held = rest[:-1], rest[-1]
    micro = part.shape[0]
    slots = mem.shape[0] // micro
    own_rows = new_ref.shape[1]
    pairs = mem.shape[1] // 128
    row_at = lax.broadcasted_iota(jnp.int32, (mem.shape[0], 1), 0)
    mine = ((row_at % slots) // own_rows == slot_ref[1]).astype(F32)
    probs, tots, lses = [], [], []
    lines = []
    for m in range(micro):
        here = slice(m * slots, (m + 1) * slots)
        line, prob_line = [], []
        for p in range(pairs):
            lanes = slice(p * 128, p * 128 + 128)
            top0 = part[m, HEAD_DIM : HEAD_DIM + 1, lanes]
            total0 = part[m, HEAD_DIM + 1 : HEAD_DIM + 2, lanes]
            own = part[m, HEAD_DIM + 2 : HEAD_DIM + 3, lanes]
            top = jnp.maximum(top0, own)
            own_e = jnp.exp(own - top)
            shift = jnp.exp(top0 - top)
            total = total0 * shift + own_e
            inverse = 1.0 / total
            prob = own_e * inverse
            values = to_slot_lanes(sv[here, lanes].astype(F32))
            mixed = part[m, :HEAD_DIM, lanes] * (shift * inverse) + prob * values
            line.append(to_slot_rows(mixed))
            prob_line.append((prob, top + jnp.log(total)))
        lines.append(jnp.concatenate(line, 1))
        probs.append(prob_line)
    written = jnp.concatenate(lines, 0)
    written_low = written.astype(BF16)
    mem_low = mem[...]
    mem_f32 = mem_low.astype(F32)
    update = dot(written_low, wso[...])
    gate = 1.0 / (1.0 + jnp.exp(-dot(mem_low, wfg[...])))
    gain_row = gain[2:3, :]
    hat, inverse = norm_parts(gate * mem_f32 + (1.0 - gate) * update)
    held[...] = hat * gain_row
    cot_f32 = cot[...].astype(F32)
    for m in range(micro):
        at = pl.multiple_of(m * slots + slot_ref[1] * own_rows, own_rows)
        new_ref[m] = held[pl.ds(at, own_rows), :].astype(BF16)
    g_gain[...] = jnp.broadcast_to(jnp.sum(cot_f32 * hat * mine, 0, keepdims=True), g_gain.shape)
    d_blend = norm_back(cot_f32, hat, inverse, gain_row)
    d_pre = (d_blend * (mem_f32 - update) * gate * (1.0 - gate) * mine).astype(BF16)
    d_update = (d_blend * (1.0 - gate)).astype(BF16)
    mem_t = mem_low.T
    d_upd = (d_update.astype(F32) * mine).astype(BF16)
    shares.put(refs, slot_ref, 1, 0, 0, dot_tn(written_low, d_upd).astype(BF16))
    shares.put(refs, slot_ref, 2, 0, 0, dot(mem_t, d_pre).astype(BF16))
    base[...] = d_blend * gate * mine + dot_nt(d_pre, wfg[...])
    d_written = dot_nt(d_update, wso[...]).astype(BF16)
    dw_f32 = d_written.astype(F32)
    product = dw_f32 * written
    tok = k.shape[0] // micro
    for m in range(micro):
        here = slice(m * slots, (m + 1) * slots)
        there = slice(m * tok, (m + 1) * tok)
        kept = jnp.broadcast_to(keep[m, 0:1, :], (128, tok)).T
        bias = jnp.where(kept > 0, 0.0, MASKED)
        for p in range(pairs):
            lanes = slice(p * 128, p * 128 + 128)
            prob, lse = probs[m][p]
            values_f32 = sv[here, lanes].astype(F32)
            delta = jnp.sum(to_slot_lanes(product[here, lanes]), 0, keepdims=True)
            own_dp = jnp.sum(to_slot_lanes(dw_f32[here, lanes] * values_f32), 0, keepdims=True)
            own_ds = prob * (own_dp - delta)
            wide = lambda r: to_slot_rows(jnp.broadcast_to(r, (HEAD_DIM, 2 * slots)))
            own_ds = wide(own_ds) * mine[here] * SCALE
            own_p = wide(prob) * mine[here]
            sq_low = sq[here, lanes]
            sq_both = both_heads(sq_low * jnp.asarray(SCALE, BF16))
            dw_low = d_written[here, lanes]
            dw_both = both_heads(dw_low)
            keys, values = k[there, lanes], v[there, lanes]
            prob = jnp.exp(dot_nt(keys, sq_both) + bias - lse)
            d_score = (prob * (dot_nt(values, dw_both) - delta)).astype(BF16)
            wdk[there, lanes] = dot(d_score, sq_both).astype(BF16)
            wdv[there, lanes] = dot(prob.astype(BF16), dw_both).astype(BF16)
            d_read = to_slot_rows(diagonal(dot_tn(keys, d_score)))
            slot_keys = sk[here, lanes].astype(F32)
            dsq_ref[here, lanes] = (d_read * SCALE + own_ds * slot_keys).astype(BF16)
            osk[here, lanes] = own_ds * sq_low.astype(F32)
            osv[here, lanes] = own_p * dw_low.astype(F32)
    shares.put(refs, slot_ref, 0, 0, 0, dot(mem_t, dsq_ref[...]).astype(BF16))


def back_kernel(
    m, q, k, v, sk, sv, da_t, out_t, inv, e_ref, wdk, wdv, osk, osv, dq, dk, dv, dsk, dsv
):
    tok, slots = dq.shape[0], dsk.shape[0]
    here, slot_here = pl.ds(m * tok, tok), pl.ds(m * slots, slots)

    @pair_loop(q.shape[1])
    def _(p, lanes):
        turned = pl.ds(pl.multiple_of(p * 128, 128), 128)
        back_pair(
            q[here, lanes], k[here, lanes], v[here, lanes], sk[slot_here, lanes],
            sv[slot_here, lanes], da_t.at[turned, :], out_t.at[turned, :], inv.at[p],
            e_ref.at[p], wdk.at[here, lanes], wdv.at[here, lanes], osk.at[slot_here, lanes],
            osv.at[slot_here, lanes], dq.at[:, lanes], dk.at[:, lanes], dv.at[:, lanes],
            dsk.at[:, lanes], dsv.at[:, lanes],
        )


def back_pair(
    q, keys, values, slot_keys, slot_values, da_t, out_t, inv, e_ref, wdk, wdv, osk, osv,
    dq, dk, dv, dsk, dsv,
):
    tok = q.shape[0]
    half = tok // 2
    slots = slot_keys.shape[0]
    scaled = q * jnp.asarray(SCALE, BF16)
    keys_t = keys.T
    slot_keys_t = slot_keys.T
    norm = jnp.concatenate(
        [jnp.broadcast_to(inv[i : i + 1, :], (HEAD_DIM, tok)) for i in range(2)], 0
    )
    da = (da_t[...] * norm).astype(BF16)
    product = da.astype(F32) * out_t[...]
    da_rows = da.T
    dq_parts = []
    dk_a = dk_b = dv_a = dv_b = dk_m = dv_m = 0.0
    for head in range(2):
        rows = slice(head * HEAD_DIM, (head + 1) * HEAD_DIM)
        qm = head_lanes(scaled, head)
        dam_t = head_rows(da, head)
        dam = head_lanes(da_rows, head)
        delta = jnp.sum(product[rows], 0, keepdims=True)
        e_mem = e_ref[head, :slots, :]
        e_a = e_ref[head, slots : slots + half, :]
        e_b = e_ref[head, slots + half :, half:]
        ds_mem = (e_mem.astype(F32) * (dot(slot_values, dam_t) - delta)).astype(BF16)
        ds_a = (e_a.astype(F32) * (dot(values[:half], dam_t) - delta)).astype(BF16)
        ds_b = (
            e_b.astype(F32) * (dot(values[half:], dam_t[:, half:]) - delta[:, half:])
        ).astype(BF16)
        part = dot(slot_keys_t[rows], ds_mem) + dot(keys_t[rows, :half], ds_a)
        part_b = part[:, half:] + dot(keys_t[rows, half:], ds_b)
        dq_parts.append(jnp.concatenate([part[:, :half], part_b], 1))
        dk_a = dk_a + dot(ds_a, qm)
        dk_b = dk_b + dot(ds_b, qm[half:])
        dk_m = dk_m + dot(ds_mem, qm)
        dv_a = dv_a + dot(e_a, dam)
        dv_b = dv_b + dot(e_b, dam[half:])
        dv_m = dv_m + dot(e_mem, dam)
    dq[...] = (jnp.concatenate(dq_parts, 0) * SCALE).T.astype(BF16)

    dk[:half, :] = (dk_a + wdk[:half, :].astype(F32)).astype(BF16)
    dk[half:, :] = (dk_b + wdk[half:, :].astype(F32)).astype(BF16)
    dv[:half, :] = (dv_a + wdv[:half, :].astype(F32)).astype(BF16)
    dv[half:, :] = (dv_b + wdv[half:, :].astype(F32)).astype(BF16)
    dsk[...] = (dk_m + osk[...]).astype(BF16)
    dsv[...] = (dv_m + osv[...]).astype(BF16)


def grads_kernel(
    shares, me_ref, normed, dq_a, dk_a, dv_a, dsk_a, dsv_a, dq_b, dk_b, dv_b, dsk_b, dsv_b,
    mem, wq, wk, wv, gain, g_ffn, g_mem, *refs
):
    count = dq_a.shape[0]
    slots = dsk_a.shape[0]
    rows_t = normed[...].T
    mem_t = mem[...].T
    weighted = 0.0
    sets = (
        (dq_a, dq_b, wq, None, None),
        (dk_a, dk_b, wk, dsk_a, dsk_b),
        (dv_a, dv_b, wv, dsv_a, dsv_b),
    )
    for i, (cot_a, cot_b, weight, slot_a, slot_b) in enumerate(sets):
        grad = dot(rows_t[:, :count], cot_a[...]) + dot(rows_t[:, count:], cot_b[...])
        weighted = weighted + grad * weight[...].astype(F32)
        if slot_a is not None:
            slot_cot = jnp.concatenate([slot_a[...], slot_b[...]], 0)
            grad = grad + dot(mem_t, slot_cot)
        shares.put(refs, me_ref, i, 0, 0, grad.astype(BF16))
    folded = weighted[:, :128]
    for i in range(1, weighted.shape[1] // 128):
        folded = folded + weighted[:, i * 128 : (i + 1) * 128]
    line = jnp.sum(folded.T, 0, keepdims=True) / gain[0:1, :]
    lines = [line, g_ffn[0:1, :], g_mem[0:1, :]]
    extra = shares.sections[3][1]
    lines = jnp.concatenate(lines + [jnp.zeros((extra - 3, line.shape[1]), F32)], 0)
    lines = lines.astype(BF16)
    for device in range(2 * shares.count):
        shares.put(refs, me_ref, 3, 0, device * extra, lines)


def input_kernel(
    me_ref, tok, d_resid,
    dq_a, dk_a, dv_a, dsk_a, dsv_a, dq_b, dk_b, dv_b, dsk_b, dsv_b, dsq, base,
    wq, wk, wv, wsq, gain, tok_grad, mem_keep, mem_send, d_mem
):
    count = dq_a.shape[0]
    for m, (dq, dk, dv) in enumerate(((dq_a, dk_a, dv_a), (dq_b, dk_b, dv_b))):

        @row_loop(count)
        def _(there):
            here = pl.ds(there.start + m * count, ROWS)
            hat, inverse = norm_parts(tok[here, :].astype(F32))
            d_normed = dot_nt(dq[there, :], wq[...]) + dot_nt(dk[there, :], wk[...])
            d_normed = d_normed + dot_nt(dv[there, :], wv[...])
            back = norm_back(d_normed, hat, inverse, gain[0:1, :])
            tok_grad[here, :] = (d_resid[here, :] + back).astype(BF16)

    d_mem[...] = (
        base[...]
        + dot_nt(dsq[...], wsq[...])
        + dot_nt(jnp.concatenate([dsk_a[...], dsk_b[...]], 0), wk[...])
        + dot_nt(jnp.concatenate([dsv_a[...], dsv_b[...]], 0), wv[...])
    )
    micro, half, _ = mem_keep.shape
    slots = 2 * half
    rows = slots // 4
    for m in range(micro):
        for i in range(2):
            at = m * slots + 2 * i * rows
            mine = pl.ds(pl.multiple_of(at + me_ref[0] * rows, rows), rows)
            other = pl.ds(pl.multiple_of(at + (1 - me_ref[0]) * rows, rows), rows)
            mem_keep[m, i * rows : (i + 1) * rows, :] = d_mem[mine, :]
            mem_send[m, i * rows : (i + 1) * rows, :] = d_mem[other, :]


def split_kernel(bit, info, held, got, keep_out, send_out):
    half = keep_out.shape[1]
    mine = lax.rem(info[1] >> bit, 2)
    for m in range(held.shape[0]):
        own = pl.ds(pl.multiple_of(mine * half, half), half)
        other = pl.ds(pl.multiple_of((1 - mine) * half, half), half)
        keep_out[m] = held[m, own, :] + got[m, own, :]
        send_out[m] = held[m, other, :] + got[m, other, :]


def kernel_call(
    body, args, out_shape, mib, price, name, after=(), scalars=1, scratch_shapes=(), far=None
):
    count = len(args)

    def run(*refs):
        body(*refs[:count], *refs[count + len(after) :])

    in_specs = [SMEM] * scalars + [VMEM] * (count - scalars) + [ANY] * len(after)
    out_specs = [VMEM] * len(out_shape)
    args, out_shape = list(args), list(out_shape)
    if far is not None and far < count:
        in_specs[far] = ANY
        args[far] = pltpu.with_memory_space_constraint(args[far], pltpu.HBM)
    elif far is not None:
        out_specs[far - count] = ANY
        out_shape[far - count] = pltpu.HBM(
            out_shape[far - count].shape, out_shape[far - count].dtype
        )
    return pl.pallas_call(
        run,
        in_specs=in_specs,
        out_specs=out_specs,
        out_shape=out_shape,
        scratch_shapes=scratch_shapes,
        compiler_params=pltpu.CompilerParams(vmem_limit_bytes=int(mib * (1 << 20))),
        cost_estimate=price,
        name=name,
    )(*args, *after)


def like(shape, dtype):
    return jax.ShapeDtypeStruct(shape, dtype)


def cost(flops, nbytes, trans=0):
    return pl.CostEstimate(flops=flops, bytes_accessed=nbytes, transcendentals=trans)


def on_device(
    tokens,
    memory,
    doc_lengths,
    key_mask,
    w_query,
    w_key,
    w_value,
    w_out,
    w_up,
    w_down,
    w_slot_query,
    w_slot_out,
    w_forget,
    norm_gain,
    ffn_gain,
    memory_gain,
    out_grad,
    memory_grad,
):
    slot_count = lax.axis_size("slot")
    slot_index = lax.axis_index("slot")
    device_count = lax.axis_size("batch") * slot_count
    device = lax.axis_index("batch") * slot_count + slot_index
    micro, tok_dev, width = tokens.shape
    slot_rows = memory.shape[2]
    slots = slot_rows * slot_count
    group_tok = tok_dev * slot_count
    dev_start = slot_index * tok_dev
    rows = w_query.shape[0]
    ff = w_up.shape[1]
    pairs = width // 128
    total = micro * tok_dev
    mem_rows = micro * slots
    keys = tok_dev + slots
    down_rows = w_down.shape[0]
    part_rows = down_rows // 2
    cuts = ff // 2 // width
    extra = 8
    me = own_info()
    lane_at = jnp.arange(width, dtype=jnp.int32) // rows
    pick = jnp.arange(width)[:, None] == device * rows + jnp.arange(rows)[None, :]
    pick = pick.astype(F32)
    keep = lax.dynamic_slice_in_dim(key_mask, dev_start, tok_dev, 1).astype(F32)
    keep = jnp.broadcast_to(keep[:, None, :], (micro, 8, tok_dev))
    segment = lax.axis_index("batch") * group_tok + dev_start
    positions = segment + jnp.arange(tok_dev, dtype=jnp.int32)
    doc_ends = jnp.cumsum(doc_lengths, axis=1, dtype=jnp.int32)
    passed = positions[None, None, :] >= doc_ends[:, :, None]
    starts = jnp.max(jnp.where(passed, doc_ends[:, :, None] - segment, 0), axis=1)
    starts = jnp.broadcast_to(starts[:, None, :], (micro, 8, tok_dev))
    lows = []
    for turn in range(2):
        orders = exchange_orders(turn)
        lows += [lane_bit(orders, step) == 0 for step in range(len(orders[0]))]
    half = len(lows) // 2
    small = lax.optimization_barrier(
        (me, keep, starts, pick, own_bit("slot", 2) == 0) + tuple(lows)
    )
    me, keep, starts, pick, slot_low = small[:5]
    lows = (small[5 : 5 + half], small[5 + half :])
    gain_rows = jnp.stack([norm_gain, ffn_gain, memory_gain])
    gain_rows = jnp.where(lane_at == device, jnp.tile(gain_rows, (1, device_count)), 0)
    gain_rows = jnp.pad(gain_rows.astype(BF16), ((0, extra - 3), (0, 0)))
    first = Gather(jnp.concatenate([w_query, w_key, w_value, gain_rows])[None], 0, lows)
    marks = [first.until(3)]
    raw = [w_slot_query, w_slot_out, w_forget, w_out, w_up, w_down]
    raw = lax.optimization_barrier(tuple(raw) + (marks[0],))
    w_up, w_down = raw[4], raw[5]
    up_parts = w_up.reshape(rows, device_count, 2, part_rows).transpose(2, 0, 1, 3)
    up_parts = up_parts.reshape(2, rows, cuts, width).transpose(0, 2, 1, 3)
    up_parts = up_parts.reshape(2, cuts * rows, width)
    rest = list(raw[:4])
    rest += [up_parts[0], w_down[:part_rows]]
    rest = Gather(jnp.concatenate(rest)[None], 0, lows)
    fourth = Gather(jnp.concatenate([up_parts[1], w_down[part_rows:]])[None], 1, lows)
    first.launch()
    marks.append(first.finish([rest.held]))
    marks.append(rest.until(3))
    first.launch()
    pair = tie(jnp.stack([memory[:, 0], memory_grad[:, 0]]), marks[1:2])
    other = swap(pair, "slot", 2)
    marks.append(first.finish())
    first.launch(marks[2:3])
    rest.launch(marks[3:])
    fourth.until(4, marks[3:])
    fourth.launch(marks[3:])
    other = tie(other, marks[3:])
    low, high = jnp.where(slot_low, pair, other), jnp.where(slot_low, other, pair)
    pair = jnp.concatenate([low, high], 2)
    other = swap(pair, "slot", 1)
    first.finish()
    rest.finish([first.held])
    fourth.finish([first.held])
    first.launch([rest.held, fourth.held])
    fourth.launch()
    second, third = [
        Gather(rest.held[:, part], 0, lows, rest.left)
        for part in (slice(0, 4 * rows), slice(4 * rows, None))
    ]
    second.launch()

    one = [(i * rows, rows, 1) for i in range(4)]
    w_query, w_key, w_value, gains = first.unpack(one[:3] + [(3 * rows, extra, 0)], me)
    w_query, w_key, w_value = w_query[0], w_key[0], w_value[0]

    tok_flat = tokens.reshape(total, width)
    cot_flat = out_grad.reshape(total, width)
    low = lambda n, w: like((n, w), BF16)

    wide = like((total, width), F32)
    slot_like = low(mem_rows, width)
    slot_wide = like((mem_rows, width), F32)
    (
        normed, queries, tok_keys, tok_values, slot_keys, slot_values, mem_low, mem_cot
    ) = kernel_call(
        project_kernel,
        [me, tok_flat, pair, other, gains, w_query, w_key, w_value],
        [low(total, width)] * 4 + [slot_like] * 4,
        6,
        cost(6 * total * width * width, 8 << 20),
        "project",
        after=[rest.held],
    )
    second.finish([normed])
    fourth.finish([normed])
    third.launch([second.held, fourth.held])
    second.launch([second.held, fourth.held])
    fourth.launch([second.held, fourth.held])

    square = low(tok_dev, width)
    reads = []
    for m in range(micro):
        reads.append(
            kernel_call(
                functools.partial(read_kernel, m),
                [queries, tok_keys, tok_values, slot_keys, slot_values, starts, keep],
                [
                    square,
                    like((width, tok_dev), F32),
                    like((pairs, 8, tok_dev), F32),
                    like((pairs, 2, keys, tok_dev), BF16),
                ],
                6,
                cost(16 * total * width * keys // micro, 8 << 20, total * keys * HEADS // micro),
                "read",
                scalars=0,
                after=(second.held,) if m == 0 else (third.held,),
                scratch_shapes=[pltpu.VMEM((tok_dev, tok_dev), F32)],
            )
        )
        if m == 0:
            third.finish([reads[0][0]])
            second.finish([reads[0][0]])
            fourth.finish([reads[0][0]])
            ready = [second.held, third.held, fourth.held]
            third.launch(ready)
            second.launch(ready)
            fourth.launch(ready)
    attended = [kept[0] for kept in reads]

    second_mats = second.unpack(one, me, [attended[1]])
    w_slot_query, w_slot_out, w_forget, w_out = (m[0] for m in second_mats)
    third.finish([attended[1]])
    third.launch([w_slot_query, third.held])
    ffn_sections = [(0, rows, cuts), (cuts * rows, part_rows, 1)]
    up_first, down_first = third.unpack(ffn_sections, me)
    slot_queries, part = kernel_call(
        write_kernel,
        [mem_low, w_slot_query, tok_keys, tok_values, slot_keys, keep],
        [slot_like, like((micro, 72, slots * HEADS), F32)],
        3,
        cost(8 * total * width * slots, 5 << 20, total * slots * HEADS),
        "write",
        scalars=0,
        after=[third.held],
    )

    def merged(part, other):
        top_a, top_b = part[:, 64:65], other[:, 64:65]
        top = jnp.maximum(top_a, top_b)
        scale_a, scale_b = jnp.exp(top_a - top), jnp.exp(top_b - top)
        mix = part[:, :64] * scale_a + other[:, :64] * scale_b
        tot = part[:, 65:66] * scale_a + other[:, 65:66] * scale_b
        return jnp.concatenate([mix, top, tot, part[:, 66:]], 1)

    part = merged(part, swap(part, "slot", 1))
    other = swap(part, "slot", 2)

    half_cost = cost(7 * total * width * ff, 14 << 20, total * ff // 2)
    tall = [pltpu.VMEM((total, ff // 2), BF16)] * 2 + [pltpu.VMEM((total, width), BF16)]
    sums_first = Shares(0, ffn_sections, me, width)
    resid, out_part, d_low, *outs = kernel_call(
        functools.partial(ffn_first_kernel, sums_first),
        [me, *attended, tok_flat, cot_flat, w_out, up_first, down_first[0], gains],
        [wide] * 3 + sums_first.shapes(),
        13,
        half_cost,
        "ffn_first",
        scratch_shapes=tall,
        after=[part],
    )
    part = merged(part, tie(other, [resid]))
    fourth.finish([resid])
    sums_first.begin(outs, [part, fourth.held])
    fourth.launch([part])

    sums_slot = Shares(0, one[:3], me, width)
    new_memory, base, d_sq, own_sk, own_sv, w_dk, w_dv, g_mem, *outs = kernel_call(
        functools.partial(memory_kernel, sums_slot),
        [me, part, mem_low, mem_cot, slot_keys, slot_values, slot_queries]
        + [tok_keys, tok_values, keep, w_slot_out, w_forget, gains],
        [like((micro, slot_rows, width), BF16), slot_wide]
        + [slot_like]
        + [slot_wide] * 2
        + [low(total, width)] * 2
        + [like((8, width), F32)]
        + sums_slot.shapes(),
        4,
        cost(12 * mem_rows * width * width + 12 * total * width * slots, 8 << 20),
        "memory",
        scratch_shapes=[pltpu.VMEM((mem_rows, width), F32)],
        after=[resid, fourth.held],
    )
    sums_first.join(sums_slot.split(outs))
    up_second, down_second = fourth.unpack(ffn_sections, me, [base])
    sums_first.finish([up_second])
    sums_first.launch()

    sections = [(0, rows, cuts), (cuts * rows, part_rows, 1)]
    sections += [(cuts * rows + part_rows, rows, 1)]
    sums_second = Shares(0, sections, me, width)
    turned = like((width, tok_dev), F32)
    layer_out, d_resid, da_a, da_b, g_ffn, *outs = kernel_call(
        functools.partial(ffn_second_kernel, sums_second),
        [me, *attended, resid, out_part, d_low, cot_flat, w_out, up_second, down_second[0], gains],
        [low(total, width), wide, turned, turned, like((8, width), F32)] + sums_second.shapes(),
        17,
        half_cost,
        "ffn_second",
        scratch_shapes=tall + [pltpu.VMEM((total, width), BF16)],
        after=[sums_first.send],
    )
    sums_first.finish([d_resid])
    sums_second.begin(outs, [sums_first.send])
    sums_first.launch()
    back = []
    for m, da_t in enumerate((da_a, da_b)):
        found = kernel_call(
            functools.partial(back_kernel, m),
            [queries, tok_keys, tok_values, slot_keys, slot_values]
            + [da_t, *reads[m][1:], w_dk, w_dv, own_sk, own_sv],
            [square] * 3 + [low(slots, width)] * 2,
            6,
            cost(24 * total * width * keys // micro, 10 << 20),
            "back",
            scalars=0,
            after=[sums_first.send] + ([sums_second.send] if m else []),
        )
        back += found
        if m == 0:
            sums_second.finish([found[0]])
            sums_first.finish([found[0]])
            sums_second.launch([sums_first.send])
            sums_first.launch([sums_second.send])

    sums_third = Shares(0, one[:3] + [(3 * rows, extra, 1)], me, width)
    outs = kernel_call(
        functools.partial(grads_kernel, sums_third),
        [me, normed, *back, mem_low, w_query, w_key, w_value, gains, g_ffn, g_mem],
        sums_third.shapes(),
        8,
        cost(6 * total * width * width, 8 << 20),
        "grads",
        after=[sums_first.send],
    )
    sums_second.finish(outs[:1])
    sums_first.finish(outs[:1])
    sums_third.begin(outs, [sums_second.send, sums_first.send])
    sums_second.launch([sums_first.send])
    sums_first.launch([sums_second.send])
    sums_third.finish([sums_first.send])
    sums_third.launch()
    tokens_grad, mem_keep, mem_send = kernel_call(
        input_kernel,
        [me, tok_flat, d_resid, *back, d_sq, base, w_query, w_key, w_value, w_slot_query, gains],
        [low(total, width)] + [like((micro, slots // 2, width), F32)] * 2,
        10,
        cost(6 * total * width * width, 12 << 20),
        "input",
        after=[sums_third.send],
        scratch_shapes=[pltpu.VMEM((mem_rows, width), F32)],
    )
    sums_third.finish([tokens_grad])
    sums_third.launch()
    ends = [sums_third.send]
    while sums_second.done < sums_second.steps:
        sums_second.finish(ends)
        sums_second.launch()
        if sums_third.done < sums_third.steps:
            sums_third.finish([sums_second.send])
            sums_third.launch()
        ends = [sums_third.send]
    held, sent = mem_keep, tie(mem_send, ends[:0])
    bits = axis_bits("slot")
    for i, (axis, distance) in enumerate(bits):
        got = swap(sent, axis, distance)
        if i + 1 < len(bits):
            held, sent = kernel_call(
                functools.partial(split_kernel, i + 1),
                [me, held, got],
                [like((micro, held.shape[1] // 2, width), F32)] * 2,
                2,
                cost(held.size, 8 * held.size),
                "split",
            )
    moved = held + got
    while sums_third.done < sums_third.steps:
        sums_third.finish()
        sums_third.launch()
    while sums_first.done < sums_first.steps:
        sums_first.finish()
        sums_first.launch()
    sums_first = sums_first.end([tokens_grad])
    sums_second, sums_third = sums_second.end(), sums_third.end()

    piece = lambda m, i: m[i * rows : (i + 1) * rows]

    def up_piece(m, at):
        return m[at : at + cuts * rows].reshape(cuts, rows, width).transpose(1, 0, 2).reshape(
            rows, device_count, 1, part_rows
        )

    up_share = jnp.concatenate([up_piece(sums_first, 0), up_piece(sums_second, 0)], 2)
    down_at = cuts * rows
    down_share = jnp.concatenate(
        [m[down_at : down_at + part_rows] for m in (sums_first, sums_second)]
    )
    mixed = sums_first[down_at + part_rows :]
    gain_share = jnp.dot(
        sums_third[3 * rows : 3 * rows + 3], pick, precision=lax.Precision.HIGHEST
    )
    return (
        layer_out.reshape(micro, tok_dev, width),
        new_memory[:, None],
        tokens_grad.reshape(micro, tok_dev, width),
        moved.astype(BF16)[:, None],
        piece(sums_third, 0),
        piece(sums_third, 1),
        piece(sums_third, 2),
        sums_second[down_at + part_rows :],
        up_share.reshape(rows, ff),
        down_share,
        piece(mixed, 0),
        piece(mixed, 1),
        piece(mixed, 2),
        gain_share[0],
        gain_share[1],
        gain_share[2],
    )


def solution(mesh):
    weight = P(("batch", "slot"), None)
    gain = P(("batch", "slot"))
    rows = P(None, ("batch", "slot"), None)
    slots = P(None, "batch", "slot", None)
    return jax.shard_map(
        on_device,
        mesh=mesh,
        in_specs=(rows, slots, P(), P(None, "batch")) + (weight,) * 9 + (gain,) * 3 + (rows, slots),
        out_specs=(rows, slots, rows, slots) + (weight,) * 9 + (gain,) * 3,
        check_vma=False,
    )
```

```python
import functools

import jax
import jax.numpy as jnp
from jax import lax
from jax.experimental import pallas as pl
from jax.experimental.pallas import tpu as pltpu
from jax.sharding import PartitionSpec as P

HEADS = 8
HEAD_DIM = 64
SEG = 512
EPSILON = 1e-05
MASKED = -1e30
BF16 = jnp.bfloat16
F32 = jnp.float32
SCALE = HEAD_DIM ** (-0.5)
SMEM = pl.BlockSpec(memory_space=pltpu.SMEM)
VMEM = pl.BlockSpec(memory_space=pltpu.VMEM)
ANY = pl.BlockSpec(memory_space=pl.ANY)


def swap(value, axis, distance):
    pairs = [(i, i ^ distance) for i in range(lax.axis_size(axis))]
    return lax.ppermute(value, axis, pairs)


def own_bit(axis, distance):
    return (lax.axis_index(axis) // distance) % 2


def axis_bits(axis):
    return [(axis, 1 << i) for i in range(lax.axis_size(axis).bit_length() - 1)]


def exchange_orders(turn):
    rest = axis_bits("slot")[1:] + axis_bits("batch")
    if turn:
        rest = rest[2:3] + rest[:2] + rest[3:]
    other = list(rest)
    for i in range(0, len(rest) - 1, 2):
        other[i], other[i + 1] = rest[i + 1], rest[i]
    return rest, other


def lane_swap(value, orders, step):
    slots = lax.axis_size("slot")
    pairs = []
    for batch in range(lax.axis_size("batch")):
        for slot in range(slots):
            axis, distance = orders[slot % 2][step]
            to_batch, to_slot = batch, slot
            if axis == "batch":
                to_batch = batch ^ distance
            else:
                to_slot = slot ^ distance
            pairs.append((batch * slots + slot, to_batch * slots + to_slot))
    return lax.ppermute(value, ("batch", "slot"), pairs)


def lane_bit(orders, step):
    lane = own_bit("slot", 1)
    return jnp.where(lane == 0, own_bit(*orders[0][step]), own_bit(*orders[1][step]))


def chunk_places(order):
    natural = (axis_bits("slot")[1:] + axis_bits("batch"))
    count = len(order)
    places = []
    for pair in range(1 << count):
        place = 0
        for step, bit in enumerate(order):
            place |= ((pair >> natural.index(bit)) & 1) << (count - 1 - step)
        places.append(place)
    return places


def tie(value, after):
    return lax.optimization_barrier((value,) + tuple(after))[0] if after else value


class Gather:
    def __init__(self, held, turn, lows, left=None):
        self.turn, self.orders, self.lows = turn, exchange_orders(turn), lows
        self.left = len(self.orders[0]) if left is None else left
        self.held, self.got = held, None

    def launch(self, after=()):
        held = tie(self.held, after)
        if self.left == 0:
            self.got = swap(held, "slot", 1)
            return
        self.left -= 1
        self.got = lane_swap(held, self.orders, self.left)

    def finish(self, after=()):
        mine = self.lows[self.turn][self.left]
        got = tie(self.got, after)
        low = jnp.where(mine, self.held, got)
        high = jnp.where(mine, got, self.held)
        self.held = jnp.concatenate([low, high], 0)
        return self.held

    def until(self, left, after=()):
        while self.left > left:
            self.launch(after)
            self.finish()
        return self.held

    def unpack(self, sections, me, after=()):
        return unpack(self.held, self.got, self.turn, sections, me, after)


def place_kernel(places, sections, me_ref, held, got, *outs):
    for lane in range(2):

        @pl.when(me_ref[0] == lane)
        def _():
            sums = []
            for kind in range(2):
                source = held if kind == lane else got
                for pair, place in enumerate(places[kind]):
                    device = 2 * pair + kind
                    for (at, rows, lead), out in zip(sections, outs):
                        if lead == 0:
                            sums.append(source[place, at : at + rows, :].astype(F32))
                        for i in range(lead):
                            here = slice(device * rows, (device + 1) * rows)
                            out[i, here, :] = source[place, at + i * rows : at + (i + 1) * rows, :]
            if sums:
                outs[-1][...] = sum(sums[1:], sums[0])


def unpack(held, got, turn, sections, me, after):
    orders = exchange_orders(turn)
    places = [chunk_places(order) for order in orders]
    count, _, width = held.shape
    if all(rows % 16 == 0 for _, rows, lead in sections if lead):
        body = functools.partial(place_kernel, places, sections)
        outs = [
            like((lead, 2 * count * rows, width), BF16) if lead else like((rows, width), F32)
            for _, rows, lead in sections
        ]
        return kernel_call(
            body, [me, held, got], outs, 4, cost(0, 4 * held.size), "place", after
        )
    low = jnp.where(me[0] == 0, held, got)[jnp.array(places[0])]
    high = jnp.where(me[0] == 0, got, held)[jnp.array(places[1])]
    full = jnp.stack([low, high], 1).reshape(2 * count, -1, width)
    outs = []
    for at, rows, lead in sections:
        if lead == 0:
            outs.append(jnp.sum(full[:, at : at + rows].astype(F32), 0))
            continue
        part = full[:, at : at + rows * lead].reshape(2 * count, lead, rows, width)
        outs.append(part.transpose(1, 0, 2, 3).reshape(lead, -1, width))
    return outs


class Shares:
    def __init__(self, turn, sections, me, width, bits):
        self.turn, self.sections, self.me, self.width = turn, sections, me, width
        self.bits = bits[turn]
        self.rows = sum(rows * lead for _, rows, lead in sections)
        self.places = [chunk_places(order) for order in exchange_orders(turn)]
        self.count = len(self.places[0])
        self.direct = all(rows % 8 == 0 for _, rows, _ in sections)

    def shapes(self):
        if self.direct:
            return [like((self.count, self.rows, self.width), BF16)] * 2
        return [
            like((lead, 2 * self.count * rows, self.width), BF16)
            for _, rows, lead in self.sections
        ]

    def put(self, refs, me_ref, section, lead, first_row, value):
        at, rows, _ = self.sections[section]
        if not self.direct:
            refs[section][lead, first_row : first_row + value.shape[0], :] = value
            return
        keep, send = refs
        at = at + lead * rows
        for lane in range(2):

            @pl.when(me_ref[0] == lane)
            def _():
                for i in range(value.shape[0] // rows):
                    device = first_row // rows + i
                    target = keep if device % 2 == lane else send
                    place = self.places[device % 2][device // 2]
                    target[place, at : at + rows, :] = value[i * rows : (i + 1) * rows]

    def split(self, outs):
        if self.direct:
            return outs
        parts = []
        for (_, rows, lead), out in zip(self.sections, outs):
            part = out.reshape(lead, 2 * self.count, rows, self.width).transpose(1, 0, 2, 3)
            parts.append(part.reshape(2 * self.count, lead * rows, self.width))
        full = jnp.concatenate(parts, 1).reshape(self.count, 2, -1, self.width)
        back = []
        for kind in range(2):
            order = [0] * self.count
            for pair, place in enumerate(self.places[kind]):
                order[place] = pair
            back.append(full[:, kind][jnp.array(order)])
        lane = self.me[0]
        return [jnp.where(lane == 0, back[0], back[1]), jnp.where(lane == 0, back[1], back[0])]

    def begin(self, outs, after=()):
        self.orders = exchange_orders(self.turn)
        self.steps = len(self.orders[0])
        self.done, self.extra = 0, []
        self.keep, self.send = self.split(outs)
        self.got = swap(tie(self.send, after), "slot", 1)

    def join(self, outs, after=()):
        keep, send = outs
        got = swap(tie(send, after), "slot", 1)
        self.extra.append((keep, got))

    def finish(self, after=()):
        bit = self.bits[self.done]
        if self.extra:
            keep, got = self.extra.pop()
            self.keep, self.send = halve_two(
                self.keep, self.got, keep, got, bit, self.direct, after
            )
            return self.send
        self.keep, self.send = halve(self.keep, self.got, bit, self.direct, after)
        return self.send

    def launch(self, after=()):
        self.got = lane_swap(tie(self.send, after), self.orders, self.done)
        self.done += 1

    def end(self, after=()):
        return self.keep[0].astype(F32) + tie(self.got, after)[0].astype(F32)


def halve_two_kernel(bit, keep_a, got_a, keep_b, got_b, keep_out, send_out):
    rows = keep_a.shape[1]
    halve_kernel(bit, keep_a, got_a, keep_out.at[:, :rows], send_out.at[:, :rows])
    halve_kernel(bit, keep_b, got_b, keep_out.at[:, rows:], send_out.at[:, rows:])


def halve_two(keep_a, got_a, keep_b, got_b, bit, direct, after):
    if not direct:
        keep = jnp.concatenate([keep_a, keep_b], 1)
        return halve(keep, jnp.concatenate([got_a, got_b], 1), bit, direct, after)
    count, rows, width = keep_a.shape
    shape = (count // 2, rows + keep_b.shape[1], width)
    return kernel_call(
        halve_two_kernel,
        [bit, keep_a, got_a, keep_b, got_b],
        [like(shape, BF16)] * 2,
        4,
        cost(2 * keep_a.size, 12 * keep_a.size),
        "halve",
        after,
    )


def halve_kernel(bit, keep, got, keep_out, send_out):
    half = keep_out.shape[0]
    mine = pl.ds(bit[0] * half, half)
    other = pl.ds((1 - bit[0]) * half, half)
    send_out[...] = keep[other] + got[other]
    keep_out[...] = keep[mine] + got[mine]


def halve(keep, got, bit, direct, after):
    count, rows, width = keep.shape
    half = count // 2
    if direct:
        return kernel_call(
            halve_kernel,
            [bit, keep, got],
            [like((half, rows, width), BF16)] * 2,
            4,
            cost(keep.size, 6 * keep.size),
            "halve",
            after,
        )
    bit = bit[0]
    total = tie(keep, after) + got
    take = lambda b: lax.dynamic_slice_in_dim(total, b * half, half, 0)
    return take(bit), take(1 - bit)


def dot(a, b):
    return jnp.dot(a, b, preferred_element_type=F32)


def dot_nt(a, b):
    return lax.dot_general(a, b, (((1,), (1,)), ((), ())), preferred_element_type=F32)


def dot_tn(a, b):
    return lax.dot_general(a, b, (((0,), (0,)), ((), ())), preferred_element_type=F32)


def norm_parts(rows):
    centre = jnp.mean(rows, axis=-1, keepdims=True)
    centred = rows - centre
    spread = jnp.mean(centred * centred, axis=-1, keepdims=True)
    inverse = lax.rsqrt(spread + EPSILON)
    return centred * inverse, inverse


def norm_back(cot, hat, inverse, gain):
    d_hat = cot * gain
    first = jnp.mean(d_hat, axis=-1, keepdims=True)
    second = jnp.mean(d_hat * hat, axis=-1, keepdims=True)
    return inverse * (d_hat - first - hat * second)


def head_lanes(value, head):
    lane = lax.broadcasted_iota(jnp.int32, value.shape, 1)
    return jnp.where(lane // HEAD_DIM == head, value, jnp.zeros_like(value))


def head_rows(value, head):
    row = lax.broadcasted_iota(jnp.int32, value.shape, 0)
    return jnp.where(row // HEAD_DIM == head, value, jnp.zeros_like(value))


def both_heads(value):
    return jnp.concatenate([head_lanes(value, 0), head_lanes(value, 1)], 0)


def to_slot_lanes(value):
    turned = value.T
    return jnp.concatenate([turned[:HEAD_DIM], turned[HEAD_DIM:]], 1)


def to_slot_rows(value):
    turned = value.T
    half = turned.shape[0] // 2
    return jnp.concatenate([turned[:half], turned[half:]], 1)


def diagonal(value):
    lane = lax.broadcasted_iota(jnp.int32, (HEAD_DIM, value.shape[1]), 1)
    return jnp.where(lane < value.shape[1] // 2, value[:HEAD_DIM], value[HEAD_DIM:])


ROWS = 512


def row_loop(total):
    return lambda body: pl.loop(0, total // ROWS)(
        lambda i: body(pl.ds(pl.multiple_of(i * ROWS, ROWS), ROWS))
    )


def pair_loop(width):
    return lambda body: pl.loop(0, width // 128, unroll=2)(
        lambda p: body(p, pl.ds(pl.multiple_of(p * 128, 128), 128))
    )


def project_kernel(
    me_ref, tok, pair, other, gain, wq, wk, wv, normed, q, k, v, sk, sv, mem, mem_cot
):
    half = pair.shape[2]
    rows = half // 2
    for lane in range(2):

        @pl.when(me_ref[0] == lane)
        def _():
            for kind, out in enumerate((mem, mem_cot)):
                for m in range(pair.shape[1]):
                    for i in range(2):
                        for core in range(2):
                            source = pair if core == lane else other
                            at = 2 * (m * half + i * rows) + core * rows
                            block = source[kind, m, i * rows : (i + 1) * rows, :]
                            out[at : at + rows, :] = block

    @row_loop(tok.shape[0])
    def _(here):
        hat, _ = norm_parts(tok[here, :].astype(F32))
        low = (hat * gain[0:1, :]).astype(BF16)
        normed[here, :] = low
        q[here, :] = dot(low, wq[...]).astype(BF16)
        k[here, :] = dot(low, wk[...]).astype(BF16)
        v[here, :] = dot(low, wv[...]).astype(BF16)

    sk[...] = dot(mem[...], wk[...]).astype(BF16)
    sv[...] = dot(mem[...], wv[...]).astype(BF16)


def read_kernel(m, q, k, v, sk, sv, starts, keep, attended, out_t, inv, e_ref, bias):
    tok = attended.shape[0]
    slots = sk.shape[0] // keep.shape[0]
    key_at = lax.broadcasted_iota(jnp.int32, (tok, tok), 0)
    query_at = lax.broadcasted_iota(jnp.int32, (tok, tok), 1)
    start = starts[m, 0:1, :]
    kept = jnp.broadcast_to(keep[m, 0:1, :], (128, tok)).T
    kept = jnp.concatenate([kept] * (tok // 128), 1)
    good = (key_at >= start) & (key_at <= query_at) & (kept > 0)
    bias[...] = jnp.where(good, 0.0, MASKED)
    here, slot_here = pl.ds(m * tok, tok), pl.ds(m * slots, slots)

    @pair_loop(q.shape[1])
    def _(p, lanes):
        read_pair(
            q[here, lanes], k[here, lanes], v[here, lanes], sk[slot_here, lanes],
            sv[slot_here, lanes], bias, attended.at[:, lanes],
            out_t.at[pl.ds(pl.multiple_of(p * 128, 128), 128), :], inv.at[p], e_ref.at[p],
        )


def read_pair(q, keys, values, slot_keys, slot_values, bias, attended, out_t, inv, e_ref):
    tok = q.shape[0]
    half = tok // 2
    slots = slot_keys.shape[0]
    scaled = q * jnp.asarray(SCALE, BF16)
    values_t = values.T
    slot_values_t = slot_values.T
    outs, inverses = [], []
    for head in range(2):
        qm = head_lanes(scaled, head)
        rows = slice(head * HEAD_DIM, (head + 1) * HEAD_DIM)
        s_mem = dot_nt(slot_keys, qm)
        s_a = dot_nt(keys[:half], qm) + bias[:half, :]
        s_b = dot_nt(keys[half:], qm[half:]) + bias[half:, half:]
        top = jnp.maximum(jnp.max(s_mem, 0, keepdims=True), jnp.max(s_a, 0, keepdims=True))
        top_b = jnp.maximum(top[:, half:], jnp.max(s_b, 0, keepdims=True))
        top = jnp.concatenate([top[:, :half], top_b], 1)
        e_mem = jnp.exp(s_mem - top)
        e_a = jnp.exp(s_a - top)
        e_b = jnp.exp(s_b - top_b)
        total = jnp.sum(e_mem, 0, keepdims=True) + jnp.sum(e_a, 0, keepdims=True)
        total_b = total[:, half:] + jnp.sum(e_b, 0, keepdims=True)
        total = jnp.concatenate([total[:, :half], total_b], 1)
        e_mem, e_a, e_b = e_mem.astype(BF16), e_a.astype(BF16), e_b.astype(BF16)
        e_ref[head, :slots, :] = e_mem
        e_ref[head, slots : slots + half, :] = e_a
        e_ref[head, slots + half :, half:] = e_b
        e_ref[head, slots + half :, :half] = jnp.zeros((half, half), BF16)
        mix = dot(slot_values_t[rows], e_mem) + dot(values_t[rows, :half], e_a)
        mix_b = mix[:, half:] + dot(values_t[rows, half:], e_b)
        mix = jnp.concatenate([mix[:, :half], mix_b], 1)
        inverse = 1.0 / total
        outs.append(mix * inverse)
        inverses.append(inverse)
    out = jnp.concatenate(outs, 0)
    out_t[...] = out
    inv[...] = jnp.concatenate(inverses + [jnp.zeros((6, tok), F32)], 0)
    attended[...] = out.T.astype(BF16)


def write_kernel(mem, wsq, k, v, sk, keep, sq_ref, part):
    micro = keep.shape[0]
    tok = k.shape[0] // micro
    slots = mem.shape[0] // micro
    pairs = k.shape[1] // 128
    sq = dot(mem[...], wsq[...]).astype(BF16)
    sq_ref[...] = sq
    for m in range(micro):
        kept = jnp.broadcast_to(keep[m, 0:1, :], (128, tok)).T
        bias = jnp.where(kept > 0, 0.0, MASKED)
        for p in range(pairs):
            lanes = slice(p * 128, p * 128 + 128)
            mine = sq[m * slots : (m + 1) * slots, lanes]
            own = to_slot_lanes(
                mine.astype(F32) * sk[m * slots : (m + 1) * slots, lanes].astype(F32)
            )
            own = jnp.sum(own, 0, keepdims=True) * SCALE
            scores = dot_nt(k[m * tok : (m + 1) * tok, lanes], both_heads(mine)) * SCALE + bias
            top = jnp.maximum(jnp.max(scores, 0, keepdims=True), own)
            e = jnp.exp(scores - top)
            total = jnp.sum(e, 0, keepdims=True)
            mix = diagonal(dot_tn(v[m * tok : (m + 1) * tok, lanes], e.astype(BF16)))
            part[m, :HEAD_DIM, lanes] = mix
            part[m, HEAD_DIM:, lanes] = jnp.concatenate(
                [top, total, own, jnp.zeros((5, 128), F32)], 0
            )


def gelu_pair(hidden):
    root = 0.7978845608028654
    square = hidden * hidden
    bent = jnp.tanh(hidden * (root + (root * 0.044715) * square))
    half = 0.5 + 0.5 * bent
    slope = half + (0.5 * hidden) * (1.0 - bent * bent) * (root + (3.0 * root * 0.044715) * square)
    return (hidden * half).astype(BF16), slope


def ffn_cuts(low, cot_low, up, down, here, act_all, dh_all):
    width = low.shape[1]
    out = d_low = 0.0
    for cut in range(up.shape[0]):
        cols = slice(cut * width, (cut + 1) * width)
        act, slope = gelu_pair(dot(low, up[cut]))
        d_hidden = (dot_nt(cot_low, down[cols, :]) * slope).astype(BF16)
        act_all[here, cols] = act
        dh_all[here, cols] = d_hidden
        out = out + dot(act, down[cols, :])
        d_low = d_low + dot_nt(d_hidden, up[cut])
    return out, d_low


def ffn_grads(shares, refs, me_ref, base, low_all, cot_all, act_all, dh_all, cuts):
    width = low_all.shape[1]
    low_t = low_all[...].T
    for cut in range(cuts):
        cols = slice(cut * width, (cut + 1) * width)
        shares.put(refs, me_ref, base, cut, 0, dot(low_t, dh_all[:, cols]).astype(BF16))
        grad = dot_tn(act_all[:, cols], cot_all[...]).astype(BF16)
        shares.put(refs, me_ref, base + 1, 0, cut * width, grad)


def ffn_first_kernel(
    shares, me_ref, att_a, att_b, tok, cot, wout, up, down, gain,
    resid_ref, out_ref, d_low_ref, *rest
):
    refs, (act_all, dh_all, low_all) = rest[:-3], rest[-3:]
    count = att_a.shape[0]
    for m, att in enumerate((att_a, att_b)):

        @row_loop(count)
        def _(there):
            here = pl.ds(there.start + m * count, ROWS)
            resid = tok[here, :].astype(F32) + dot(att[there, :], wout[...])
            hat, _ = norm_parts(resid)
            low = (hat * gain[1:2, :]).astype(BF16)
            low_all[here, :] = low
            out, d_low = ffn_cuts(low, cot[here, :], up, down, here, act_all, dh_all)
            resid_ref[here, :] = resid
            out_ref[here, :] = resid + out
            d_low_ref[here, :] = d_low

    ffn_grads(shares, refs, me_ref, 0, low_all, cot, act_all, dh_all, up.shape[0])


def ffn_second_kernel(
    shares, me_ref, att_a, att_b, resid, part, d_part, cot, wout, up, down, gain,
    layer_out, d_resid_ref, da_a, da_b, g_gain, *rest
):
    refs, (act_all, dh_all, low_all, dattn_all) = rest[:-4], rest[-4:]
    count = att_a.shape[0]
    gain_row = gain[1:2, :]
    g_gain[...] = jnp.zeros_like(g_gain)
    for m, da_t in enumerate((da_a, da_b)):

        @row_loop(count)
        def _(there):
            here = pl.ds(there.start + m * count, ROWS)
            hat, inverse = norm_parts(resid[here, :])
            low = (hat * gain_row).astype(BF16)
            low_all[here, :] = low
            cot_low = cot[here, :]
            out, d_low = ffn_cuts(low, cot_low, up, down, here, act_all, dh_all)
            layer_out[here, :] = (part[here, :] + out).astype(BF16)
            d_low = d_part[here, :] + d_low
            d_resid = cot_low.astype(F32) + norm_back(d_low, hat, inverse, gain_row)
            d_resid_ref[here, :] = d_resid
            d_attn = d_resid.astype(BF16)
            dattn_all[here, :] = d_attn
            da_t[:, there] = dot_nt(wout[...], d_attn)
            g_gain[0:1, :] += jnp.sum(d_low * hat, 0, keepdims=True)

    ffn_grads(shares, refs, me_ref, 0, low_all, cot, act_all, dh_all, up.shape[0])
    grad = dot_tn(att_a[...], dattn_all[:count, :]) + dot_tn(att_b[...], dattn_all[count:, :])
    shares.put(refs, me_ref, 2, 0, 0, grad.astype(BF16))


def memory_kernel(
    shares, me_ref, slot_ref, part, mem, cot, sk, sv, sq, k, v, keep, wso, wfg, gain,
    new_ref, base, dsq_ref, osk, osv, wdk, wdv, g_gain, *rest
):
    refs, held = rest[:-1], rest[-1]
    micro = part.shape[0]
    slots = mem.shape[0] // micro
    own_rows = new_ref.shape[1]
    pairs = mem.shape[1] // 128
    row_at = lax.broadcasted_iota(jnp.int32, (mem.shape[0], 1), 0)
    mine = ((row_at % slots) // own_rows == slot_ref[0]).astype(F32)
    probs, tots, lses = [], [], []
    lines = []
    for m in range(micro):
        here = slice(m * slots, (m + 1) * slots)
        line, prob_line = [], []
        for p in range(pairs):
            lanes = slice(p * 128, p * 128 + 128)
            top0 = part[m, HEAD_DIM : HEAD_DIM + 1, lanes]
            total0 = part[m, HEAD_DIM + 1 : HEAD_DIM + 2, lanes]
            own = part[m, HEAD_DIM + 2 : HEAD_DIM + 3, lanes]
            top = jnp.maximum(top0, own)
            own_e = jnp.exp(own - top)
            shift = jnp.exp(top0 - top)
            total = total0 * shift + own_e
            inverse = 1.0 / total
            prob = own_e * inverse
            values = to_slot_lanes(sv[here, lanes].astype(F32))
            mixed = part[m, :HEAD_DIM, lanes] * (shift * inverse) + prob * values
            line.append(to_slot_rows(mixed))
            prob_line.append((prob, top + jnp.log(total)))
        lines.append(jnp.concatenate(line, 1))
        probs.append(prob_line)
    written = jnp.concatenate(lines, 0)
    written_low = written.astype(BF16)
    mem_low = mem[...]
    mem_f32 = mem_low.astype(F32)
    update = dot(written_low, wso[...])
    gate = 1.0 / (1.0 + jnp.exp(-dot(mem_low, wfg[...])))
    gain_row = gain[2:3, :]
    hat, inverse = norm_parts(gate * mem_f32 + (1.0 - gate) * update)
    held[...] = hat * gain_row
    cot_f32 = cot[...].astype(F32)
    for m in range(micro):
        at = pl.multiple_of(m * slots + slot_ref[0] * own_rows, own_rows)
        new_ref[m] = held[pl.ds(at, own_rows), :].astype(BF16)
    g_gain[...] = jnp.broadcast_to(jnp.sum(cot_f32 * hat * mine, 0, keepdims=True), g_gain.shape)
    d_blend = norm_back(cot_f32, hat, inverse, gain_row)
    d_pre = (d_blend * (mem_f32 - update) * gate * (1.0 - gate) * mine).astype(BF16)
    d_update = (d_blend * (1.0 - gate)).astype(BF16)
    mem_t = mem_low.T
    d_upd = (d_update.astype(F32) * mine).astype(BF16)
    shares.put(refs, me_ref, 1, 0, 0, dot_tn(written_low, d_upd).astype(BF16))
    shares.put(refs, me_ref, 2, 0, 0, dot(mem_t, d_pre).astype(BF16))
    base[...] = d_blend * gate * mine + dot_nt(d_pre, wfg[...])
    d_written = dot_nt(d_update, wso[...]).astype(BF16)
    dw_f32 = d_written.astype(F32)
    product = dw_f32 * written
    tok = k.shape[0] // micro
    for m in range(micro):
        here = slice(m * slots, (m + 1) * slots)
        there = slice(m * tok, (m + 1) * tok)
        kept = jnp.broadcast_to(keep[m, 0:1, :], (128, tok)).T
        bias = jnp.where(kept > 0, 0.0, MASKED)
        for p in range(pairs):
            lanes = slice(p * 128, p * 128 + 128)
            prob, lse = probs[m][p]
            values_f32 = sv[here, lanes].astype(F32)
            delta = jnp.sum(to_slot_lanes(product[here, lanes]), 0, keepdims=True)
            own_dp = jnp.sum(to_slot_lanes(dw_f32[here, lanes] * values_f32), 0, keepdims=True)
            own_ds = prob * (own_dp - delta)
            wide = lambda r: to_slot_rows(jnp.broadcast_to(r, (HEAD_DIM, 2 * slots)))
            own_ds = wide(own_ds) * mine[here] * SCALE
            own_p = wide(prob) * mine[here]
            sq_low = sq[here, lanes]
            sq_both = both_heads(sq_low * jnp.asarray(SCALE, BF16))
            dw_low = d_written[here, lanes]
            dw_both = both_heads(dw_low)
            keys, values = k[there, lanes], v[there, lanes]
            prob = jnp.exp(dot_nt(keys, sq_both) + bias - lse)
            d_score = (prob * (dot_nt(values, dw_both) - delta)).astype(BF16)
            wdk[there, lanes] = dot(d_score, sq_both).astype(BF16)
            wdv[there, lanes] = dot(prob.astype(BF16), dw_both).astype(BF16)
            d_read = to_slot_rows(diagonal(dot_tn(keys, d_score)))
            slot_keys = sk[here, lanes].astype(F32)
            dsq_ref[here, lanes] = (d_read * SCALE + own_ds * slot_keys).astype(BF16)
            osk[here, lanes] = own_ds * sq_low.astype(F32)
            osv[here, lanes] = own_p * dw_low.astype(F32)
    shares.put(refs, me_ref, 0, 0, 0, dot(mem_t, dsq_ref[...]).astype(BF16))


def back_kernel(
    m, q, k, v, sk, sv, da_t, out_t, inv, e_ref, wdk, wdv, osk, osv, dq, dk, dv, dsk, dsv
):
    tok, slots = dq.shape[0], dsk.shape[0]
    here, slot_here = pl.ds(m * tok, tok), pl.ds(m * slots, slots)

    @pair_loop(q.shape[1])
    def _(p, lanes):
        turned = pl.ds(pl.multiple_of(p * 128, 128), 128)
        back_pair(
            q[here, lanes], k[here, lanes], v[here, lanes], sk[slot_here, lanes],
            sv[slot_here, lanes], da_t.at[turned, :], out_t.at[turned, :], inv.at[p],
            e_ref.at[p], wdk.at[here, lanes], wdv.at[here, lanes], osk.at[slot_here, lanes],
            osv.at[slot_here, lanes], dq.at[:, lanes], dk.at[:, lanes], dv.at[:, lanes],
            dsk.at[:, lanes], dsv.at[:, lanes],
        )


def back_pair(
    q, keys, values, slot_keys, slot_values, da_t, out_t, inv, e_ref, wdk, wdv, osk, osv,
    dq, dk, dv, dsk, dsv,
):
    tok = q.shape[0]
    half = tok // 2
    slots = slot_keys.shape[0]
    scaled = q * jnp.asarray(SCALE, BF16)
    keys_t = keys.T
    slot_keys_t = slot_keys.T
    norm = jnp.concatenate(
        [jnp.broadcast_to(inv[i : i + 1, :], (HEAD_DIM, tok)) for i in range(2)], 0
    )
    da = (da_t[...] * norm).astype(BF16)
    product = da.astype(F32) * out_t[...]
    da_rows = da.T
    dq_parts = []
    dk_a = dk_b = dv_a = dv_b = dk_m = dv_m = 0.0
    for head in range(2):
        rows = slice(head * HEAD_DIM, (head + 1) * HEAD_DIM)
        qm = head_lanes(scaled, head)
        dam_t = head_rows(da, head)
        dam = head_lanes(da_rows, head)
        delta = jnp.sum(product[rows], 0, keepdims=True)
        e_mem = e_ref[head, :slots, :]
        e_a = e_ref[head, slots : slots + half, :]
        e_b = e_ref[head, slots + half :, half:]
        ds_mem = (e_mem.astype(F32) * (dot(slot_values, dam_t) - delta)).astype(BF16)
        ds_a = (e_a.astype(F32) * (dot(values[:half], dam_t) - delta)).astype(BF16)
        ds_b = (
            e_b.astype(F32) * (dot(values[half:], dam_t[:, half:]) - delta[:, half:])
        ).astype(BF16)
        part = dot(slot_keys_t[rows], ds_mem) + dot(keys_t[rows, :half], ds_a)
        part_b = part[:, half:] + dot(keys_t[rows, half:], ds_b)
        dq_parts.append(jnp.concatenate([part[:, :half], part_b], 1))
        dk_a = dk_a + dot(ds_a, qm)
        dk_b = dk_b + dot(ds_b, qm[half:])
        dk_m = dk_m + dot(ds_mem, qm)
        dv_a = dv_a + dot(e_a, dam)
        dv_b = dv_b + dot(e_b, dam[half:])
        dv_m = dv_m + dot(e_mem, dam)
    dq[...] = (jnp.concatenate(dq_parts, 0) * SCALE).T.astype(BF16)

    dk[:half, :] = (dk_a + wdk[:half, :].astype(F32)).astype(BF16)
    dk[half:, :] = (dk_b + wdk[half:, :].astype(F32)).astype(BF16)
    dv[:half, :] = (dv_a + wdv[:half, :].astype(F32)).astype(BF16)
    dv[half:, :] = (dv_b + wdv[half:, :].astype(F32)).astype(BF16)
    dsk[...] = (dk_m + osk[...]).astype(BF16)
    dsv[...] = (dv_m + osv[...]).astype(BF16)


def grads_kernel(
    shares, me_ref, normed, dq_a, dk_a, dv_a, dsk_a, dsv_a, dq_b, dk_b, dv_b, dsk_b, dsv_b,
    mem, wq, wk, wv, gain, g_ffn, g_mem, *refs
):
    count = dq_a.shape[0]
    slots = dsk_a.shape[0]
    rows_t = normed[...].T
    mem_t = mem[...].T
    weighted = 0.0
    sets = (
        (dq_a, dq_b, wq, None, None),
        (dk_a, dk_b, wk, dsk_a, dsk_b),
        (dv_a, dv_b, wv, dsv_a, dsv_b),
    )
    for i, (cot_a, cot_b, weight, slot_a, slot_b) in enumerate(sets):
        grad = dot(rows_t[:, :count], cot_a[...]) + dot(rows_t[:, count:], cot_b[...])
        weighted = weighted + grad * weight[...].astype(F32)
        if slot_a is not None:
            slot_cot = jnp.concatenate([slot_a[...], slot_b[...]], 0)
            grad = grad + dot(mem_t, slot_cot)
        shares.put(refs, me_ref, i, 0, 0, grad.astype(BF16))
    folded = weighted[:, :128]
    for i in range(1, weighted.shape[1] // 128):
        folded = folded + weighted[:, i * 128 : (i + 1) * 128]
    line = jnp.sum(folded.T, 0, keepdims=True) / gain[0:1, :]
    lines = [line, g_ffn[0:1, :], g_mem[0:1, :]]
    extra = shares.sections[3][1]
    lines = jnp.concatenate(lines + [jnp.zeros((extra - 3, line.shape[1]), F32)], 0)
    lines = lines.astype(BF16)
    for device in range(2 * shares.count):
        shares.put(refs, me_ref, 3, 0, device * extra, lines)


def input_kernel(
    me_ref, tok, d_resid,
    dq_a, dk_a, dv_a, dsk_a, dsv_a, dq_b, dk_b, dv_b, dsk_b, dsv_b, dsq, base,
    wq, wk, wv, wsq, gain, tok_grad, mem_keep, mem_send, d_mem
):
    count = dq_a.shape[0]
    for m, (dq, dk, dv) in enumerate(((dq_a, dk_a, dv_a), (dq_b, dk_b, dv_b))):

        @row_loop(count)
        def _(there):
            here = pl.ds(there.start + m * count, ROWS)
            hat, inverse = norm_parts(tok[here, :].astype(F32))
            d_normed = dot_nt(dq[there, :], wq[...]) + dot_nt(dk[there, :], wk[...])
            d_normed = d_normed + dot_nt(dv[there, :], wv[...])
            back = norm_back(d_normed, hat, inverse, gain[0:1, :])
            tok_grad[here, :] = (d_resid[here, :] + back).astype(BF16)

    d_mem[...] = (
        base[...]
        + dot_nt(dsq[...], wsq[...])
        + dot_nt(jnp.concatenate([dsk_a[...], dsk_b[...]], 0), wk[...])
        + dot_nt(jnp.concatenate([dsv_a[...], dsv_b[...]], 0), wv[...])
    )
    micro, half, _ = mem_keep.shape
    slots = 2 * half
    rows = slots // 4
    for m in range(micro):
        for i in range(2):
            at = m * slots + 2 * i * rows
            mine = pl.ds(pl.multiple_of(at + me_ref[0] * rows, rows), rows)
            other = pl.ds(pl.multiple_of(at + (1 - me_ref[0]) * rows, rows), rows)
            mem_keep[m, i * rows : (i + 1) * rows, :] = d_mem[mine, :]
            mem_send[m, i * rows : (i + 1) * rows, :] = d_mem[other, :]


def split_kernel(bit, held, got, keep_out, send_out):
    half = keep_out.shape[1]
    mine = bit[0]
    for m in range(held.shape[0]):
        own = pl.ds(pl.multiple_of(mine * half, half), half)
        other = pl.ds(pl.multiple_of((1 - mine) * half, half), half)
        keep_out[m] = held[m, own, :] + got[m, own, :]
        send_out[m] = held[m, other, :] + got[m, other, :]


def kernel_call(
    body, args, out_shape, mib, price, name, after=(), scalars=1, scratch_shapes=(), far=None
):
    count = len(args)

    def run(*refs):
        body(*refs[:count], *refs[count + len(after) :])

    in_specs = [SMEM] * scalars + [VMEM] * (count - scalars) + [ANY] * len(after)
    out_specs = [VMEM] * len(out_shape)
    args, out_shape = list(args), list(out_shape)
    if far is not None and far < count:
        in_specs[far] = ANY
        args[far] = pltpu.with_memory_space_constraint(args[far], pltpu.HBM)
    elif far is not None:
        out_specs[far - count] = ANY
        out_shape[far - count] = pltpu.HBM(
            out_shape[far - count].shape, out_shape[far - count].dtype
        )
    return pl.pallas_call(
        run,
        in_specs=in_specs,
        out_specs=out_specs,
        out_shape=out_shape,
        scratch_shapes=scratch_shapes,
        compiler_params=pltpu.CompilerParams(vmem_limit_bytes=int(mib * (1 << 20))),
        cost_estimate=price,
        name=name,
    )(*args, *after)


def like(shape, dtype):
    return jax.ShapeDtypeStruct(shape, dtype)


def cost(flops, nbytes, trans=0):
    return pl.CostEstimate(flops=flops, bytes_accessed=nbytes, transcendentals=trans)


def on_device(
    tokens,
    memory,
    doc_lengths,
    key_mask,
    w_query,
    w_key,
    w_value,
    w_out,
    w_up,
    w_down,
    w_slot_query,
    w_slot_out,
    w_forget,
    norm_gain,
    ffn_gain,
    memory_gain,
    out_grad,
    memory_grad,
):
    slot_count = lax.axis_size("slot")
    slot_index = lax.axis_index("slot")
    device_count = lax.axis_size("batch") * slot_count
    device = lax.axis_index("batch") * slot_count + slot_index
    micro, tok_dev, width = tokens.shape
    slot_rows = memory.shape[2]
    slots = slot_rows * slot_count
    group_tok = tok_dev * slot_count
    dev_start = slot_index * tok_dev
    rows = w_query.shape[0]
    ff = w_up.shape[1]
    pairs = width // 128
    total = micro * tok_dev
    mem_rows = micro * slots
    keys = tok_dev + slots
    down_rows = w_down.shape[0]
    part_rows = down_rows // 2
    cuts = ff // 2 // width
    extra = 8
    lane_at = jnp.arange(width, dtype=jnp.int32) // rows
    pick = jnp.arange(width)[:, None] == device * rows + jnp.arange(rows)[None, :]
    pick = pick.astype(F32)
    keep = lax.dynamic_slice_in_dim(key_mask, dev_start, tok_dev, 1).astype(F32)
    keep = jnp.broadcast_to(keep[:, None, :], (micro, 8, tok_dev))
    segment = lax.axis_index("batch") * group_tok + dev_start
    positions = segment + jnp.arange(tok_dev, dtype=jnp.int32)
    doc_ends = jnp.cumsum(doc_lengths, axis=1, dtype=jnp.int32)
    passed = positions[None, None, :] >= doc_ends[:, :, None]
    starts = jnp.max(jnp.where(passed, doc_ends[:, :, None] - segment, 0), axis=1)
    starts = jnp.broadcast_to(starts[:, None, :], (micro, 8, tok_dev))
    bits = []
    for turn in range(2):
        orders = exchange_orders(turn)
        bits += [lane_bit(orders, step) for step in range(len(orders[0]))]
    scalars = [own_bit("slot", 1), slot_index, own_bit("slot", 2)] + bits
    scalars = [jnp.asarray(entry, jnp.int32) for entry in scalars]
    small = (keep, starts, pick, tuple(scalars), tuple(entry == 0 for entry in scalars))
    keep, starts, pick, scalars, lows = lax.optimization_barrier(small)
    me, slot_scalar, slot_high, *bits = (entry.reshape(1) for entry in scalars)
    slot_low, lows = lows[2], lows[3:]
    half = len(bits) // 2
    lows, bits = (lows[:half], lows[half:]), (bits[:half], bits[half:])
    gain_rows = jnp.stack([norm_gain, ffn_gain, memory_gain])
    gain_rows = jnp.where(lane_at == device, jnp.tile(gain_rows, (1, device_count)), 0)
    gain_rows = jnp.pad(gain_rows.astype(BF16), ((0, extra - 3), (0, 0)))
    first = Gather(jnp.concatenate([w_query, w_key, w_value, gain_rows])[None], 0, lows)
    marks = [first.until(3)]
    raw = [w_slot_query, w_slot_out, w_forget, w_out, w_up, w_down]
    raw = lax.optimization_barrier(tuple(raw) + (marks[0],))
    w_up, w_down = raw[4], raw[5]
    up_parts = w_up.reshape(rows, device_count, 2, part_rows).transpose(2, 0, 1, 3)
    up_parts = up_parts.reshape(2, rows, cuts, width).transpose(0, 2, 1, 3)
    up_parts = up_parts.reshape(2, cuts * rows, width)
    rest = list(raw[:4])
    rest += [up_parts[0], w_down[:part_rows]]
    rest = Gather(jnp.concatenate(rest)[None], 0, lows)
    fourth = Gather(jnp.concatenate([up_parts[1], w_down[part_rows:]])[None], 1, lows)
    first.launch()
    marks.append(first.finish([rest.held]))
    marks.append(rest.until(3))
    first.launch()
    pair = tie(jnp.stack([memory[:, 0], memory_grad[:, 0]]), marks[1:2])
    other = swap(pair, "slot", 2)
    marks.append(first.finish())
    other = tie(other, marks[3:])
    low, high = jnp.where(slot_low, pair, other), jnp.where(slot_low, other, pair)
    pair = jnp.concatenate([low, high], 2)
    first.launch([marks[2], pair])
    rest.launch(marks[3:])
    fourth.until(4, marks[3:])
    fourth.launch(marks[3:])
    other = swap(pair, "slot", 1)
    first.finish()
    rest.finish([first.held])
    fourth.finish([first.held])
    first.launch([rest.held, fourth.held])
    fourth.launch()
    second, third = [
        Gather(rest.held[:, part], 0, lows, rest.left)
        for part in (slice(0, 4 * rows), slice(4 * rows, None))
    ]
    second.launch()

    one = [(i * rows, rows, 1) for i in range(4)]
    w_query, w_key, w_value, gains = first.unpack(one[:3] + [(3 * rows, extra, 0)], me)
    w_query, w_key, w_value = w_query[0], w_key[0], w_value[0]

    tok_flat = tokens.reshape(total, width)
    cot_flat = out_grad.reshape(total, width)
    low = lambda n, w: like((n, w), BF16)

    wide = like((total, width), F32)
    slot_like = low(mem_rows, width)
    slot_wide = like((mem_rows, width), F32)
    (
        normed, queries, tok_keys, tok_values, slot_keys, slot_values, mem_low, mem_cot
    ) = kernel_call(
        project_kernel,
        [me, tok_flat, pair, other, gains, w_query, w_key, w_value],
        [low(total, width)] * 4 + [slot_like] * 4,
        6,
        cost(6 * total * width * width, 8 << 20),
        "project",
        after=[rest.held],
    )
    second.finish([normed])
    fourth.finish([normed])
    third.launch([second.held, fourth.held])
    second.launch([second.held, fourth.held])
    fourth.launch([second.held, fourth.held])

    square = low(tok_dev, width)
    reads = []
    for m in range(micro):
        reads.append(
            kernel_call(
                functools.partial(read_kernel, m),
                [queries, tok_keys, tok_values, slot_keys, slot_values, starts, keep],
                [
                    square,
                    like((width, tok_dev), F32),
                    like((pairs, 8, tok_dev), F32),
                    like((pairs, 2, keys, tok_dev), BF16),
                ],
                6,
                cost(16 * total * width * keys // micro, 8 << 20, total * keys * HEADS // micro),
                "read",
                scalars=0,
                after=(second.held,) if m == 0 else (third.held,),
                scratch_shapes=[pltpu.VMEM((tok_dev, tok_dev), F32)],
            )
        )
        if m == 0:
            third.finish([reads[0][0]])
            second.finish([reads[0][0]])
            fourth.finish([reads[0][0]])
            ready = [second.held, third.held, fourth.held]
            third.launch(ready)
            second.launch(ready)
            fourth.launch(ready)
    attended = [kept[0] for kept in reads]

    second_mats = second.unpack(one, me, [attended[1]])
    w_slot_query, w_slot_out, w_forget, w_out = (m[0] for m in second_mats)
    third.finish([attended[1]])
    third.launch([w_slot_query, third.held])
    ffn_sections = [(0, rows, cuts), (cuts * rows, part_rows, 1)]
    up_first, down_first = third.unpack(ffn_sections, me)
    slot_queries, part = kernel_call(
        write_kernel,
        [mem_low, w_slot_query, tok_keys, tok_values, slot_keys, keep],
        [slot_like, like((micro, 72, slots * HEADS), F32)],
        3,
        cost(8 * total * width * slots, 5 << 20, total * slots * HEADS),
        "write",
        scalars=0,
        after=[third.held],
    )

    def merged(part, other):
        top_a, top_b = part[:, 64:65], other[:, 64:65]
        top = jnp.maximum(top_a, top_b)
        scale_a, scale_b = jnp.exp(top_a - top), jnp.exp(top_b - top)
        mix = part[:, :64] * scale_a + other[:, :64] * scale_b
        tot = part[:, 65:66] * scale_a + other[:, 65:66] * scale_b
        return jnp.concatenate([mix, top, tot, part[:, 66:]], 1)

    part = merged(part, swap(part, "slot", 1))
    other = swap(part, "slot", 2)

    half_cost = cost(7 * total * width * ff, 14 << 20, total * ff // 2)
    tall = [pltpu.VMEM((total, ff // 2), BF16)] * 2 + [pltpu.VMEM((total, width), BF16)]
    sums_first = Shares(0, ffn_sections, me, width, bits)
    resid, out_part, d_low, *outs = kernel_call(
        functools.partial(ffn_first_kernel, sums_first),
        [me, *attended, tok_flat, cot_flat, w_out, up_first, down_first[0], gains],
        [wide] * 3 + sums_first.shapes(),
        13,
        half_cost,
        "ffn_first",
        scratch_shapes=tall,
        after=[part],
    )
    part = merged(part, tie(other, [resid]))
    fourth.finish([resid])
    sums_first.begin(outs, [part, fourth.held])
    fourth.launch([part])

    sums_slot = Shares(0, one[:3], me, width, bits)
    new_memory, base, d_sq, own_sk, own_sv, w_dk, w_dv, g_mem, *outs = kernel_call(
        functools.partial(memory_kernel, sums_slot),
        [me, slot_scalar, part, mem_low, mem_cot, slot_keys, slot_values, slot_queries]
        + [tok_keys, tok_values, keep, w_slot_out, w_forget, gains],
        [like((micro, slot_rows, width), BF16), slot_wide]
        + [slot_like]
        + [slot_wide] * 2
        + [low(total, width)] * 2
        + [like((8, width), F32)]
        + sums_slot.shapes(),
        4,
        cost(12 * mem_rows * width * width + 12 * total * width * slots, 8 << 20),
        "memory",
        scalars=2,
        scratch_shapes=[pltpu.VMEM((mem_rows, width), F32)],
        after=[resid, fourth.held],
    )
    sums_first.join(sums_slot.split(outs))
    up_second, down_second = fourth.unpack(ffn_sections, me, [base])
    sums_first.finish([up_second])
    sums_first.launch()

    sections = [(0, rows, cuts), (cuts * rows, part_rows, 1)]
    sections += [(cuts * rows + part_rows, rows, 1)]
    sums_second = Shares(0, sections, me, width, bits)
    turned = like((width, tok_dev), F32)
    layer_out, d_resid, da_a, da_b, g_ffn, *outs = kernel_call(
        functools.partial(ffn_second_kernel, sums_second),
        [me, *attended, resid, out_part, d_low, cot_flat, w_out, up_second, down_second[0], gains],
        [low(total, width), wide, turned, turned, like((8, width), F32)] + sums_second.shapes(),
        17,
        half_cost,
        "ffn_second",
        scratch_shapes=tall + [pltpu.VMEM((total, width), BF16)],
        after=[sums_first.send],
    )
    sums_first.finish([d_resid])
    sums_second.begin(outs, [sums_first.send])
    sums_first.launch()
    back = []
    for m, da_t in enumerate((da_a, da_b)):
        found = kernel_call(
            functools.partial(back_kernel, m),
            [queries, tok_keys, tok_values, slot_keys, slot_values]
            + [da_t, *reads[m][1:], w_dk, w_dv, own_sk, own_sv],
            [square] * 3 + [low(slots, width)] * 2,
            6,
            cost(24 * total * width * keys // micro, 10 << 20),
            "back",
            scalars=0,
            after=[sums_first.send] + ([sums_second.send] if m else []),
        )
        back += found
        if m == 0:
            sums_second.finish([found[0]])
            sums_first.finish([found[0]])
            sums_second.launch([sums_first.send])
            sums_first.launch([sums_second.send])

    sums_third = Shares(0, one[:3] + [(3 * rows, extra, 1)], me, width, bits)
    outs = kernel_call(
        functools.partial(grads_kernel, sums_third),
        [me, normed, *back, mem_low, w_query, w_key, w_value, gains, g_ffn, g_mem],
        sums_third.shapes(),
        8,
        cost(6 * total * width * width, 8 << 20),
        "grads",
        after=[sums_first.send],
    )
    sums_second.finish(outs[:1])
    sums_first.finish(outs[:1])
    sums_third.begin(outs, [sums_second.send, sums_first.send])
    sums_second.launch([sums_first.send])
    sums_first.launch([sums_second.send])
    sums_second.finish()
    sums_third.finish([sums_second.send])
    sums_third.launch()
    sums_second.launch([sums_third.send])
    tokens_grad, mem_keep, mem_send = kernel_call(
        input_kernel,
        [me, tok_flat, d_resid, *back, d_sq, base, w_query, w_key, w_value, w_slot_query, gains],
        [low(total, width)] + [like((micro, slots // 2, width), F32)] * 2,
        10,
        cost(6 * total * width * width, 12 << 20),
        "input",
        after=[sums_third.send, sums_second.send],
        scratch_shapes=[pltpu.VMEM((mem_rows, width), F32)],
    )
    piece = lambda m, i: m[i * rows : (i + 1) * rows]

    def up_piece(m, at):
        return m[at : at + cuts * rows].reshape(cuts, rows, width).transpose(1, 0, 2).reshape(
            rows, device_count, 1, part_rows
        )

    while sums_first.done < sums_first.steps:
        sums_first.finish()
        sums_first.launch()
    sums_second.finish([mem_keep])
    total_first = sums_first.end([sums_second.send])
    sums_third.finish([sums_second.send, total_first])
    got = swap(tie(mem_send, [sums_third.send]), "slot", 1)
    sums_third.launch()
    sums_second.launch([sums_third.send])
    while sums_second.done < sums_second.steps:
        sums_second.finish()
        sums_second.launch()
    total_second = sums_second.end([sums_third.send])
    held, sent = kernel_call(
        split_kernel,
        [slot_high, mem_keep, got],
        [like((micro, slot_rows, width), F32)] * 2,
        2,
        cost(mem_keep.size, 8 * mem_keep.size),
        "split",
        after=[sums_third.send],
    )
    got = swap(sent, "slot", 2)
    sums_third.finish([total_second, held])
    sums_third.launch()
    moved = held + tie(got, [sums_third.send])
    total_first, total_second = lax.optimization_barrier(
        (total_first, total_second, sums_third.send)
    )[:2]
    up_share = jnp.concatenate([up_piece(total_first, 0), up_piece(total_second, 0)], 2)
    down_at = cuts * rows
    down_share = jnp.concatenate(
        [m[down_at : down_at + part_rows] for m in (total_first, total_second)]
    )
    mixed = total_first[down_at + part_rows :]
    sums_third.finish([moved, up_share])
    sums_third.launch()
    while sums_third.done < sums_third.steps:
        sums_third.finish()
        sums_third.launch()
    sums_third = sums_third.end()
    gain_share = jnp.dot(
        sums_third[3 * rows : 3 * rows + 3], pick, precision=lax.Precision.HIGHEST
    )
    return (
        layer_out.reshape(micro, tok_dev, width),
        new_memory[:, None],
        tokens_grad.reshape(micro, tok_dev, width),
        moved.astype(BF16)[:, None],
        piece(sums_third, 0),
        piece(sums_third, 1),
        piece(sums_third, 2),
        total_second[down_at + part_rows :],
        up_share.reshape(rows, ff),
        down_share,
        piece(mixed, 0),
        piece(mixed, 1),
        piece(mixed, 2),
        gain_share[0],
        gain_share[1],
        gain_share[2],
    )


def solution(mesh):
    weight = P(("batch", "slot"), None)
    gain = P(("batch", "slot"))
    rows = P(None, ("batch", "slot"), None)
    slots = P(None, "batch", "slot", None)
    return jax.shard_map(
        on_device,
        mesh=mesh,
        in_specs=(rows, slots, P(), P(None, "batch")) + (weight,) * 9 + (gain,) * 3 + (rows, slots),
        out_specs=(rows, slots, rows, slots) + (weight,) * 9 + (gain,) * 3,
        check_vma=False,
    )
```

```python
import functools

import jax
import jax.numpy as jnp
from jax import lax
from jax.experimental import pallas as pl
from jax.experimental.pallas import tpu as pltpu
from jax.sharding import PartitionSpec as P

HEADS = 8
HEAD_DIM = 64
SEG = 512
EPSILON = 1e-05
MASKED = -1e30
BF16 = jnp.bfloat16
F32 = jnp.float32
SCALE = HEAD_DIM ** (-0.5)
SMEM = pl.BlockSpec(memory_space=pltpu.SMEM)
VMEM = pl.BlockSpec(memory_space=pltpu.VMEM)
ANY = pl.BlockSpec(memory_space=pl.ANY)


def swap(value, axis, distance):
    pairs = [(i, i ^ distance) for i in range(lax.axis_size(axis))]
    return lax.ppermute(value, axis, pairs)


def own_bit(axis, distance):
    return (lax.axis_index(axis) // distance) % 2


def axis_bits(axis):
    return [(axis, 1 << i) for i in range(lax.axis_size(axis).bit_length() - 1)]


def exchange_orders(turn):
    rest = axis_bits("slot")[1:] + axis_bits("batch")
    if turn:
        rest = rest[2:3] + rest[:2] + rest[3:]
    other = list(rest)
    for i in range(0, len(rest) - 1, 2):
        other[i], other[i + 1] = rest[i + 1], rest[i]
    return rest, other


def lane_swap(value, orders, step):
    slots = lax.axis_size("slot")
    pairs = []
    for batch in range(lax.axis_size("batch")):
        for slot in range(slots):
            axis, distance = orders[slot % 2][step]
            to_batch, to_slot = batch, slot
            if axis == "batch":
                to_batch = batch ^ distance
            else:
                to_slot = slot ^ distance
            pairs.append((batch * slots + slot, to_batch * slots + to_slot))
    return lax.ppermute(value, ("batch", "slot"), pairs)


def lane_bit(orders, step):
    lane = own_bit("slot", 1)
    return jnp.where(lane == 0, own_bit(*orders[0][step]), own_bit(*orders[1][step]))


def chunk_places(order):
    natural = (axis_bits("slot")[1:] + axis_bits("batch"))
    count = len(order)
    places = []
    for pair in range(1 << count):
        place = 0
        for step, bit in enumerate(order):
            place |= ((pair >> natural.index(bit)) & 1) << (count - 1 - step)
        places.append(place)
    return places


def tie(value, after):
    return lax.optimization_barrier((value,) + tuple(after))[0] if after else value


class Gather:
    def __init__(self, held, turn, lows, left=None):
        self.turn, self.orders, self.lows = turn, exchange_orders(turn), lows
        self.left = len(self.orders[0]) if left is None else left
        self.held, self.got = held, None

    def launch(self, after=()):
        held = tie(self.held, after)
        if self.left == 0:
            self.got = swap(held, "slot", 1)
            return
        self.left -= 1
        self.got = lane_swap(held, self.orders, self.left)

    def finish(self, after=()):
        mine = self.lows[self.turn][self.left]
        got = tie(self.got, after)
        low = jnp.where(mine, self.held, got)
        high = jnp.where(mine, got, self.held)
        self.held = jnp.concatenate([low, high], 0)
        return self.held

    def until(self, left, after=()):
        while self.left > left:
            self.launch(after)
            self.finish()
        return self.held

    def unpack(self, sections, me, after=()):
        return unpack(self.held, self.got, self.turn, sections, me, after)


def place_kernel(places, sections, me_ref, held, got, *outs):
    for lane in range(2):

        @pl.when(me_ref[0] == lane)
        def _():
            sums = []
            for kind in range(2):
                source = held if kind == lane else got
                for pair, place in enumerate(places[kind]):
                    device = 2 * pair + kind
                    for (at, rows, lead), out in zip(sections, outs):
                        if lead == 0:
                            sums.append(source[place, at : at + rows, :].astype(F32))
                        for i in range(lead):
                            here = slice(device * rows, (device + 1) * rows)
                            out[i, here, :] = source[place, at + i * rows : at + (i + 1) * rows, :]
            if sums:
                outs[-1][...] = sum(sums[1:], sums[0])


def unpack(held, got, turn, sections, me, after):
    orders = exchange_orders(turn)
    places = [chunk_places(order) for order in orders]
    count, _, width = held.shape
    if all(rows % 16 == 0 for _, rows, lead in sections if lead):
        body = functools.partial(place_kernel, places, sections)
        outs = [
            like((lead, 2 * count * rows, width), BF16) if lead else like((rows, width), F32)
            for _, rows, lead in sections
        ]
        return kernel_call(
            body, [me, held, got], outs, 4, cost(0, 4 * held.size), "place", after
        )
    low = jnp.where(me[0] == 0, held, got)[jnp.array(places[0])]
    high = jnp.where(me[0] == 0, got, held)[jnp.array(places[1])]
    full = jnp.stack([low, high], 1).reshape(2 * count, -1, width)
    outs = []
    for at, rows, lead in sections:
        if lead == 0:
            outs.append(jnp.sum(full[:, at : at + rows].astype(F32), 0))
            continue
        part = full[:, at : at + rows * lead].reshape(2 * count, lead, rows, width)
        outs.append(part.transpose(1, 0, 2, 3).reshape(lead, -1, width))
    return outs


class Shares:
    def __init__(self, turn, sections, me, width, bits):
        self.turn, self.sections, self.me, self.width = turn, sections, me, width
        self.bits = bits[turn]
        self.rows = sum(rows * lead for _, rows, lead in sections)
        self.places = [chunk_places(order) for order in exchange_orders(turn)]
        self.count = len(self.places[0])
        self.direct = all(rows % 8 == 0 for _, rows, _ in sections)

    def shapes(self):
        if self.direct:
            return [like((self.count, self.rows, self.width), BF16)] * 2
        return [
            like((lead, 2 * self.count * rows, self.width), BF16)
            for _, rows, lead in self.sections
        ]

    def put(self, refs, me_ref, section, lead, first_row, value):
        at, rows, _ = self.sections[section]
        if not self.direct:
            refs[section][lead, first_row : first_row + value.shape[0], :] = value
            return
        keep, send = refs
        at = at + lead * rows
        for lane in range(2):

            @pl.when(me_ref[0] == lane)
            def _():
                for i in range(value.shape[0] // rows):
                    device = first_row // rows + i
                    target = keep if device % 2 == lane else send
                    place = self.places[device % 2][device // 2]
                    target[place, at : at + rows, :] = value[i * rows : (i + 1) * rows]

    def split(self, outs):
        if self.direct:
            return outs
        parts = []
        for (_, rows, lead), out in zip(self.sections, outs):
            part = out.reshape(lead, 2 * self.count, rows, self.width).transpose(1, 0, 2, 3)
            parts.append(part.reshape(2 * self.count, lead * rows, self.width))
        full = jnp.concatenate(parts, 1).reshape(self.count, 2, -1, self.width)
        back = []
        for kind in range(2):
            order = [0] * self.count
            for pair, place in enumerate(self.places[kind]):
                order[place] = pair
            back.append(full[:, kind][jnp.array(order)])
        lane = self.me[0]
        return [jnp.where(lane == 0, back[0], back[1]), jnp.where(lane == 0, back[1], back[0])]

    def begin(self, outs, after=()):
        self.orders = exchange_orders(self.turn)
        self.steps = len(self.orders[0])
        self.done, self.extra = 0, []
        self.keep, self.send = self.split(outs)
        self.got = swap(tie(self.send, after), "slot", 1)

    def join(self, outs, after=()):
        keep, send = outs
        got = swap(tie(send, after), "slot", 1)
        self.extra.append((keep, got))

    def finish(self, after=()):
        bit = self.bits[self.done]
        if self.extra:
            keep, got = self.extra.pop()
            self.keep, self.send = halve_two(
                self.keep, self.got, keep, got, bit, self.direct, after
            )
            return self.send
        self.keep, self.send = halve(self.keep, self.got, bit, self.direct, after)
        return self.send

    def launch(self, after=()):
        self.got = lane_swap(tie(self.send, after), self.orders, self.done)
        self.done += 1

    def end(self, after=()):
        return self.keep[0].astype(F32) + tie(self.got, after)[0].astype(F32)


def halve_two_kernel(bit, keep_a, got_a, keep_b, got_b, keep_out, send_out):
    rows = keep_a.shape[1]
    halve_kernel(bit, keep_a, got_a, keep_out.at[:, :rows], send_out.at[:, :rows])
    halve_kernel(bit, keep_b, got_b, keep_out.at[:, rows:], send_out.at[:, rows:])


def halve_two(keep_a, got_a, keep_b, got_b, bit, direct, after):
    if not direct:
        keep = jnp.concatenate([keep_a, keep_b], 1)
        return halve(keep, jnp.concatenate([got_a, got_b], 1), bit, direct, after)
    count, rows, width = keep_a.shape
    shape = (count // 2, rows + keep_b.shape[1], width)
    return kernel_call(
        halve_two_kernel,
        [bit, keep_a, got_a, keep_b, got_b],
        [like(shape, BF16)] * 2,
        4,
        cost(2 * keep_a.size, 12 * keep_a.size),
        "halve",
        after,
    )


def halve_kernel(bit, keep, got, keep_out, send_out):
    half = keep_out.shape[0]
    mine = pl.ds(bit[0] * half, half)
    other = pl.ds((1 - bit[0]) * half, half)
    send_out[...] = keep[other] + got[other]
    keep_out[...] = keep[mine] + got[mine]


def halve(keep, got, bit, direct, after):
    count, rows, width = keep.shape
    half = count // 2
    if direct:
        return kernel_call(
            halve_kernel,
            [bit, keep, got],
            [like((half, rows, width), BF16)] * 2,
            4,
            cost(keep.size, 6 * keep.size),
            "halve",
            after,
        )
    bit = bit[0]
    total = tie(keep, after) + got
    take = lambda b: lax.dynamic_slice_in_dim(total, b * half, half, 0)
    return take(bit), take(1 - bit)


def dot(a, b):
    return jnp.dot(a, b, preferred_element_type=F32)


def dot_nt(a, b):
    return lax.dot_general(a, b, (((1,), (1,)), ((), ())), preferred_element_type=F32)


def dot_tn(a, b):
    return lax.dot_general(a, b, (((0,), (0,)), ((), ())), preferred_element_type=F32)


def norm_parts(rows):
    centre = jnp.mean(rows, axis=-1, keepdims=True)
    centred = rows - centre
    spread = jnp.mean(centred * centred, axis=-1, keepdims=True)
    inverse = lax.rsqrt(spread + EPSILON)
    return centred * inverse, inverse


def norm_back(cot, hat, inverse, gain):
    d_hat = cot * gain
    first = jnp.mean(d_hat, axis=-1, keepdims=True)
    second = jnp.mean(d_hat * hat, axis=-1, keepdims=True)
    return inverse * (d_hat - first - hat * second)


def head_lanes(value, head):
    lane = lax.broadcasted_iota(jnp.int32, value.shape, 1)
    return jnp.where(lane // HEAD_DIM == head, value, jnp.zeros_like(value))


def head_rows(value, head):
    row = lax.broadcasted_iota(jnp.int32, value.shape, 0)
    return jnp.where(row // HEAD_DIM == head, value, jnp.zeros_like(value))


def both_heads(value):
    return jnp.concatenate([head_lanes(value, 0), head_lanes(value, 1)], 0)


def to_slot_lanes(value):
    turned = value.T
    return jnp.concatenate([turned[:HEAD_DIM], turned[HEAD_DIM:]], 1)


def to_slot_rows(value):
    turned = value.T
    half = turned.shape[0] // 2
    return jnp.concatenate([turned[:half], turned[half:]], 1)


def diagonal(value):
    lane = lax.broadcasted_iota(jnp.int32, (HEAD_DIM, value.shape[1]), 1)
    return jnp.where(lane < value.shape[1] // 2, value[:HEAD_DIM], value[HEAD_DIM:])


ROWS = 512


def row_loop(total):
    return lambda body: pl.loop(0, total // ROWS)(
        lambda i: body(pl.ds(pl.multiple_of(i * ROWS, ROWS), ROWS))
    )


def pair_loop(width):
    return lambda body: pl.loop(0, width // 128, unroll=2)(
        lambda p: body(p, pl.ds(pl.multiple_of(p * 128, 128), 128))
    )


def project_kernel(
    me_ref, tok, pair, other, gain, wq, wk, wv, normed, q, k, v, sk, sv, mem, mem_cot
):
    half = pair.shape[2]
    rows = half // 2
    for lane in range(2):

        @pl.when(me_ref[0] == lane)
        def _():
            for kind, out in enumerate((mem, mem_cot)):
                for m in range(pair.shape[1]):
                    for i in range(2):
                        for core in range(2):
                            source = pair if core == lane else other
                            at = 2 * (m * half + i * rows) + core * rows
                            block = source[kind, m, i * rows : (i + 1) * rows, :]
                            out[at : at + rows, :] = block

    @row_loop(tok.shape[0])
    def _(here):
        hat, _ = norm_parts(tok[here, :].astype(F32))
        low = (hat * gain[0:1, :]).astype(BF16)
        normed[here, :] = low
        q[here, :] = dot(low, wq[...]).astype(BF16)
        k[here, :] = dot(low, wk[...]).astype(BF16)
        v[here, :] = dot(low, wv[...]).astype(BF16)

    sk[...] = dot(mem[...], wk[...]).astype(BF16)
    sv[...] = dot(mem[...], wv[...]).astype(BF16)


def read_kernel(m, q, k, v, sk, sv, starts, keep, attended, out_t, inv, e_ref, bias):
    tok = attended.shape[0]
    slots = sk.shape[0] // keep.shape[0]
    key_at = lax.broadcasted_iota(jnp.int32, (tok, tok), 0)
    query_at = lax.broadcasted_iota(jnp.int32, (tok, tok), 1)
    start = starts[m, 0:1, :]
    kept = jnp.broadcast_to(keep[m, 0:1, :], (128, tok)).T
    kept = jnp.concatenate([kept] * (tok // 128), 1)
    good = (key_at >= start) & (key_at <= query_at) & (kept > 0)
    bias[...] = jnp.where(good, 0.0, MASKED)
    here, slot_here = pl.ds(m * tok, tok), pl.ds(m * slots, slots)

    @pair_loop(q.shape[1])
    def _(p, lanes):
        read_pair(
            q[here, lanes], k[here, lanes], v[here, lanes], sk[slot_here, lanes],
            sv[slot_here, lanes], bias, attended.at[:, lanes],
            out_t.at[pl.ds(pl.multiple_of(p * 128, 128), 128), :], inv.at[p], e_ref.at[p],
        )


def read_pair(q, keys, values, slot_keys, slot_values, bias, attended, out_t, inv, e_ref):
    tok = q.shape[0]
    half = tok // 2
    slots = slot_keys.shape[0]
    scaled = q * jnp.asarray(SCALE, BF16)
    values_t = values.T
    slot_values_t = slot_values.T
    outs, inverses = [], []
    for head in range(2):
        qm = head_lanes(scaled, head)
        rows = slice(head * HEAD_DIM, (head + 1) * HEAD_DIM)
        s_mem = dot_nt(slot_keys, qm)
        s_a = dot_nt(keys[:half], qm) + bias[:half, :]
        s_b = dot_nt(keys[half:], qm[half:]) + bias[half:, half:]
        top = jnp.maximum(jnp.max(s_mem, 0, keepdims=True), jnp.max(s_a, 0, keepdims=True))
        top_b = jnp.maximum(top[:, half:], jnp.max(s_b, 0, keepdims=True))
        top = jnp.concatenate([top[:, :half], top_b], 1)
        e_mem = jnp.exp(s_mem - top)
        e_a = jnp.exp(s_a - top)
        e_b = jnp.exp(s_b - top_b)
        total = jnp.sum(e_mem, 0, keepdims=True) + jnp.sum(e_a, 0, keepdims=True)
        total_b = total[:, half:] + jnp.sum(e_b, 0, keepdims=True)
        total = jnp.concatenate([total[:, :half], total_b], 1)
        e_mem, e_a, e_b = e_mem.astype(BF16), e_a.astype(BF16), e_b.astype(BF16)
        e_ref[head, :slots, :] = e_mem
        e_ref[head, slots : slots + half, :] = e_a
        e_ref[head, slots + half :, half:] = e_b
        e_ref[head, slots + half :, :half] = jnp.zeros((half, half), BF16)
        mix = dot(slot_values_t[rows], e_mem) + dot(values_t[rows, :half], e_a)
        mix_b = mix[:, half:] + dot(values_t[rows, half:], e_b)
        mix = jnp.concatenate([mix[:, :half], mix_b], 1)
        inverse = 1.0 / total
        outs.append(mix * inverse)
        inverses.append(inverse)
    out = jnp.concatenate(outs, 0)
    out_t[...] = out
    inv[...] = jnp.concatenate(inverses + [jnp.zeros((6, tok), F32)], 0)
    attended[...] = out.T.astype(BF16)


def write_kernel(mem, wsq, k, v, sk, keep, sq_ref, part):
    micro = keep.shape[0]
    tok = k.shape[0] // micro
    slots = mem.shape[0] // micro
    pairs = k.shape[1] // 128
    sq = dot(mem[...], wsq[...]).astype(BF16)
    sq_ref[...] = sq
    for m in range(micro):
        kept = jnp.broadcast_to(keep[m, 0:1, :], (128, tok)).T
        bias = jnp.where(kept > 0, 0.0, MASKED)
        for p in range(pairs):
            lanes = slice(p * 128, p * 128 + 128)
            mine = sq[m * slots : (m + 1) * slots, lanes]
            own = to_slot_lanes(
                mine.astype(F32) * sk[m * slots : (m + 1) * slots, lanes].astype(F32)
            )
            own = jnp.sum(own, 0, keepdims=True) * SCALE
            scores = dot_nt(k[m * tok : (m + 1) * tok, lanes], both_heads(mine)) * SCALE + bias
            top = jnp.maximum(jnp.max(scores, 0, keepdims=True), own)
            e = jnp.exp(scores - top)
            total = jnp.sum(e, 0, keepdims=True)
            mix = diagonal(dot_tn(v[m * tok : (m + 1) * tok, lanes], e.astype(BF16)))
            part[m, :HEAD_DIM, lanes] = mix
            part[m, HEAD_DIM:, lanes] = jnp.concatenate(
                [top, total, own, jnp.zeros((5, 128), F32)], 0
            )


def gelu_pair(hidden):
    root = 0.7978845608028654
    square = hidden * hidden
    bent = jnp.tanh(hidden * (root + (root * 0.044715) * square))
    half = 0.5 + 0.5 * bent
    slope = half + (0.5 * hidden) * (1.0 - bent * bent) * (root + (3.0 * root * 0.044715) * square)
    return (hidden * half).astype(BF16), slope


def ffn_cuts(low, cot_low, up, down, here, act_all, dh_all):
    width = low.shape[1]
    out = d_low = 0.0
    for cut in range(up.shape[0]):
        cols = slice(cut * width, (cut + 1) * width)
        act, slope = gelu_pair(dot(low, up[cut]))
        d_hidden = (dot_nt(cot_low, down[cols, :]) * slope).astype(BF16)
        act_all[here, cols] = act
        dh_all[here, cols] = d_hidden
        out = out + dot(act, down[cols, :])
        d_low = d_low + dot_nt(d_hidden, up[cut])
    return out, d_low


def ffn_grads(shares, refs, me_ref, base, low_all, cot_all, act_all, dh_all, cuts):
    width = low_all.shape[1]
    low_t = low_all[...].T
    for cut in range(cuts):
        cols = slice(cut * width, (cut + 1) * width)
        shares.put(refs, me_ref, base, cut, 0, dot(low_t, dh_all[:, cols]).astype(BF16))
        grad = dot_tn(act_all[:, cols], cot_all[...]).astype(BF16)
        shares.put(refs, me_ref, base + 1, 0, cut * width, grad)


def ffn_first_kernel(
    shares, me_ref, att_a, att_b, tok, cot, wout, up, down, gain,
    resid_ref, out_ref, d_low_ref, *rest
):
    refs, (act_all, dh_all, low_all) = rest[:-3], rest[-3:]
    count = att_a.shape[0]
    for m, att in enumerate((att_a, att_b)):

        @row_loop(count)
        def _(there):
            here = pl.ds(there.start + m * count, ROWS)
            resid = tok[here, :].astype(F32) + dot(att[there, :], wout[...])
            hat, _ = norm_parts(resid)
            low = (hat * gain[1:2, :]).astype(BF16)
            low_all[here, :] = low
            out, d_low = ffn_cuts(low, cot[here, :], up, down, here, act_all, dh_all)
            resid_ref[here, :] = resid
            out_ref[here, :] = resid + out
            d_low_ref[here, :] = d_low

    ffn_grads(shares, refs, me_ref, 0, low_all, cot, act_all, dh_all, up.shape[0])


def ffn_second_kernel(
    shares, me_ref, att_a, att_b, resid, part, d_part, cot, wout, up, down, gain,
    layer_out, d_resid_ref, da_a, da_b, g_gain, *rest
):
    refs, (act_all, dh_all, low_all, dattn_all) = rest[:-4], rest[-4:]
    count = att_a.shape[0]
    gain_row = gain[1:2, :]
    g_gain[...] = jnp.zeros_like(g_gain)
    for m, da_t in enumerate((da_a, da_b)):

        @row_loop(count)
        def _(there):
            here = pl.ds(there.start + m * count, ROWS)
            hat, inverse = norm_parts(resid[here, :])
            low = (hat * gain_row).astype(BF16)
            low_all[here, :] = low
            cot_low = cot[here, :]
            out, d_low = ffn_cuts(low, cot_low, up, down, here, act_all, dh_all)
            layer_out[here, :] = (part[here, :] + out).astype(BF16)
            d_low = d_part[here, :] + d_low
            d_resid = cot_low.astype(F32) + norm_back(d_low, hat, inverse, gain_row)
            d_resid_ref[here, :] = d_resid
            d_attn = d_resid.astype(BF16)
            dattn_all[here, :] = d_attn
            da_t[:, there] = dot_nt(wout[...], d_attn)
            g_gain[0:1, :] += jnp.sum(d_low * hat, 0, keepdims=True)

    ffn_grads(shares, refs, me_ref, 0, low_all, cot, act_all, dh_all, up.shape[0])
    grad = dot_tn(att_a[...], dattn_all[:count, :]) + dot_tn(att_b[...], dattn_all[count:, :])
    shares.put(refs, me_ref, 2, 0, 0, grad.astype(BF16))


def memory_kernel(
    shares, me_ref, slot_ref, part, mem, cot, sk, sv, sq, k, v, keep, wso, wfg, gain,
    new_ref, base, dsq_ref, osk, osv, wdk, wdv, g_gain, *rest
):
    refs, held = rest[:-1], rest[-1]
    micro = part.shape[0]
    slots = mem.shape[0] // micro
    own_rows = new_ref.shape[1]
    pairs = mem.shape[1] // 128
    row_at = lax.broadcasted_iota(jnp.int32, (mem.shape[0], 1), 0)
    mine = ((row_at % slots) // own_rows == slot_ref[0]).astype(F32)
    probs, tots, lses = [], [], []
    lines = []
    for m in range(micro):
        here = slice(m * slots, (m + 1) * slots)
        line, prob_line = [], []
        for p in range(pairs):
            lanes = slice(p * 128, p * 128 + 128)
            top0 = part[m, HEAD_DIM : HEAD_DIM + 1, lanes]
            total0 = part[m, HEAD_DIM + 1 : HEAD_DIM + 2, lanes]
            own = part[m, HEAD_DIM + 2 : HEAD_DIM + 3, lanes]
            top = jnp.maximum(top0, own)
            own_e = jnp.exp(own - top)
            shift = jnp.exp(top0 - top)
            total = total0 * shift + own_e
            inverse = 1.0 / total
            prob = own_e * inverse
            values = to_slot_lanes(sv[here, lanes].astype(F32))
            mixed = part[m, :HEAD_DIM, lanes] * (shift * inverse) + prob * values
            line.append(to_slot_rows(mixed))
            prob_line.append((prob, top + jnp.log(total)))
        lines.append(jnp.concatenate(line, 1))
        probs.append(prob_line)
    written = jnp.concatenate(lines, 0)
    written_low = written.astype(BF16)
    mem_low = mem[...]
    mem_f32 = mem_low.astype(F32)
    update = dot(written_low, wso[...])
    gate = 1.0 / (1.0 + jnp.exp(-dot(mem_low, wfg[...])))
    gain_row = gain[2:3, :]
    hat, inverse = norm_parts(gate * mem_f32 + (1.0 - gate) * update)
    held[...] = hat * gain_row
    cot_f32 = cot[...].astype(F32)
    for m in range(micro):
        at = pl.multiple_of(m * slots + slot_ref[0] * own_rows, own_rows)
        new_ref[m] = held[pl.ds(at, own_rows), :].astype(BF16)
    g_gain[...] = jnp.broadcast_to(jnp.sum(cot_f32 * hat * mine, 0, keepdims=True), g_gain.shape)
    d_blend = norm_back(cot_f32, hat, inverse, gain_row)
    d_pre = (d_blend * (mem_f32 - update) * gate * (1.0 - gate) * mine).astype(BF16)
    d_update = (d_blend * (1.0 - gate)).astype(BF16)
    mem_t = mem_low.T
    d_upd = (d_update.astype(F32) * mine).astype(BF16)
    shares.put(refs, me_ref, 1, 0, 0, dot_tn(written_low, d_upd).astype(BF16))
    shares.put(refs, me_ref, 2, 0, 0, dot(mem_t, d_pre).astype(BF16))
    base[...] = d_blend * gate * mine + dot_nt(d_pre, wfg[...])
    d_written = dot_nt(d_update, wso[...]).astype(BF16)
    dw_f32 = d_written.astype(F32)
    product = dw_f32 * written
    tok = k.shape[0] // micro
    for m in range(micro):
        here = slice(m * slots, (m + 1) * slots)
        there = slice(m * tok, (m + 1) * tok)
        kept = jnp.broadcast_to(keep[m, 0:1, :], (128, tok)).T
        bias = jnp.where(kept > 0, 0.0, MASKED)
        for p in range(pairs):
            lanes = slice(p * 128, p * 128 + 128)
            prob, lse = probs[m][p]
            values_f32 = sv[here, lanes].astype(F32)
            delta = jnp.sum(to_slot_lanes(product[here, lanes]), 0, keepdims=True)
            own_dp = jnp.sum(to_slot_lanes(dw_f32[here, lanes] * values_f32), 0, keepdims=True)
            own_ds = prob * (own_dp - delta)
            wide = lambda r: to_slot_rows(jnp.broadcast_to(r, (HEAD_DIM, 2 * slots)))
            own_ds = wide(own_ds) * mine[here] * SCALE
            own_p = wide(prob) * mine[here]
            sq_low = sq[here, lanes]
            sq_both = both_heads(sq_low * jnp.asarray(SCALE, BF16))
            dw_low = d_written[here, lanes]
            dw_both = both_heads(dw_low)
            keys, values = k[there, lanes], v[there, lanes]
            prob = jnp.exp(dot_nt(keys, sq_both) + bias - lse)
            d_score = (prob * (dot_nt(values, dw_both) - delta)).astype(BF16)
            wdk[there, lanes] = dot(d_score, sq_both).astype(BF16)
            wdv[there, lanes] = dot(prob.astype(BF16), dw_both).astype(BF16)
            d_read = to_slot_rows(diagonal(dot_tn(keys, d_score)))
            slot_keys = sk[here, lanes].astype(F32)
            dsq_ref[here, lanes] = (d_read * SCALE + own_ds * slot_keys).astype(BF16)
            osk[here, lanes] = own_ds * sq_low.astype(F32)
            osv[here, lanes] = own_p * dw_low.astype(F32)
    shares.put(refs, me_ref, 0, 0, 0, dot(mem_t, dsq_ref[...]).astype(BF16))


def back_kernel(
    m, q, k, v, sk, sv, da_t, out_t, inv, e_ref, wdk, wdv, osk, osv, dq, dk, dv, dsk, dsv
):
    tok, slots = dq.shape[0], dsk.shape[0]
    here, slot_here = pl.ds(m * tok, tok), pl.ds(m * slots, slots)

    @pair_loop(q.shape[1])
    def _(p, lanes):
        turned = pl.ds(pl.multiple_of(p * 128, 128), 128)
        back_pair(
            q[here, lanes], k[here, lanes], v[here, lanes], sk[slot_here, lanes],
            sv[slot_here, lanes], da_t.at[turned, :], out_t.at[turned, :], inv.at[p],
            e_ref.at[p], wdk.at[here, lanes], wdv.at[here, lanes], osk.at[slot_here, lanes],
            osv.at[slot_here, lanes], dq.at[:, lanes], dk.at[:, lanes], dv.at[:, lanes],
            dsk.at[:, lanes], dsv.at[:, lanes],
        )


def back_pair(
    q, keys, values, slot_keys, slot_values, da_t, out_t, inv, e_ref, wdk, wdv, osk, osv,
    dq, dk, dv, dsk, dsv,
):
    tok = q.shape[0]
    half = tok // 2
    slots = slot_keys.shape[0]
    scaled = q * jnp.asarray(SCALE, BF16)
    keys_t = keys.T
    slot_keys_t = slot_keys.T
    norm = jnp.concatenate(
        [jnp.broadcast_to(inv[i : i + 1, :], (HEAD_DIM, tok)) for i in range(2)], 0
    )
    da = (da_t[...] * norm).astype(BF16)
    product = da.astype(F32) * out_t[...]
    da_rows = da.T
    dq_parts = []
    dk_a = dk_b = dv_a = dv_b = dk_m = dv_m = 0.0
    for head in range(2):
        rows = slice(head * HEAD_DIM, (head + 1) * HEAD_DIM)
        qm = head_lanes(scaled, head)
        dam_t = head_rows(da, head)
        dam = head_lanes(da_rows, head)
        delta = jnp.sum(product[rows], 0, keepdims=True)
        e_mem = e_ref[head, :slots, :]
        e_a = e_ref[head, slots : slots + half, :]
        e_b = e_ref[head, slots + half :, half:]
        ds_mem = (e_mem.astype(F32) * (dot(slot_values, dam_t) - delta)).astype(BF16)
        ds_a = (e_a.astype(F32) * (dot(values[:half], dam_t) - delta)).astype(BF16)
        ds_b = (
            e_b.astype(F32) * (dot(values[half:], dam_t[:, half:]) - delta[:, half:])
        ).astype(BF16)
        part = dot(slot_keys_t[rows], ds_mem) + dot(keys_t[rows, :half], ds_a)
        part_b = part[:, half:] + dot(keys_t[rows, half:], ds_b)
        dq_parts.append(jnp.concatenate([part[:, :half], part_b], 1))
        dk_a = dk_a + dot(ds_a, qm)
        dk_b = dk_b + dot(ds_b, qm[half:])
        dk_m = dk_m + dot(ds_mem, qm)
        dv_a = dv_a + dot(e_a, dam)
        dv_b = dv_b + dot(e_b, dam[half:])
        dv_m = dv_m + dot(e_mem, dam)
    dq[...] = (jnp.concatenate(dq_parts, 0) * SCALE).T.astype(BF16)

    dk[:half, :] = (dk_a + wdk[:half, :].astype(F32)).astype(BF16)
    dk[half:, :] = (dk_b + wdk[half:, :].astype(F32)).astype(BF16)
    dv[:half, :] = (dv_a + wdv[:half, :].astype(F32)).astype(BF16)
    dv[half:, :] = (dv_b + wdv[half:, :].astype(F32)).astype(BF16)
    dsk[...] = (dk_m + osk[...]).astype(BF16)
    dsv[...] = (dv_m + osv[...]).astype(BF16)


def grads_kernel(
    shares, me_ref, normed, dq_a, dk_a, dv_a, dsk_a, dsv_a, dq_b, dk_b, dv_b, dsk_b, dsv_b,
    mem, wq, wk, wv, gain, g_ffn, g_mem, *refs
):
    count = dq_a.shape[0]
    slots = dsk_a.shape[0]
    rows_t = normed[...].T
    mem_t = mem[...].T
    weighted = 0.0
    sets = (
        (dq_a, dq_b, wq, None, None),
        (dk_a, dk_b, wk, dsk_a, dsk_b),
        (dv_a, dv_b, wv, dsv_a, dsv_b),
    )
    for i, (cot_a, cot_b, weight, slot_a, slot_b) in enumerate(sets):
        grad = dot(rows_t[:, :count], cot_a[...]) + dot(rows_t[:, count:], cot_b[...])
        weighted = weighted + grad * weight[...].astype(F32)
        if slot_a is not None:
            slot_cot = jnp.concatenate([slot_a[...], slot_b[...]], 0)
            grad = grad + dot(mem_t, slot_cot)
        shares.put(refs, me_ref, i, 0, 0, grad.astype(BF16))
    folded = weighted[:, :128]
    for i in range(1, weighted.shape[1] // 128):
        folded = folded + weighted[:, i * 128 : (i + 1) * 128]
    line = jnp.sum(folded.T, 0, keepdims=True) / gain[0:1, :]
    lines = [line, g_ffn[0:1, :], g_mem[0:1, :]]
    extra = shares.sections[3][1]
    lines = jnp.concatenate(lines + [jnp.zeros((extra - 3, line.shape[1]), F32)], 0)
    lines = lines.astype(BF16)
    for device in range(2 * shares.count):
        shares.put(refs, me_ref, 3, 0, device * extra, lines)


def input_kernel(
    me_ref, tok, d_resid,
    dq_a, dk_a, dv_a, dsk_a, dsv_a, dq_b, dk_b, dv_b, dsk_b, dsv_b, dsq, base,
    wq, wk, wv, wsq, gain, tok_grad, mem_keep, mem_send, d_mem
):
    count = dq_a.shape[0]
    for m, (dq, dk, dv) in enumerate(((dq_a, dk_a, dv_a), (dq_b, dk_b, dv_b))):

        @row_loop(count)
        def _(there):
            here = pl.ds(there.start + m * count, ROWS)
            hat, inverse = norm_parts(tok[here, :].astype(F32))
            d_normed = dot_nt(dq[there, :], wq[...]) + dot_nt(dk[there, :], wk[...])
            d_normed = d_normed + dot_nt(dv[there, :], wv[...])
            back = norm_back(d_normed, hat, inverse, gain[0:1, :])
            tok_grad[here, :] = (d_resid[here, :] + back).astype(BF16)

    d_mem[...] = (
        base[...]
        + dot_nt(dsq[...], wsq[...])
        + dot_nt(jnp.concatenate([dsk_a[...], dsk_b[...]], 0), wk[...])
        + dot_nt(jnp.concatenate([dsv_a[...], dsv_b[...]], 0), wv[...])
    )
    micro, half, _ = mem_keep.shape
    slots = 2 * half
    rows = slots // 4
    for m in range(micro):
        for i in range(2):
            at = m * slots + 2 * i * rows
            mine = pl.ds(pl.multiple_of(at + me_ref[0] * rows, rows), rows)
            other = pl.ds(pl.multiple_of(at + (1 - me_ref[0]) * rows, rows), rows)
            mem_keep[m, i * rows : (i + 1) * rows, :] = d_mem[mine, :]
            mem_send[m, i * rows : (i + 1) * rows, :] = d_mem[other, :]


def split_kernel(bit, held, got, keep_out, send_out):
    half = keep_out.shape[1]
    mine = bit[0]
    for m in range(held.shape[0]):
        own = pl.ds(pl.multiple_of(mine * half, half), half)
        other = pl.ds(pl.multiple_of((1 - mine) * half, half), half)
        keep_out[m] = held[m, own, :] + got[m, own, :]
        send_out[m] = held[m, other, :] + got[m, other, :]


def kernel_call(
    body, args, out_shape, mib, price, name, after=(), scalars=1, scratch_shapes=(), far=None
):
    count = len(args)

    def run(*refs):
        body(*refs[:count], *refs[count + len(after) :])

    in_specs = [SMEM] * scalars + [VMEM] * (count - scalars) + [ANY] * len(after)
    out_specs = [VMEM] * len(out_shape)
    args, out_shape = list(args), list(out_shape)
    if far is not None and far < count:
        in_specs[far] = ANY
        args[far] = pltpu.with_memory_space_constraint(args[far], pltpu.HBM)
    elif far is not None:
        out_specs[far - count] = ANY
        out_shape[far - count] = pltpu.HBM(
            out_shape[far - count].shape, out_shape[far - count].dtype
        )
    return pl.pallas_call(
        run,
        in_specs=in_specs,
        out_specs=out_specs,
        out_shape=out_shape,
        scratch_shapes=scratch_shapes,
        compiler_params=pltpu.CompilerParams(vmem_limit_bytes=int(mib * (1 << 20))),
        cost_estimate=price,
        name=name,
    )(*args, *after)


def like(shape, dtype):
    return jax.ShapeDtypeStruct(shape, dtype)


def cost(flops, nbytes, trans=0):
    return pl.CostEstimate(flops=flops, bytes_accessed=nbytes, transcendentals=trans)


def on_device(
    tokens,
    memory,
    doc_lengths,
    key_mask,
    w_query,
    w_key,
    w_value,
    w_out,
    w_up,
    w_down,
    w_slot_query,
    w_slot_out,
    w_forget,
    norm_gain,
    ffn_gain,
    memory_gain,
    out_grad,
    memory_grad,
):
    slot_count = lax.axis_size("slot")
    slot_index = lax.axis_index("slot")
    device_count = lax.axis_size("batch") * slot_count
    device = lax.axis_index("batch") * slot_count + slot_index
    micro, tok_dev, width = tokens.shape
    slot_rows = memory.shape[2]
    slots = slot_rows * slot_count
    group_tok = tok_dev * slot_count
    dev_start = slot_index * tok_dev
    rows = w_query.shape[0]
    ff = w_up.shape[1]
    pairs = width // 128
    total = micro * tok_dev
    mem_rows = micro * slots
    keys = tok_dev + slots
    down_rows = w_down.shape[0]
    part_rows = down_rows // 2
    cuts = ff // 2 // width
    extra = 8
    lane_at = jnp.arange(width, dtype=jnp.int32) // rows
    pick = jnp.arange(width)[:, None] == device * rows + jnp.arange(rows)[None, :]
    pick = pick.astype(F32)
    keep = lax.dynamic_slice_in_dim(key_mask, dev_start, tok_dev, 1).astype(F32)
    keep = jnp.broadcast_to(keep[:, None, :], (micro, 8, tok_dev))
    segment = lax.axis_index("batch") * group_tok + dev_start
    positions = segment + jnp.arange(tok_dev, dtype=jnp.int32)
    doc_ends = jnp.cumsum(doc_lengths, axis=1, dtype=jnp.int32)
    passed = positions[None, None, :] >= doc_ends[:, :, None]
    starts = jnp.max(jnp.where(passed, doc_ends[:, :, None] - segment, 0), axis=1)
    starts = jnp.broadcast_to(starts[:, None, :], (micro, 8, tok_dev))
    bits = []
    for turn in range(2):
        orders = exchange_orders(turn)
        bits += [lane_bit(orders, step) for step in range(len(orders[0]))]
    scalars = [own_bit("slot", 1), slot_index, own_bit("slot", 2)] + bits
    scalars = [jnp.asarray(entry, jnp.int32) for entry in scalars]
    small = (keep, starts, pick, tuple(scalars), tuple(entry == 0 for entry in scalars))
    keep, starts, pick, scalars, lows = lax.optimization_barrier(small)
    me, slot_scalar, slot_high, *bits = (entry.reshape(1) for entry in scalars)
    slot_low, lows = lows[2], lows[3:]
    half = len(bits) // 2
    lows, bits = (lows[:half], lows[half:]), (bits[:half], bits[half:])
    gain_rows = jnp.stack([norm_gain, ffn_gain, memory_gain])
    gain_rows = jnp.where(lane_at == device, jnp.tile(gain_rows, (1, device_count)), 0)
    gain_rows = jnp.pad(gain_rows.astype(BF16), ((0, extra - 3), (0, 0)))
    first = Gather(jnp.concatenate([w_query, w_key, w_value, gain_rows])[None], 0, lows)
    marks = [first.until(3)]
    raw = [w_slot_query, w_slot_out, w_forget, w_out, w_up, w_down]
    raw = lax.optimization_barrier(tuple(raw) + (marks[0],))
    w_up, w_down = raw[4], raw[5]
    up_parts = w_up.reshape(rows, device_count, 2, part_rows).transpose(2, 0, 1, 3)
    up_parts = up_parts.reshape(2, rows, cuts, width).transpose(0, 2, 1, 3)
    up_parts = up_parts.reshape(2, cuts * rows, width)
    rest = list(raw[:4])
    rest += [up_parts[0], w_down[:part_rows]]
    rest = Gather(jnp.concatenate(rest)[None], 0, lows)
    fourth = Gather(jnp.concatenate([up_parts[1], w_down[part_rows:]])[None], 1, lows)
    first.launch()
    marks.append(first.finish([rest.held]))
    marks.append(rest.until(3))
    first.launch()
    pair = tie(jnp.stack([memory[:, 0], memory_grad[:, 0]]), marks[1:2])
    other = swap(pair, "slot", 2)
    marks.append(first.finish())
    other = tie(other, marks[3:])
    low, high = jnp.where(slot_low, pair, other), jnp.where(slot_low, other, pair)
    pair = jnp.concatenate([low, high], 2)
    first.launch([marks[2], pair])
    rest.launch(marks[3:])
    fourth.until(4, marks[3:])
    fourth.launch(marks[3:])
    other = swap(pair, "slot", 1)
    first.finish()
    rest.finish([first.held])
    fourth.finish([first.held])
    first.launch([rest.held, fourth.held])
    fourth.launch()
    second, third = [
        Gather(rest.held[:, part], 0, lows, rest.left)
        for part in (slice(0, 4 * rows), slice(4 * rows, None))
    ]
    second.launch()

    one = [(i * rows, rows, 1) for i in range(4)]
    w_query, w_key, w_value, gains = first.unpack(one[:3] + [(3 * rows, extra, 0)], me)
    w_query, w_key, w_value = w_query[0], w_key[0], w_value[0]

    tok_flat = tokens.reshape(total, width)
    cot_flat = out_grad.reshape(total, width)
    low = lambda n, w: like((n, w), BF16)

    wide = like((total, width), F32)
    slot_like = low(mem_rows, width)
    slot_wide = like((mem_rows, width), F32)
    (
        normed, queries, tok_keys, tok_values, slot_keys, slot_values, mem_low, mem_cot
    ) = kernel_call(
        project_kernel,
        [me, tok_flat, pair, other, gains, w_query, w_key, w_value],
        [low(total, width)] * 4 + [slot_like] * 4,
        6,
        cost(6 * total * width * width, 8 << 20),
        "project",
        after=[rest.held],
    )
    second.finish([normed])
    fourth.finish([normed])
    third.launch([second.held, fourth.held])
    second.launch([second.held, fourth.held])
    fourth.launch([second.held, fourth.held])

    square = low(tok_dev, width)
    reads = []
    for m in range(micro):
        reads.append(
            kernel_call(
                functools.partial(read_kernel, m),
                [queries, tok_keys, tok_values, slot_keys, slot_values, starts, keep],
                [
                    square,
                    like((width, tok_dev), F32),
                    like((pairs, 8, tok_dev), F32),
                    like((pairs, 2, keys, tok_dev), BF16),
                ],
                6,
                cost(16 * total * width * keys // micro, 8 << 20, total * keys * HEADS // micro),
                "read",
                scalars=0,
                after=(second.held,) if m == 0 else (third.held,),
                scratch_shapes=[pltpu.VMEM((tok_dev, tok_dev), F32)],
            )
        )
        if m == 0:
            third.finish([reads[0][0]])
            second.finish([reads[0][0]])
            fourth.finish([reads[0][0]])
            ready = [second.held, third.held, fourth.held]
            third.launch(ready)
            second.launch(ready)
            fourth.launch(ready)
    attended = [kept[0] for kept in reads]

    second_mats = second.unpack(one, me, [attended[1]])
    w_slot_query, w_slot_out, w_forget, w_out = (m[0] for m in second_mats)
    third.finish([attended[1]])
    third.launch([w_slot_query, third.held])
    ffn_sections = [(0, rows, cuts), (cuts * rows, part_rows, 1)]
    up_first, down_first = third.unpack(ffn_sections, me)
    slot_queries, part = kernel_call(
        write_kernel,
        [mem_low, w_slot_query, tok_keys, tok_values, slot_keys, keep],
        [slot_like, like((micro, 72, slots * HEADS), F32)],
        3,
        cost(8 * total * width * slots, 5 << 20, total * slots * HEADS),
        "write",
        scalars=0,
        after=[third.held],
    )

    def merged(part, other):
        top_a, top_b = part[:, 64:65], other[:, 64:65]
        top = jnp.maximum(top_a, top_b)
        scale_a, scale_b = jnp.exp(top_a - top), jnp.exp(top_b - top)
        mix = part[:, :64] * scale_a + other[:, :64] * scale_b
        tot = part[:, 65:66] * scale_a + other[:, 65:66] * scale_b
        return jnp.concatenate([mix, top, tot, part[:, 66:]], 1)

    part = merged(part, swap(part, "slot", 1))
    other = swap(part, "slot", 2)

    half_cost = cost(7 * total * width * ff, 14 << 20, total * ff // 2)
    tall = [pltpu.VMEM((total, ff // 2), BF16)] * 2 + [pltpu.VMEM((total, width), BF16)]
    sums_first = Shares(0, ffn_sections, me, width, bits)
    resid, out_part, d_low, *outs = kernel_call(
        functools.partial(ffn_first_kernel, sums_first),
        [me, *attended, tok_flat, cot_flat, w_out, up_first, down_first[0], gains],
        [wide] * 3 + sums_first.shapes(),
        13,
        half_cost,
        "ffn_first",
        scratch_shapes=tall,
        after=[part],
    )
    part = merged(part, tie(other, [resid]))
    fourth.finish([resid])
    sums_first.begin(outs, [part, fourth.held])
    fourth.launch([part])

    sums_slot = Shares(0, one[:3], me, width, bits)
    new_memory, base, d_sq, own_sk, own_sv, w_dk, w_dv, g_mem, *outs = kernel_call(
        functools.partial(memory_kernel, sums_slot),
        [me, slot_scalar, part, mem_low, mem_cot, slot_keys, slot_values, slot_queries]
        + [tok_keys, tok_values, keep, w_slot_out, w_forget, gains],
        [like((micro, slot_rows, width), BF16), slot_wide]
        + [slot_like]
        + [slot_wide] * 2
        + [low(total, width)] * 2
        + [like((8, width), F32)]
        + sums_slot.shapes(),
        4,
        cost(12 * mem_rows * width * width + 12 * total * width * slots, 8 << 20),
        "memory",
        scalars=2,
        scratch_shapes=[pltpu.VMEM((mem_rows, width), F32)],
        after=[resid, fourth.held],
    )
    sums_first.join(sums_slot.split(outs))
    up_second, down_second = fourth.unpack(ffn_sections, me, [base])
    sums_first.finish([up_second])
    sums_first.launch()

    sections = [(0, rows, cuts), (cuts * rows, part_rows, 1)]
    sections += [(cuts * rows + part_rows, rows, 1)]
    sums_second = Shares(0, sections, me, width, bits)
    turned = like((width, tok_dev), F32)
    layer_out, d_resid, da_a, da_b, g_ffn, *outs = kernel_call(
        functools.partial(ffn_second_kernel, sums_second),
        [me, *attended, resid, out_part, d_low, cot_flat, w_out, up_second, down_second[0], gains],
        [low(total, width), wide, turned, turned, like((8, width), F32)] + sums_second.shapes(),
        17,
        half_cost,
        "ffn_second",
        scratch_shapes=tall + [pltpu.VMEM((total, width), BF16)],
        after=[sums_first.send],
    )
    sums_first.finish([d_resid])
    sums_second.begin(outs, [sums_first.send])
    sums_first.launch()
    back = []
    for m, da_t in enumerate((da_a, da_b)):
        found = kernel_call(
            functools.partial(back_kernel, m),
            [queries, tok_keys, tok_values, slot_keys, slot_values]
            + [da_t, *reads[m][1:], w_dk, w_dv, own_sk, own_sv],
            [square] * 3 + [low(slots, width)] * 2,
            6,
            cost(24 * total * width * keys // micro, 10 << 20),
            "back",
            scalars=0,
            after=[sums_first.send] + ([sums_second.send] if m else []),
        )
        back += found
        if m == 0:
            sums_second.finish([found[0]])
            sums_first.finish([found[0]])
            sums_second.launch([sums_first.send])
            sums_first.launch([sums_second.send])

    sums_third = Shares(0, one[:3] + [(3 * rows, extra, 1)], me, width, bits)
    outs = kernel_call(
        functools.partial(grads_kernel, sums_third),
        [me, normed, *back, mem_low, w_query, w_key, w_value, gains, g_ffn, g_mem],
        sums_third.shapes(),
        8,
        cost(6 * total * width * width, 8 << 20),
        "grads",
        after=[sums_first.send],
    )
    sums_second.finish(outs[:1])
    sums_first.finish(outs[:1])
    sums_third.begin(outs, [sums_second.send, sums_first.send])
    sums_second.launch([sums_first.send])
    sums_first.launch([sums_second.send])
    sums_third.finish([sums_first.send])
    sums_third.launch()
    tokens_grad, mem_keep, mem_send = kernel_call(
        input_kernel,
        [me, tok_flat, d_resid, *back, d_sq, base, w_query, w_key, w_value, w_slot_query, gains],
        [low(total, width)] + [like((micro, slots // 2, width), F32)] * 2,
        10,
        cost(6 * total * width * width, 12 << 20),
        "input",
        after=[sums_third.send],
        scratch_shapes=[pltpu.VMEM((mem_rows, width), F32)],
    )
    piece = lambda m, i: m[i * rows : (i + 1) * rows]

    def up_piece(m, at):
        return m[at : at + cuts * rows].reshape(cuts, rows, width).transpose(1, 0, 2).reshape(
            rows, device_count, 1, part_rows
        )

    sums_second.finish([mem_keep])
    sums_third.finish([sums_second.send])
    sums_third.launch()
    sums_second.launch([sums_third.send])
    both = [sums_second.send, sums_third.send]
    got = swap(tie(mem_send, both), "slot", 1)
    while sums_first.done < sums_first.steps:
        sums_first.finish()
        sums_first.launch()
    total_first = sums_first.end(both)
    sums_third.finish([total_first, sums_second.send])
    sums_third.launch()
    sums_second.finish([sums_third.send])
    sums_second.launch()
    held, sent = kernel_call(
        split_kernel,
        [slot_high, mem_keep, got],
        [like((micro, slot_rows, width), F32)] * 2,
        2,
        cost(mem_keep.size, 8 * mem_keep.size),
        "split",
        after=[sums_second.send],
    )
    got = swap(sent, "slot", 2)
    while sums_second.done < sums_second.steps:
        sums_second.finish()
        sums_second.launch()
    sums_third.finish([sums_second.send, held])
    sums_third.launch()
    total_second = sums_second.end([sums_third.send])
    moved = held + tie(got, [sums_third.send])
    total_first, total_second = lax.optimization_barrier(
        (total_first, total_second, sums_third.send)
    )[:2]
    up_share = jnp.concatenate([up_piece(total_first, 0), up_piece(total_second, 0)], 2)
    down_at = cuts * rows
    down_share = jnp.concatenate(
        [m[down_at : down_at + part_rows] for m in (total_first, total_second)]
    )
    mixed = total_first[down_at + part_rows :]
    while sums_third.done < sums_third.steps:
        sums_third.finish()
        sums_third.launch()
    sums_third = sums_third.end()
    gain_share = jnp.dot(
        sums_third[3 * rows : 3 * rows + 3], pick, precision=lax.Precision.HIGHEST
    )
    return (
        layer_out.reshape(micro, tok_dev, width),
        new_memory[:, None],
        tokens_grad.reshape(micro, tok_dev, width),
        moved.astype(BF16)[:, None],
        piece(sums_third, 0),
        piece(sums_third, 1),
        piece(sums_third, 2),
        total_second[down_at + part_rows :],
        up_share.reshape(rows, ff),
        down_share,
        piece(mixed, 0),
        piece(mixed, 1),
        piece(mixed, 2),
        gain_share[0],
        gain_share[1],
        gain_share[2],
    )


def solution(mesh):
    weight = P(("batch", "slot"), None)
    gain = P(("batch", "slot"))
    rows = P(None, ("batch", "slot"), None)
    slots = P(None, "batch", "slot", None)
    return jax.shard_map(
        on_device,
        mesh=mesh,
        in_specs=(rows, slots, P(), P(None, "batch")) + (weight,) * 9 + (gain,) * 3 + (rows, slots),
        out_specs=(rows, slots, rows, slots) + (weight,) * 9 + (gain,) * 3,
        check_vma=False,
    )
```

```python
import functools

import jax
import jax.numpy as jnp
from jax import lax
from jax.experimental import pallas as pl
from jax.experimental.pallas import tpu as pltpu
from jax.sharding import PartitionSpec as P

HEADS = 8
HEAD_DIM = 64
SEG = 512
EPSILON = 1e-05
MASKED = -1e30
BF16 = jnp.bfloat16
F32 = jnp.float32
SCALE = HEAD_DIM ** (-0.5)
SMEM = pl.BlockSpec(memory_space=pltpu.SMEM)
VMEM = pl.BlockSpec(memory_space=pltpu.VMEM)
ANY = pl.BlockSpec(memory_space=pl.ANY)


def swap(value, axis, distance):
    pairs = [(i, i ^ distance) for i in range(lax.axis_size(axis))]
    return lax.ppermute(value, axis, pairs)


def own_bit(axis, distance):
    return (lax.axis_index(axis) // distance) % 2


def axis_bits(axis):
    return [(axis, 1 << i) for i in range(lax.axis_size(axis).bit_length() - 1)]


def exchange_orders(turn):
    rest = axis_bits("slot")[1:] + axis_bits("batch")
    if turn:
        rest = rest[2:3] + rest[:2] + rest[3:]
    other = list(rest)
    for i in range(0, len(rest) - 1, 2):
        other[i], other[i + 1] = rest[i + 1], rest[i]
    return rest, other


def lane_swap(value, orders, step):
    slots = lax.axis_size("slot")
    pairs = []
    for batch in range(lax.axis_size("batch")):
        for slot in range(slots):
            axis, distance = orders[slot % 2][step]
            to_batch, to_slot = batch, slot
            if axis == "batch":
                to_batch = batch ^ distance
            else:
                to_slot = slot ^ distance
            pairs.append((batch * slots + slot, to_batch * slots + to_slot))
    return lax.ppermute(value, ("batch", "slot"), pairs)


def lane_bit(orders, step):
    lane = own_bit("slot", 1)
    return jnp.where(lane == 0, own_bit(*orders[0][step]), own_bit(*orders[1][step]))


def chunk_places(order):
    natural = (axis_bits("slot")[1:] + axis_bits("batch"))
    count = len(order)
    places = []
    for pair in range(1 << count):
        place = 0
        for step, bit in enumerate(order):
            place |= ((pair >> natural.index(bit)) & 1) << (count - 1 - step)
        places.append(place)
    return places


def tie(value, after):
    return lax.optimization_barrier((value,) + tuple(after))[0] if after else value


class Gather:
    def __init__(self, held, turn, lows, left=None):
        self.turn, self.orders, self.lows = turn, exchange_orders(turn), lows
        self.left = len(self.orders[0]) if left is None else left
        self.held, self.got = held, None

    def launch(self, after=()):
        held = tie(self.held, after)
        if self.left == 0:
            self.got = swap(held, "slot", 1)
            return
        self.left -= 1
        self.got = lane_swap(held, self.orders, self.left)

    def finish(self, after=()):
        mine = self.lows[self.turn][self.left]
        got = tie(self.got, after)
        low = jnp.where(mine, self.held, got)
        high = jnp.where(mine, got, self.held)
        self.held = jnp.concatenate([low, high], 0)
        return self.held

    def until(self, left, after=()):
        while self.left > left:
            self.launch(after)
            self.finish()
        return self.held

    def unpack(self, sections, me, after=()):
        return unpack(self.held, self.got, self.turn, sections, me, after)


def place_kernel(places, sections, me_ref, held, got, *outs):
    for lane in range(2):

        @pl.when(me_ref[0] == lane)
        def _():
            sums = []
            for kind in range(2):
                source = held if kind == lane else got
                for pair, place in enumerate(places[kind]):
                    device = 2 * pair + kind
                    for (at, rows, lead), out in zip(sections, outs):
                        if lead == 0:
                            sums.append(source[place, at : at + rows, :].astype(F32))
                        for i in range(lead):
                            here = slice(device * rows, (device + 1) * rows)
                            out[i, here, :] = source[place, at + i * rows : at + (i + 1) * rows, :]
            if sums:
                outs[-1][...] = sum(sums[1:], sums[0])


def unpack(held, got, turn, sections, me, after):
    orders = exchange_orders(turn)
    places = [chunk_places(order) for order in orders]
    count, _, width = held.shape
    if all(rows % 16 == 0 for _, rows, lead in sections if lead):
        body = functools.partial(place_kernel, places, sections)
        outs = [
            like((lead, 2 * count * rows, width), BF16) if lead else like((rows, width), F32)
            for _, rows, lead in sections
        ]
        return kernel_call(
            body, [me, held, got], outs, 4, cost(0, 4 * held.size), "place", after
        )
    low = jnp.where(me[0] == 0, held, got)[jnp.array(places[0])]
    high = jnp.where(me[0] == 0, got, held)[jnp.array(places[1])]
    full = jnp.stack([low, high], 1).reshape(2 * count, -1, width)
    outs = []
    for at, rows, lead in sections:
        if lead == 0:
            outs.append(jnp.sum(full[:, at : at + rows].astype(F32), 0))
            continue
        part = full[:, at : at + rows * lead].reshape(2 * count, lead, rows, width)
        outs.append(part.transpose(1, 0, 2, 3).reshape(lead, -1, width))
    return outs


class Shares:
    def __init__(self, turn, sections, me, width, bits):
        self.turn, self.sections, self.me, self.width = turn, sections, me, width
        self.bits = bits[turn]
        self.rows = sum(rows * lead for _, rows, lead in sections)
        self.places = [chunk_places(order) for order in exchange_orders(turn)]
        self.count = len(self.places[0])
        self.direct = all(rows % 8 == 0 for _, rows, _ in sections)

    def shapes(self):
        if self.direct:
            return [like((self.count, self.rows, self.width), BF16)] * 2
        return [
            like((lead, 2 * self.count * rows, self.width), BF16)
            for _, rows, lead in self.sections
        ]

    def put(self, refs, me_ref, section, lead, first_row, value):
        at, rows, _ = self.sections[section]
        if not self.direct:
            refs[section][lead, first_row : first_row + value.shape[0], :] = value
            return
        keep, send = refs
        at = at + lead * rows
        for lane in range(2):

            @pl.when(me_ref[0] == lane)
            def _():
                for i in range(value.shape[0] // rows):
                    device = first_row // rows + i
                    target = keep if device % 2 == lane else send
                    place = self.places[device % 2][device // 2]
                    target[place, at : at + rows, :] = value[i * rows : (i + 1) * rows]

    def split(self, outs):
        if self.direct:
            return outs
        parts = []
        for (_, rows, lead), out in zip(self.sections, outs):
            part = out.reshape(lead, 2 * self.count, rows, self.width).transpose(1, 0, 2, 3)
            parts.append(part.reshape(2 * self.count, lead * rows, self.width))
        full = jnp.concatenate(parts, 1).reshape(self.count, 2, -1, self.width)
        back = []
        for kind in range(2):
            order = [0] * self.count
            for pair, place in enumerate(self.places[kind]):
                order[place] = pair
            back.append(full[:, kind][jnp.array(order)])
        lane = self.me[0]
        return [jnp.where(lane == 0, back[0], back[1]), jnp.where(lane == 0, back[1], back[0])]

    def begin(self, outs, after=()):
        self.orders = exchange_orders(self.turn)
        self.steps = len(self.orders[0])
        self.done, self.extra = 0, []
        self.keep, self.send = self.split(outs)
        self.got = swap(tie(self.send, after), "slot", 1)

    def join(self, outs, after=()):
        keep, send = outs
        got = swap(tie(send, after), "slot", 1)
        self.extra.append((keep, got))

    def finish(self, after=()):
        bit = self.bits[self.done]
        if self.extra:
            keep, got = self.extra.pop()
            self.keep, self.send = halve_two(
                self.keep, self.got, keep, got, bit, self.direct, after
            )
            return self.send
        self.keep, self.send = halve(self.keep, self.got, bit, self.direct, after)
        return self.send

    def launch(self, after=()):
        self.got = lane_swap(tie(self.send, after), self.orders, self.done)
        self.done += 1

    def end(self, after=()):
        return self.keep[0].astype(F32) + tie(self.got, after)[0].astype(F32)


def halve_two_kernel(bit, keep_a, got_a, keep_b, got_b, keep_out, send_out):
    rows = keep_a.shape[1]
    halve_kernel(bit, keep_a, got_a, keep_out.at[:, :rows], send_out.at[:, :rows])
    halve_kernel(bit, keep_b, got_b, keep_out.at[:, rows:], send_out.at[:, rows:])


def halve_two(keep_a, got_a, keep_b, got_b, bit, direct, after):
    if not direct:
        keep = jnp.concatenate([keep_a, keep_b], 1)
        return halve(keep, jnp.concatenate([got_a, got_b], 1), bit, direct, after)
    count, rows, width = keep_a.shape
    shape = (count // 2, rows + keep_b.shape[1], width)
    return kernel_call(
        halve_two_kernel,
        [bit, keep_a, got_a, keep_b, got_b],
        [like(shape, BF16)] * 2,
        4,
        cost(2 * keep_a.size, 12 * keep_a.size),
        "halve",
        after,
    )


def halve_kernel(bit, keep, got, keep_out, send_out):
    half = keep_out.shape[0]
    mine = pl.ds(bit[0] * half, half)
    other = pl.ds((1 - bit[0]) * half, half)
    send_out[...] = keep[other] + got[other]
    keep_out[...] = keep[mine] + got[mine]


def halve(keep, got, bit, direct, after):
    count, rows, width = keep.shape
    half = count // 2
    if direct:
        return kernel_call(
            halve_kernel,
            [bit, keep, got],
            [like((half, rows, width), BF16)] * 2,
            4,
            cost(keep.size, 6 * keep.size),
            "halve",
            after,
        )
    bit = bit[0]
    total = tie(keep, after) + got
    take = lambda b: lax.dynamic_slice_in_dim(total, b * half, half, 0)
    return take(bit), take(1 - bit)


def dot(a, b):
    return jnp.dot(a, b, preferred_element_type=F32)


def dot_nt(a, b):
    return lax.dot_general(a, b, (((1,), (1,)), ((), ())), preferred_element_type=F32)


def dot_tn(a, b):
    return lax.dot_general(a, b, (((0,), (0,)), ((), ())), preferred_element_type=F32)


def norm_parts(rows):
    centre = jnp.mean(rows, axis=-1, keepdims=True)
    centred = rows - centre
    spread = jnp.mean(centred * centred, axis=-1, keepdims=True)
    inverse = lax.rsqrt(spread + EPSILON)
    return centred * inverse, inverse


def norm_back(cot, hat, inverse, gain):
    d_hat = cot * gain
    first = jnp.mean(d_hat, axis=-1, keepdims=True)
    second = jnp.mean(d_hat * hat, axis=-1, keepdims=True)
    return inverse * (d_hat - first - hat * second)


def head_lanes(value, head):
    lane = lax.broadcasted_iota(jnp.int32, value.shape, 1)
    return jnp.where(lane // HEAD_DIM == head, value, jnp.zeros_like(value))


def head_rows(value, head):
    row = lax.broadcasted_iota(jnp.int32, value.shape, 0)
    return jnp.where(row // HEAD_DIM == head, value, jnp.zeros_like(value))


def both_heads(value):
    return jnp.concatenate([head_lanes(value, 0), head_lanes(value, 1)], 0)


def to_slot_lanes(value):
    turned = value.T
    return jnp.concatenate([turned[:HEAD_DIM], turned[HEAD_DIM:]], 1)


def to_slot_rows(value):
    turned = value.T
    half = turned.shape[0] // 2
    return jnp.concatenate([turned[:half], turned[half:]], 1)


def diagonal(value):
    lane = lax.broadcasted_iota(jnp.int32, (HEAD_DIM, value.shape[1]), 1)
    return jnp.where(lane < value.shape[1] // 2, value[:HEAD_DIM], value[HEAD_DIM:])


ROWS = 512


def row_loop(total):
    return lambda body: pl.loop(0, total // ROWS)(
        lambda i: body(pl.ds(pl.multiple_of(i * ROWS, ROWS), ROWS))
    )


def pair_loop(width):
    return lambda body: pl.loop(0, width // 128, unroll=2)(
        lambda p: body(p, pl.ds(pl.multiple_of(p * 128, 128), 128))
    )


def project_kernel(
    me_ref, tok, pair, other, gain, wq, wk, wv, normed, q, k, v, sk, sv, mem, mem_cot
):
    half = pair.shape[2]
    rows = half // 2
    for lane in range(2):

        @pl.when(me_ref[0] == lane)
        def _():
            for kind, out in enumerate((mem, mem_cot)):
                for m in range(pair.shape[1]):
                    for i in range(2):
                        for core in range(2):
                            source = pair if core == lane else other
                            at = 2 * (m * half + i * rows) + core * rows
                            block = source[kind, m, i * rows : (i + 1) * rows, :]
                            out[at : at + rows, :] = block

    @row_loop(tok.shape[0])
    def _(here):
        hat, _ = norm_parts(tok[here, :].astype(F32))
        low = (hat * gain[0:1, :]).astype(BF16)
        normed[here, :] = low
        q[here, :] = dot(low, wq[...]).astype(BF16)
        k[here, :] = dot(low, wk[...]).astype(BF16)
        v[here, :] = dot(low, wv[...]).astype(BF16)

    sk[...] = dot(mem[...], wk[...]).astype(BF16)
    sv[...] = dot(mem[...], wv[...]).astype(BF16)


def read_kernel(m, q, k, v, sk, sv, starts, keep, attended, out_t, inv, e_ref, bias):
    tok = attended.shape[0]
    slots = sk.shape[0] // keep.shape[0]
    key_at = lax.broadcasted_iota(jnp.int32, (tok, tok), 0)
    query_at = lax.broadcasted_iota(jnp.int32, (tok, tok), 1)
    start = starts[m, 0:1, :]
    kept = jnp.broadcast_to(keep[m, 0:1, :], (128, tok)).T
    kept = jnp.concatenate([kept] * (tok // 128), 1)
    good = (key_at >= start) & (key_at <= query_at) & (kept > 0)
    bias[...] = jnp.where(good, 0.0, MASKED)
    here, slot_here = pl.ds(m * tok, tok), pl.ds(m * slots, slots)

    @pair_loop(q.shape[1])
    def _(p, lanes):
        read_pair(
            q[here, lanes], k[here, lanes], v[here, lanes], sk[slot_here, lanes],
            sv[slot_here, lanes], bias, attended.at[:, lanes],
            out_t.at[pl.ds(pl.multiple_of(p * 128, 128), 128), :], inv.at[p], e_ref.at[p],
        )


def read_pair(q, keys, values, slot_keys, slot_values, bias, attended, out_t, inv, e_ref):
    tok = q.shape[0]
    half = tok // 2
    slots = slot_keys.shape[0]
    scaled = q * jnp.asarray(SCALE, BF16)
    values_t = values.T
    slot_values_t = slot_values.T
    outs, inverses = [], []
    for head in range(2):
        qm = head_lanes(scaled, head)
        rows = slice(head * HEAD_DIM, (head + 1) * HEAD_DIM)
        s_mem = dot_nt(slot_keys, qm)
        s_a = dot_nt(keys[:half], qm) + bias[:half, :]
        s_b = dot_nt(keys[half:], qm[half:]) + bias[half:, half:]
        top = jnp.maximum(jnp.max(s_mem, 0, keepdims=True), jnp.max(s_a, 0, keepdims=True))
        top_b = jnp.maximum(top[:, half:], jnp.max(s_b, 0, keepdims=True))
        top = jnp.concatenate([top[:, :half], top_b], 1)
        e_mem = jnp.exp(s_mem - top)
        e_a = jnp.exp(s_a - top)
        e_b = jnp.exp(s_b - top_b)
        total = jnp.sum(e_mem, 0, keepdims=True) + jnp.sum(e_a, 0, keepdims=True)
        total_b = total[:, half:] + jnp.sum(e_b, 0, keepdims=True)
        total = jnp.concatenate([total[:, :half], total_b], 1)
        e_mem, e_a, e_b = e_mem.astype(BF16), e_a.astype(BF16), e_b.astype(BF16)
        e_ref[head, :slots, :] = e_mem
        e_ref[head, slots : slots + half, :] = e_a
        e_ref[head, slots + half :, half:] = e_b
        e_ref[head, slots + half :, :half] = jnp.zeros((half, half), BF16)
        mix = dot(slot_values_t[rows], e_mem) + dot(values_t[rows, :half], e_a)
        mix_b = mix[:, half:] + dot(values_t[rows, half:], e_b)
        mix = jnp.concatenate([mix[:, :half], mix_b], 1)
        inverse = 1.0 / total
        outs.append(mix * inverse)
        inverses.append(inverse)
    out = jnp.concatenate(outs, 0)
    out_t[...] = out
    inv[...] = jnp.concatenate(inverses + [jnp.zeros((6, tok), F32)], 0)
    attended[...] = out.T.astype(BF16)


def write_kernel(mem, wsq, k, v, sk, keep, sq_ref, part):
    micro = keep.shape[0]
    tok = k.shape[0] // micro
    slots = mem.shape[0] // micro
    pairs = k.shape[1] // 128
    sq = dot(mem[...], wsq[...]).astype(BF16)
    sq_ref[...] = sq
    for m in range(micro):
        kept = jnp.broadcast_to(keep[m, 0:1, :], (128, tok)).T
        bias = jnp.where(kept > 0, 0.0, MASKED)
        for p in range(pairs):
            lanes = slice(p * 128, p * 128 + 128)
            mine = sq[m * slots : (m + 1) * slots, lanes]
            own = to_slot_lanes(
                mine.astype(F32) * sk[m * slots : (m + 1) * slots, lanes].astype(F32)
            )
            own = jnp.sum(own, 0, keepdims=True) * SCALE
            scores = dot_nt(k[m * tok : (m + 1) * tok, lanes], both_heads(mine)) * SCALE + bias
            top = jnp.maximum(jnp.max(scores, 0, keepdims=True), own)
            e = jnp.exp(scores - top)
            total = jnp.sum(e, 0, keepdims=True)
            mix = diagonal(dot_tn(v[m * tok : (m + 1) * tok, lanes], e.astype(BF16)))
            part[m, :HEAD_DIM, lanes] = mix
            part[m, HEAD_DIM:, lanes] = jnp.concatenate(
                [top, total, own, jnp.zeros((5, 128), F32)], 0
            )


def gelu_pair(hidden):
    root = 0.7978845608028654
    square = hidden * hidden
    bent = jnp.tanh(hidden * (root + (root * 0.044715) * square))
    half = 0.5 + 0.5 * bent
    slope = half + (0.5 * hidden) * (1.0 - bent * bent) * (root + (3.0 * root * 0.044715) * square)
    return (hidden * half).astype(BF16), slope


def ffn_cuts(low, cot_low, up, down, here, act_all, dh_all):
    width = low.shape[1]
    out = d_low = 0.0
    for cut in range(up.shape[0]):
        cols = slice(cut * width, (cut + 1) * width)
        act, slope = gelu_pair(dot(low, up[cut]))
        d_hidden = (dot_nt(cot_low, down[cols, :]) * slope).astype(BF16)
        act_all[here, cols] = act
        dh_all[here, cols] = d_hidden
        out = out + dot(act, down[cols, :])
        d_low = d_low + dot_nt(d_hidden, up[cut])
    return out, d_low


def ffn_grads(shares, refs, me_ref, base, low_all, cot_all, act_all, dh_all, cuts):
    width = low_all.shape[1]
    low_t = low_all[...].T
    for cut in range(cuts):
        cols = slice(cut * width, (cut + 1) * width)
        shares.put(refs, me_ref, base, cut, 0, dot(low_t, dh_all[:, cols]).astype(BF16))
        grad = dot_tn(act_all[:, cols], cot_all[...]).astype(BF16)
        shares.put(refs, me_ref, base + 1, 0, cut * width, grad)


def ffn_first_kernel(
    shares, me_ref, att_a, att_b, tok, cot, wout, up, down, gain,
    resid_ref, out_ref, d_low_ref, *rest
):
    refs, (act_all, dh_all, low_all) = rest[:-3], rest[-3:]
    count = att_a.shape[0]
    for m, att in enumerate((att_a, att_b)):

        @row_loop(count)
        def _(there):
            here = pl.ds(there.start + m * count, ROWS)
            resid = tok[here, :].astype(F32) + dot(att[there, :], wout[...])
            hat, _ = norm_parts(resid)
            low = (hat * gain[1:2, :]).astype(BF16)
            low_all[here, :] = low
            out, d_low = ffn_cuts(low, cot[here, :], up, down, here, act_all, dh_all)
            resid_ref[here, :] = resid
            out_ref[here, :] = resid + out
            d_low_ref[here, :] = d_low

    ffn_grads(shares, refs, me_ref, 0, low_all, cot, act_all, dh_all, up.shape[0])


def ffn_second_kernel(
    shares, me_ref, att_a, att_b, resid, part, d_part, cot, wout, up, down, gain,
    layer_out, d_resid_ref, da_a, da_b, g_gain, *rest
):
    refs, (act_all, dh_all, low_all, dattn_all) = rest[:-4], rest[-4:]
    count = att_a.shape[0]
    gain_row = gain[1:2, :]
    g_gain[...] = jnp.zeros_like(g_gain)
    for m, da_t in enumerate((da_a, da_b)):

        @row_loop(count)
        def _(there):
            here = pl.ds(there.start + m * count, ROWS)
            hat, inverse = norm_parts(resid[here, :])
            low = (hat * gain_row).astype(BF16)
            low_all[here, :] = low
            cot_low = cot[here, :]
            out, d_low = ffn_cuts(low, cot_low, up, down, here, act_all, dh_all)
            layer_out[here, :] = (part[here, :] + out).astype(BF16)
            d_low = d_part[here, :] + d_low
            d_resid = cot_low.astype(F32) + norm_back(d_low, hat, inverse, gain_row)
            d_resid_ref[here, :] = d_resid
            d_attn = d_resid.astype(BF16)
            dattn_all[here, :] = d_attn
            da_t[:, there] = dot_nt(wout[...], d_attn)
            g_gain[0:1, :] += jnp.sum(d_low * hat, 0, keepdims=True)

    ffn_grads(shares, refs, me_ref, 0, low_all, cot, act_all, dh_all, up.shape[0])
    grad = dot_tn(att_a[...], dattn_all[:count, :]) + dot_tn(att_b[...], dattn_all[count:, :])
    shares.put(refs, me_ref, 2, 0, 0, grad.astype(BF16))


def memory_kernel(
    shares, me_ref, slot_ref, part, mem, cot, sk, sv, sq, k, v, keep, wso, wfg, gain,
    new_ref, base, dsq_ref, osk, osv, wdk, wdv, g_gain, *rest
):
    refs, held = rest[:-1], rest[-1]
    micro = part.shape[0]
    slots = mem.shape[0] // micro
    own_rows = new_ref.shape[1]
    pairs = mem.shape[1] // 128
    row_at = lax.broadcasted_iota(jnp.int32, (mem.shape[0], 1), 0)
    mine = ((row_at % slots) // own_rows == slot_ref[0]).astype(F32)
    probs, tots, lses = [], [], []
    lines = []
    for m in range(micro):
        here = slice(m * slots, (m + 1) * slots)
        line, prob_line = [], []
        for p in range(pairs):
            lanes = slice(p * 128, p * 128 + 128)
            top0 = part[m, HEAD_DIM : HEAD_DIM + 1, lanes]
            total0 = part[m, HEAD_DIM + 1 : HEAD_DIM + 2, lanes]
            own = part[m, HEAD_DIM + 2 : HEAD_DIM + 3, lanes]
            top = jnp.maximum(top0, own)
            own_e = jnp.exp(own - top)
            shift = jnp.exp(top0 - top)
            total = total0 * shift + own_e
            inverse = 1.0 / total
            prob = own_e * inverse
            values = to_slot_lanes(sv[here, lanes].astype(F32))
            mixed = part[m, :HEAD_DIM, lanes] * (shift * inverse) + prob * values
            line.append(to_slot_rows(mixed))
            prob_line.append((prob, top + jnp.log(total)))
        lines.append(jnp.concatenate(line, 1))
        probs.append(prob_line)
    written = jnp.concatenate(lines, 0)
    written_low = written.astype(BF16)
    mem_low = mem[...]
    mem_f32 = mem_low.astype(F32)
    update = dot(written_low, wso[...])
    gate = 1.0 / (1.0 + jnp.exp(-dot(mem_low, wfg[...])))
    gain_row = gain[2:3, :]
    hat, inverse = norm_parts(gate * mem_f32 + (1.0 - gate) * update)
    held[...] = hat * gain_row
    cot_f32 = cot[...].astype(F32)
    for m in range(micro):
        at = pl.multiple_of(m * slots + slot_ref[0] * own_rows, own_rows)
        new_ref[m] = held[pl.ds(at, own_rows), :].astype(BF16)
    g_gain[...] = jnp.broadcast_to(jnp.sum(cot_f32 * hat * mine, 0, keepdims=True), g_gain.shape)
    d_blend = norm_back(cot_f32, hat, inverse, gain_row)
    d_pre = (d_blend * (mem_f32 - update) * gate * (1.0 - gate) * mine).astype(BF16)
    d_update = (d_blend * (1.0 - gate)).astype(BF16)
    mem_t = mem_low.T
    d_upd = (d_update.astype(F32) * mine).astype(BF16)
    shares.put(refs, me_ref, 1, 0, 0, dot_tn(written_low, d_upd).astype(BF16))
    shares.put(refs, me_ref, 2, 0, 0, dot(mem_t, d_pre).astype(BF16))
    base[...] = d_blend * gate * mine + dot_nt(d_pre, wfg[...])
    d_written = dot_nt(d_update, wso[...]).astype(BF16)
    dw_f32 = d_written.astype(F32)
    product = dw_f32 * written
    tok = k.shape[0] // micro
    for m in range(micro):
        here = slice(m * slots, (m + 1) * slots)
        there = slice(m * tok, (m + 1) * tok)
        kept = jnp.broadcast_to(keep[m, 0:1, :], (128, tok)).T
        bias = jnp.where(kept > 0, 0.0, MASKED)
        for p in range(pairs):
            lanes = slice(p * 128, p * 128 + 128)
            prob, lse = probs[m][p]
            values_f32 = sv[here, lanes].astype(F32)
            delta = jnp.sum(to_slot_lanes(product[here, lanes]), 0, keepdims=True)
            own_dp = jnp.sum(to_slot_lanes(dw_f32[here, lanes] * values_f32), 0, keepdims=True)
            own_ds = prob * (own_dp - delta)
            wide = lambda r: to_slot_rows(jnp.broadcast_to(r, (HEAD_DIM, 2 * slots)))
            own_ds = wide(own_ds) * mine[here] * SCALE
            own_p = wide(prob) * mine[here]
            sq_low = sq[here, lanes]
            sq_both = both_heads(sq_low * jnp.asarray(SCALE, BF16))
            dw_low = d_written[here, lanes]
            dw_both = both_heads(dw_low)
            keys, values = k[there, lanes], v[there, lanes]
            prob = jnp.exp(dot_nt(keys, sq_both) + bias - lse)
            d_score = (prob * (dot_nt(values, dw_both) - delta)).astype(BF16)
            wdk[there, lanes] = dot(d_score, sq_both).astype(BF16)
            wdv[there, lanes] = dot(prob.astype(BF16), dw_both).astype(BF16)
            d_read = to_slot_rows(diagonal(dot_tn(keys, d_score)))
            slot_keys = sk[here, lanes].astype(F32)
            dsq_ref[here, lanes] = (d_read * SCALE + own_ds * slot_keys).astype(BF16)
            osk[here, lanes] = own_ds * sq_low.astype(F32)
            osv[here, lanes] = own_p * dw_low.astype(F32)
    shares.put(refs, me_ref, 0, 0, 0, dot(mem_t, dsq_ref[...]).astype(BF16))


def back_kernel(
    m, q, k, v, sk, sv, da_t, out_t, inv, e_ref, wdk, wdv, osk, osv, dq, dk, dv, dsk, dsv
):
    tok, slots = dq.shape[0], dsk.shape[0]
    here, slot_here = pl.ds(m * tok, tok), pl.ds(m * slots, slots)

    @pair_loop(q.shape[1])
    def _(p, lanes):
        turned = pl.ds(pl.multiple_of(p * 128, 128), 128)
        back_pair(
            q[here, lanes], k[here, lanes], v[here, lanes], sk[slot_here, lanes],
            sv[slot_here, lanes], da_t.at[turned, :], out_t.at[turned, :], inv.at[p],
            e_ref.at[p], wdk.at[here, lanes], wdv.at[here, lanes], osk.at[slot_here, lanes],
            osv.at[slot_here, lanes], dq.at[:, lanes], dk.at[:, lanes], dv.at[:, lanes],
            dsk.at[:, lanes], dsv.at[:, lanes],
        )


def back_pair(
    q, keys, values, slot_keys, slot_values, da_t, out_t, inv, e_ref, wdk, wdv, osk, osv,
    dq, dk, dv, dsk, dsv,
):
    tok = q.shape[0]
    half = tok // 2
    slots = slot_keys.shape[0]
    scaled = q * jnp.asarray(SCALE, BF16)
    keys_t = keys.T
    slot_keys_t = slot_keys.T
    norm = jnp.concatenate(
        [jnp.broadcast_to(inv[i : i + 1, :], (HEAD_DIM, tok)) for i in range(2)], 0
    )
    da = (da_t[...] * norm).astype(BF16)
    product = da.astype(F32) * out_t[...]
    da_rows = da.T
    dq_parts = []
    dk_a = dk_b = dv_a = dv_b = dk_m = dv_m = 0.0
    for head in range(2):
        rows = slice(head * HEAD_DIM, (head + 1) * HEAD_DIM)
        qm = head_lanes(scaled, head)
        dam_t = head_rows(da, head)
        dam = head_lanes(da_rows, head)
        delta = jnp.sum(product[rows], 0, keepdims=True)
        e_mem = e_ref[head, :slots, :]
        e_a = e_ref[head, slots : slots + half, :]
        e_b = e_ref[head, slots + half :, half:]
        ds_mem = (e_mem.astype(F32) * (dot(slot_values, dam_t) - delta)).astype(BF16)
        ds_a = (e_a.astype(F32) * (dot(values[:half], dam_t) - delta)).astype(BF16)
        ds_b = (
            e_b.astype(F32) * (dot(values[half:], dam_t[:, half:]) - delta[:, half:])
        ).astype(BF16)
        part = dot(slot_keys_t[rows], ds_mem) + dot(keys_t[rows, :half], ds_a)
        part_b = part[:, half:] + dot(keys_t[rows, half:], ds_b)
        dq_parts.append(jnp.concatenate([part[:, :half], part_b], 1))
        dk_a = dk_a + dot(ds_a, qm)
        dk_b = dk_b + dot(ds_b, qm[half:])
        dk_m = dk_m + dot(ds_mem, qm)
        dv_a = dv_a + dot(e_a, dam)
        dv_b = dv_b + dot(e_b, dam[half:])
        dv_m = dv_m + dot(e_mem, dam)
    dq[...] = (jnp.concatenate(dq_parts, 0) * SCALE).T.astype(BF16)

    dk[:half, :] = (dk_a + wdk[:half, :].astype(F32)).astype(BF16)
    dk[half:, :] = (dk_b + wdk[half:, :].astype(F32)).astype(BF16)
    dv[:half, :] = (dv_a + wdv[:half, :].astype(F32)).astype(BF16)
    dv[half:, :] = (dv_b + wdv[half:, :].astype(F32)).astype(BF16)
    dsk[...] = (dk_m + osk[...]).astype(BF16)
    dsv[...] = (dv_m + osv[...]).astype(BF16)


def grads_kernel(
    shares, me_ref, normed, dq_a, dk_a, dv_a, dsk_a, dsv_a, dq_b, dk_b, dv_b, dsk_b, dsv_b,
    mem, wq, wk, wv, gain, g_ffn, g_mem, *refs
):
    count = dq_a.shape[0]
    slots = dsk_a.shape[0]
    rows_t = normed[...].T
    mem_t = mem[...].T
    weighted = 0.0
    sets = (
        (dq_a, dq_b, wq, None, None),
        (dk_a, dk_b, wk, dsk_a, dsk_b),
        (dv_a, dv_b, wv, dsv_a, dsv_b),
    )
    for i, (cot_a, cot_b, weight, slot_a, slot_b) in enumerate(sets):
        grad = dot(rows_t[:, :count], cot_a[...]) + dot(rows_t[:, count:], cot_b[...])
        weighted = weighted + grad * weight[...].astype(F32)
        if slot_a is not None:
            slot_cot = jnp.concatenate([slot_a[...], slot_b[...]], 0)
            grad = grad + dot(mem_t, slot_cot)
        shares.put(refs, me_ref, i, 0, 0, grad.astype(BF16))
    folded = weighted[:, :128]
    for i in range(1, weighted.shape[1] // 128):
        folded = folded + weighted[:, i * 128 : (i + 1) * 128]
    line = jnp.sum(folded.T, 0, keepdims=True) / gain[0:1, :]
    lines = [line, g_ffn[0:1, :], g_mem[0:1, :]]
    extra = shares.sections[3][1]
    lines = jnp.concatenate(lines + [jnp.zeros((extra - 3, line.shape[1]), F32)], 0)
    lines = lines.astype(BF16)
    for device in range(2 * shares.count):
        shares.put(refs, me_ref, 3, 0, device * extra, lines)


def input_kernel(
    me_ref, tok, d_resid,
    dq_a, dk_a, dv_a, dsk_a, dsv_a, dq_b, dk_b, dv_b, dsk_b, dsv_b, dsq, base,
    wq, wk, wv, wsq, gain, tok_grad, mem_keep, mem_send, d_mem
):
    count = dq_a.shape[0]
    for m, (dq, dk, dv) in enumerate(((dq_a, dk_a, dv_a), (dq_b, dk_b, dv_b))):

        @row_loop(count)
        def _(there):
            here = pl.ds(there.start + m * count, ROWS)
            hat, inverse = norm_parts(tok[here, :].astype(F32))
            d_normed = dot_nt(dq[there, :], wq[...]) + dot_nt(dk[there, :], wk[...])
            d_normed = d_normed + dot_nt(dv[there, :], wv[...])
            back = norm_back(d_normed, hat, inverse, gain[0:1, :])
            tok_grad[here, :] = (d_resid[here, :] + back).astype(BF16)

    d_mem[...] = (
        base[...]
        + dot_nt(dsq[...], wsq[...])
        + dot_nt(jnp.concatenate([dsk_a[...], dsk_b[...]], 0), wk[...])
        + dot_nt(jnp.concatenate([dsv_a[...], dsv_b[...]], 0), wv[...])
    )
    micro, half, _ = mem_keep.shape
    slots = 2 * half
    rows = slots // 4
    for m in range(micro):
        for i in range(2):
            at = m * slots + 2 * i * rows
            mine = pl.ds(pl.multiple_of(at + me_ref[0] * rows, rows), rows)
            other = pl.ds(pl.multiple_of(at + (1 - me_ref[0]) * rows, rows), rows)
            mem_keep[m, i * rows : (i + 1) * rows, :] = d_mem[mine, :]
            mem_send[m, i * rows : (i + 1) * rows, :] = d_mem[other, :]


def split_kernel(bit, held, got, keep_out, send_out):
    half = keep_out.shape[1]
    mine = bit[0]
    for m in range(held.shape[0]):
        own = pl.ds(pl.multiple_of(mine * half, half), half)
        other = pl.ds(pl.multiple_of((1 - mine) * half, half), half)
        keep_out[m] = held[m, own, :] + got[m, own, :]
        send_out[m] = held[m, other, :] + got[m, other, :]


def kernel_call(
    body, args, out_shape, mib, price, name, after=(), scalars=1, scratch_shapes=(), far=None
):
    count = len(args)

    def run(*refs):
        body(*refs[:count], *refs[count + len(after) :])

    in_specs = [SMEM] * scalars + [VMEM] * (count - scalars) + [ANY] * len(after)
    out_specs = [VMEM] * len(out_shape)
    args, out_shape = list(args), list(out_shape)
    if far is not None and far < count:
        in_specs[far] = ANY
        args[far] = pltpu.with_memory_space_constraint(args[far], pltpu.HBM)
    elif far is not None:
        out_specs[far - count] = ANY
        out_shape[far - count] = pltpu.HBM(
            out_shape[far - count].shape, out_shape[far - count].dtype
        )
    return pl.pallas_call(
        run,
        in_specs=in_specs,
        out_specs=out_specs,
        out_shape=out_shape,
        scratch_shapes=scratch_shapes,
        compiler_params=pltpu.CompilerParams(vmem_limit_bytes=int(mib * (1 << 20))),
        cost_estimate=price,
        name=name,
    )(*args, *after)


def like(shape, dtype):
    return jax.ShapeDtypeStruct(shape, dtype)


def cost(flops, nbytes, trans=0):
    return pl.CostEstimate(flops=flops, bytes_accessed=nbytes, transcendentals=trans)


def on_device(
    tokens,
    memory,
    doc_lengths,
    key_mask,
    w_query,
    w_key,
    w_value,
    w_out,
    w_up,
    w_down,
    w_slot_query,
    w_slot_out,
    w_forget,
    norm_gain,
    ffn_gain,
    memory_gain,
    out_grad,
    memory_grad,
):
    slot_count = lax.axis_size("slot")
    slot_index = lax.axis_index("slot")
    device_count = lax.axis_size("batch") * slot_count
    device = lax.axis_index("batch") * slot_count + slot_index
    micro, tok_dev, width = tokens.shape
    slot_rows = memory.shape[2]
    slots = slot_rows * slot_count
    group_tok = tok_dev * slot_count
    dev_start = slot_index * tok_dev
    rows = w_query.shape[0]
    ff = w_up.shape[1]
    pairs = width // 128
    total = micro * tok_dev
    mem_rows = micro * slots
    keys = tok_dev + slots
    down_rows = w_down.shape[0]
    part_rows = down_rows // 2
    cuts = ff // 2 // width
    extra = 8
    lane_at = jnp.arange(width, dtype=jnp.int32) // rows
    pick = jnp.arange(width)[:, None] == device * rows + jnp.arange(rows)[None, :]
    pick = pick.astype(F32)
    keep = lax.dynamic_slice_in_dim(key_mask, dev_start, tok_dev, 1).astype(F32)
    keep = jnp.broadcast_to(keep[:, None, :], (micro, 8, tok_dev))
    segment = lax.axis_index("batch") * group_tok + dev_start
    positions = segment + jnp.arange(tok_dev, dtype=jnp.int32)
    doc_ends = jnp.cumsum(doc_lengths, axis=1, dtype=jnp.int32)
    passed = positions[None, None, :] >= doc_ends[:, :, None]
    starts = jnp.max(jnp.where(passed, doc_ends[:, :, None] - segment, 0), axis=1)
    starts = jnp.broadcast_to(starts[:, None, :], (micro, 8, tok_dev))
    bits = []
    for turn in range(2):
        orders = exchange_orders(turn)
        bits += [lane_bit(orders, step) for step in range(len(orders[0]))]
    scalars = [own_bit("slot", 1), slot_index, own_bit("slot", 2)] + bits
    scalars = [jnp.asarray(entry, jnp.int32) for entry in scalars]
    small = (keep, starts, pick, tuple(scalars), tuple(entry == 0 for entry in scalars))
    keep, starts, pick, scalars, lows = lax.optimization_barrier(small)
    me, slot_scalar, slot_high, *bits = (entry.reshape(1) for entry in scalars)
    slot_low, lows = lows[2], lows[3:]
    half = len(bits) // 2
    lows, bits = (lows[:half], lows[half:]), (bits[:half], bits[half:])
    gain_rows = jnp.stack([norm_gain, ffn_gain, memory_gain])
    gain_rows = jnp.where(lane_at == device, jnp.tile(gain_rows, (1, device_count)), 0)
    gain_rows = jnp.pad(gain_rows.astype(BF16), ((0, extra - 3), (0, 0)))
    first = Gather(jnp.concatenate([w_query, w_key, w_value, gain_rows])[None], 0, lows)
    marks = [first.until(3)]
    raw = [w_slot_query, w_slot_out, w_forget, w_out, w_up, w_down]
    raw = lax.optimization_barrier(tuple(raw) + (marks[0],))
    w_up, w_down = raw[4], raw[5]
    up_parts = w_up.reshape(rows, device_count, 2, part_rows).transpose(2, 0, 1, 3)
    up_parts = up_parts.reshape(2, rows, cuts, width).transpose(0, 2, 1, 3)
    up_parts = up_parts.reshape(2, cuts * rows, width)
    rest = list(raw[:4])
    rest += [up_parts[0], w_down[:part_rows]]
    rest = Gather(jnp.concatenate(rest)[None], 0, lows)
    fourth = Gather(jnp.concatenate([up_parts[1], w_down[part_rows:]])[None], 1, lows)
    first.launch()
    marks.append(first.finish([rest.held]))
    marks.append(rest.until(3))
    first.launch()
    pair = tie(jnp.stack([memory[:, 0], memory_grad[:, 0]]), marks[1:2])
    other = swap(pair, "slot", 2)
    marks.append(first.finish())
    other = tie(other, marks[3:])
    low, high = jnp.where(slot_low, pair, other), jnp.where(slot_low, other, pair)
    pair = jnp.concatenate([low, high], 2)
    first.launch([marks[2], pair])
    rest.launch(marks[3:])
    fourth.until(4, marks[3:])
    fourth.launch(marks[3:])
    other = swap(pair, "slot", 1)
    first.finish()
    rest.finish([first.held])
    fourth.finish([first.held])
    first.launch([rest.held, fourth.held])
    fourth.launch()
    second, third = [
        Gather(rest.held[:, part], 0, lows, rest.left)
        for part in (slice(0, 4 * rows), slice(4 * rows, None))
    ]
    second.launch()

    one = [(i * rows, rows, 1) for i in range(4)]
    w_query, w_key, w_value, gains = first.unpack(one[:3] + [(3 * rows, extra, 0)], me)
    w_query, w_key, w_value = w_query[0], w_key[0], w_value[0]

    tok_flat = tokens.reshape(total, width)
    cot_flat = out_grad.reshape(total, width)
    low = lambda n, w: like((n, w), BF16)

    wide = like((total, width), F32)
    slot_like = low(mem_rows, width)
    slot_wide = like((mem_rows, width), F32)
    (
        normed, queries, tok_keys, tok_values, slot_keys, slot_values, mem_low, mem_cot
    ) = kernel_call(
        project_kernel,
        [me, tok_flat, pair, other, gains, w_query, w_key, w_value],
        [low(total, width)] * 4 + [slot_like] * 4,
        6,
        cost(6 * total * width * width, 8 << 20),
        "project",
        after=[rest.held],
    )
    second.finish([normed])
    third.launch([second.held])
    second.launch([second.held])

    square = low(tok_dev, width)
    reads = []
    for m in range(micro):
        reads.append(
            kernel_call(
                functools.partial(read_kernel, m),
                [queries, tok_keys, tok_values, slot_keys, slot_values, starts, keep],
                [
                    square,
                    like((width, tok_dev), F32),
                    like((pairs, 8, tok_dev), F32),
                    like((pairs, 2, keys, tok_dev), BF16),
                ],
                6,
                cost(16 * total * width * keys // micro, 8 << 20, total * keys * HEADS // micro),
                "read",
                scalars=0,
                after=(second.held,) if m == 0 else (third.held,),
                scratch_shapes=[pltpu.VMEM((tok_dev, tok_dev), F32)],
            )
        )
        if m == 0:
            third.finish([reads[0][0]])
            second.finish([reads[0][0]])
            fourth.finish([reads[0][0]])
            ready = [second.held, third.held, fourth.held]
            third.launch(ready)
            second.launch(ready)
            fourth.launch(ready)
    attended = [kept[0] for kept in reads]

    second_mats = second.unpack(one, me, [attended[1]])
    w_slot_query, w_slot_out, w_forget, w_out = (m[0] for m in second_mats)
    third.finish([attended[1]])
    fourth.finish([attended[1]])
    third.launch([w_slot_query, third.held, fourth.held])
    fourth.launch([w_slot_query, third.held, fourth.held])
    ffn_sections = [(0, rows, cuts), (cuts * rows, part_rows, 1)]
    up_first, down_first = third.unpack(ffn_sections, me)
    slot_queries, part = kernel_call(
        write_kernel,
        [mem_low, w_slot_query, tok_keys, tok_values, slot_keys, keep],
        [slot_like, like((micro, 72, slots * HEADS), F32)],
        3,
        cost(8 * total * width * slots, 5 << 20, total * slots * HEADS),
        "write",
        scalars=0,
        after=[third.held, fourth.held],
    )

    def merged(part, other):
        top_a, top_b = part[:, 64:65], other[:, 64:65]
        top = jnp.maximum(top_a, top_b)
        scale_a, scale_b = jnp.exp(top_a - top), jnp.exp(top_b - top)
        mix = part[:, :64] * scale_a + other[:, :64] * scale_b
        tot = part[:, 65:66] * scale_a + other[:, 65:66] * scale_b
        return jnp.concatenate([mix, top, tot, part[:, 66:]], 1)

    part = merged(part, swap(part, "slot", 1))
    other = swap(part, "slot", 2)

    half_cost = cost(7 * total * width * ff, 14 << 20, total * ff // 2)
    tall = [pltpu.VMEM((total, ff // 2), BF16)] * 2 + [pltpu.VMEM((total, width), BF16)]
    sums_first = Shares(0, ffn_sections, me, width, bits)
    resid, out_part, d_low, *outs = kernel_call(
        functools.partial(ffn_first_kernel, sums_first),
        [me, *attended, tok_flat, cot_flat, w_out, up_first, down_first[0], gains],
        [wide] * 3 + sums_first.shapes(),
        13,
        half_cost,
        "ffn_first",
        scratch_shapes=tall,
        after=[part],
    )
    part = merged(part, tie(other, [resid]))
    fourth.finish([resid])
    sums_first.begin(outs, [part, fourth.held])
    fourth.launch([part])

    sums_slot = Shares(0, one[:3], me, width, bits)
    new_memory, base, d_sq, own_sk, own_sv, w_dk, w_dv, g_mem, *outs = kernel_call(
        functools.partial(memory_kernel, sums_slot),
        [me, slot_scalar, part, mem_low, mem_cot, slot_keys, slot_values, slot_queries]
        + [tok_keys, tok_values, keep, w_slot_out, w_forget, gains],
        [like((micro, slot_rows, width), BF16), slot_wide]
        + [slot_like]
        + [slot_wide] * 2
        + [low(total, width)] * 2
        + [like((8, width), F32)]
        + sums_slot.shapes(),
        4,
        cost(12 * mem_rows * width * width + 12 * total * width * slots, 8 << 20),
        "memory",
        scalars=2,
        scratch_shapes=[pltpu.VMEM((mem_rows, width), F32)],
        after=[resid, fourth.held],
    )
    sums_first.join(sums_slot.split(outs))
    up_second, down_second = fourth.unpack(ffn_sections, me, [base])
    sums_first.finish([up_second])
    sums_first.launch()

    sections = [(0, rows, cuts), (cuts * rows, part_rows, 1)]
    sections += [(cuts * rows + part_rows, rows, 1)]
    sums_second = Shares(0, sections, me, width, bits)
    turned = like((width, tok_dev), F32)
    layer_out, d_resid, da_a, da_b, g_ffn, *outs = kernel_call(
        functools.partial(ffn_second_kernel, sums_second),
        [me, *attended, resid, out_part, d_low, cot_flat, w_out, up_second, down_second[0], gains],
        [low(total, width), wide, turned, turned, like((8, width), F32)] + sums_second.shapes(),
        17,
        half_cost,
        "ffn_second",
        scratch_shapes=tall + [pltpu.VMEM((total, width), BF16)],
        after=[sums_first.send],
    )
    sums_first.finish([d_resid])
    sums_second.begin(outs, [sums_first.send])
    sums_first.launch()
    back = []
    for m, da_t in enumerate((da_a, da_b)):
        found = kernel_call(
            functools.partial(back_kernel, m),
            [queries, tok_keys, tok_values, slot_keys, slot_values]
            + [da_t, *reads[m][1:], w_dk, w_dv, own_sk, own_sv],
            [square] * 3 + [low(slots, width)] * 2,
            6,
            cost(24 * total * width * keys // micro, 10 << 20),
            "back",
            scalars=0,
            after=[sums_first.send] + ([sums_second.send] if m else []),
        )
        back += found
        if m == 0:
            sums_second.finish([found[0]])
            sums_first.finish([found[0]])
            sums_second.launch([sums_first.send])
            sums_first.launch([sums_second.send])

    sums_third = Shares(0, one[:3] + [(3 * rows, extra, 1)], me, width, bits)
    outs = kernel_call(
        functools.partial(grads_kernel, sums_third),
        [me, normed, *back, mem_low, w_query, w_key, w_value, gains, g_ffn, g_mem],
        sums_third.shapes(),
        8,
        cost(6 * total * width * width, 8 << 20),
        "grads",
        after=[sums_first.send],
    )
    sums_second.finish(outs[:1])
    sums_first.finish(outs[:1])
    sums_third.begin(outs, [sums_second.send, sums_first.send])
    sums_second.launch([sums_first.send])
    sums_first.launch([sums_second.send])
    sums_third.finish([sums_first.send])
    sums_third.launch()
    tokens_grad, mem_keep, mem_send = kernel_call(
        input_kernel,
        [me, tok_flat, d_resid, *back, d_sq, base, w_query, w_key, w_value, w_slot_query, gains],
        [low(total, width)] + [like((micro, slots // 2, width), F32)] * 2,
        10,
        cost(6 * total * width * width, 12 << 20),
        "input",
        after=[sums_third.send],
        scratch_shapes=[pltpu.VMEM((mem_rows, width), F32)],
    )
    piece = lambda m, i: m[i * rows : (i + 1) * rows]

    def up_piece(m, at):
        return m[at : at + cuts * rows].reshape(cuts, rows, width).transpose(1, 0, 2).reshape(
            rows, device_count, 1, part_rows
        )

    sums_second.finish([mem_keep])
    sums_third.finish([sums_second.send])
    sums_third.launch()
    sums_second.launch([sums_third.send])
    both = [sums_second.send, sums_third.send]
    got = swap(tie(mem_send, both), "slot", 1)
    while sums_first.done < sums_first.steps:
        sums_first.finish()
        sums_first.launch()
    total_first = sums_first.end(both)
    up_low = up_piece(total_first, 0)
    mixed = total_first[cuts * rows + part_rows :]
    slot_shares = [piece(mixed, i) for i in range(3)]
    sums_third.finish([total_first, sums_second.send])
    sums_third.launch()
    sums_second.finish([sums_third.send])
    sums_second.launch()
    held, sent = kernel_call(
        split_kernel,
        [slot_high, mem_keep, got],
        [like((micro, slot_rows, width), F32)] * 2,
        2,
        cost(mem_keep.size, 8 * mem_keep.size),
        "split",
        after=[sums_second.send],
    )
    got = swap(sent, "slot", 2)
    while sums_second.done < sums_second.steps:
        sums_second.finish()
        sums_second.launch()
    sums_third.finish([sums_second.send, held, up_low] + slot_shares)
    sums_third.launch()
    total_second = sums_second.end([sums_third.send])
    moved = held + tie(got, [sums_third.send])
    total_second = tie(total_second, [sums_third.send])
    up_share = jnp.concatenate([up_low, up_piece(total_second, 0)], 2)
    down_at = cuts * rows
    down_share = jnp.concatenate(
        [m[down_at : down_at + part_rows] for m in (total_first, total_second)]
    )
    while sums_third.done < sums_third.steps:
        sums_third.finish()
        sums_third.launch()
    sums_third = sums_third.end()
    gain_share = jnp.dot(
        sums_third[3 * rows : 3 * rows + 3], pick, precision=lax.Precision.HIGHEST
    )
    return (
        layer_out.reshape(micro, tok_dev, width),
        new_memory[:, None],
        tokens_grad.reshape(micro, tok_dev, width),
        moved.astype(BF16)[:, None],
        piece(sums_third, 0),
        piece(sums_third, 1),
        piece(sums_third, 2),
        total_second[down_at + part_rows :],
        up_share.reshape(rows, ff),
        down_share,
        *slot_shares,
        gain_share[0],
        gain_share[1],
        gain_share[2],
    )


def solution(mesh):
    weight = P(("batch", "slot"), None)
    gain = P(("batch", "slot"))
    rows = P(None, ("batch", "slot"), None)
    slots = P(None, "batch", "slot", None)
    return jax.shard_map(
        on_device,
        mesh=mesh,
        in_specs=(rows, slots, P(), P(None, "batch")) + (weight,) * 9 + (gain,) * 3 + (rows, slots),
        out_specs=(rows, slots, rows, slots) + (weight,) * 9 + (gain,) * 3,
        check_vma=False,
    )
```
